32 devices in a mesh: section: 4 (over y, x), dp: 8 (over z, core).
Axes of the slice: x: 2, y: 2, z: 4, core: 2. Of those that a mesh axis runs over, the one named last changes fastest.
Arguments:
- inputs: bfloat16 [16, 1024, 768], P('dp'), may hold values from -6 to 6
- cotangent: bfloat16 [16, 1024, 768], P('dp'), may hold values from -30 to 30
- included: int32 [16], P('dp'), may hold values 0 or 1
- qkv_weight: bfloat16 [768, 4608], P(None, 'section'), may hold values from -0.21875 to 0.21875
- qkv_bias: float32 [4608], P('section'), may hold values from -2.5 to 2.5
- out_weight: bfloat16 [1536, 768], P('section'), may hold values from -0.875 to 0.875
- fc_weight: bfloat16 [768, 6144], P(None, 'section'), may hold values from -0.21875 to 0.21875
- fc_bias: float32 [6144], P('section'), may hold values from -2.5 to 2.5
- proj_weight: bfloat16 [6144, 768], P('section'), may hold values from -0.109375 to 0.109375
- norm_gains: float32 [2, 1536], P(None, 'section'), may hold values from 0.5 to 1.5
- shifts: float32 [4, 1536], P(None, 'section'), may hold values from -2.5 to 2.5
- noise: bfloat16 [14175744], P('section'), may hold values from -6 to 6
Outputs:
- layer_outputs: bfloat16 [16, 1024, 1536], P('dp', None, 'section')
- input_grad: bfloat16 [16, 1024, 768], P('dp', 'section')
- qkv_weight_grad: float32 [768, 4608], P(None, 'section')
- qkv_bias_grad: float32 [4608], P('section')
- out_weight_grad: float32 [1536, 768], P('section')
- fc_weight_grad: float32 [768, 6144], P(None, 'section')
- fc_bias_grad: float32 [6144], P('section')
- proj_weight_grad: float32 [6144, 768], P('section')
- norm_gains_grad: float32 [2, 1536], P(None, 'section')
- shifts_grad: float32 [4, 1536], P(None, 'section')
The draws below stay inside these ranges and needn't reach their ends.
All inputs are finite; a program needn't handle non-finite values. No bound on the sum of `included` on one device may be relied on, other than what follows from the above.
Results may differ from the reference program's by a relative error of at most 0.017.
Values may be sent and summed in bfloat16 or wider, within the bound.
No kernel may reach another device: no remote copies, remote signals or barrier semaphores. Data moves between devices by JAX's collectives and lax.ppermute only.
A program may use at most 384 MiB of HBM per device.

```python
import math
import jax
import jax.numpy as jnp
from jax import lax

D = 768
FF = 3072
HS = 64
LEN = 1024
NSEQ = 16
LAYERS = 2
PARAMS_SECTION = 3543936
N_SECTION = 4


def draw_cotangent(key, part):
    key = jax.random.fold_in(key, 7)
    scale_key, value_key = jax.random.split(key)
    scales = jnp.exp(jax.random.uniform(scale_key, (NSEQ, 1, 1), jnp.float32, math.log(0.3), math.log(10.0)))
    values = jax.random.truncated_normal(value_key, -3.0, 3.0, (NSEQ, LEN, D), jnp.float32)
    return (scales * values).astype(jnp.bfloat16)


def touch_ends(values, key, smallest, high):
    extent = values.shape
    place = [jax.random.randint(jax.random.fold_in(key, axis), (), 0, extent[axis]) for axis in range(len(extent))]
    values = values.at[tuple(place)].set(smallest)
    longest = extent.index(max(extent))
    place[longest] = (place[longest] + 1) % extent[longest]
    return values.at[tuple(place)].set(high)


def steps_of(rng, dims, cuts, least, high):
    loudness, own = 1.0, jax.random.fold_in(rng, 6)
    for dim, shards_of in cuts:
        heights = jnp.exp(jax.random.uniform(jax.random.fold_in(own, dim), (shards_of,), jnp.float32, least / len(cuts), high / len(cuts)))
        loudness = loudness * jnp.repeat(heights, dims[dim] // shards_of).reshape([-1 if axis == dim else 1 for axis in range(len(dims))])
    return loudness


def normal_values(own_key, extent, width, limit, shards=(), kind=jnp.bfloat16):
    drawn = width * jax.random.normal(own_key, extent, jnp.float32)
    if shards:
        drawn = drawn * steps_of(own_key, extent, shards, -0.22, 0.18)
    return jnp.clip(drawn, -limit, limit).astype(kind)


def setup_inputs(seed: int = 0) -> dict:
    arg_keys = jax.random.split(jax.random.key(seed), 13)
    return {
        "inputs": normal_values(arg_keys[0], (NSEQ, LEN, D), 1.0, 6.0, ((0, 8),)),
        "cotangent": draw_cotangent(jax.random.fold_in(arg_keys[12], 71), 0),
        "included": touch_ends((jax.random.randint(arg_keys[2], (NSEQ,), 0, 2) < 1).astype(jnp.int32), jax.random.fold_in(arg_keys[2], 1), 0, 1),
        "qkv_weight": normal_values(arg_keys[3], (D, LAYERS * 3 * D), D ** -0.5, 0.21875, ((1, 4),)),
        "qkv_bias": normal_values(arg_keys[4], (LAYERS * 3 * D,), 0.3, 2.5, ((0, 4),), jnp.float32),
        "out_weight": normal_values(arg_keys[5], (LAYERS * D, D), (D // 16) ** -0.5, 0.875, ((0, 4),)),
        "fc_weight": normal_values(arg_keys[6], (D, LAYERS * FF), D ** -0.5, 0.21875, ((1, 4),)),
        "fc_bias": normal_values(arg_keys[7], (LAYERS * FF,), 0.3, 2.5, ((0, 4),), jnp.float32),
        "proj_weight": normal_values(arg_keys[8], (LAYERS * FF, D), FF ** -0.5, 0.109375, ((0, 4),)),
        "norm_gains": jnp.clip(1.0 + 0.1 * jax.random.normal(arg_keys[9], (2, LAYERS * D), jnp.float32), 0.5, 1.5),
        "shifts": normal_values(arg_keys[10], (4, LAYERS * D), 0.3, 2.5, ((1, 4),), jnp.float32),
        "noise": normal_values(arg_keys[11], (N_SECTION * PARAMS_SECTION,), 1.0, 6.0, ((0, 4),)),
    }


CLIP_FRACTION = 0.05
NOISE_MULT = 0.001
SAMPLE_RATE = 0.5
NORM_EPS = 1e-05
MASKED_SCORE = -1e+30

@jax.custom_vjp
def low(v):
    return lax.optimization_barrier(v.astype(jnp.bfloat16)).astype(jnp.float32)

@jax.custom_vjp
def low_back(v):
    return v

def low_keep(v):
    return (low(v), None)

def low_pass(kept, grad):
    return (grad,)

def back_keep(v):
    return (v, None)

def back_low(kept, grad):
    return (low(grad),)
low.defvjp(low_keep, low_pass)
low_back.defvjp(back_keep, back_low)

def layer_norm(values, gain_row, shift_row):
    center = values - lax.optimization_barrier(jnp.mean(values, axis=-1, keepdims=True))
    spread = lax.optimization_barrier(jnp.mean(center * center, axis=-1, keepdims=True))
    return center * lax.rsqrt(spread + NORM_EPS) * gain_row + shift_row

def product(left, right):
    return jnp.dot(left, right, precision=lax.Precision.HIGHEST)

def apply_layer(weights, layer_index, values):
    qkv_w, qkv_b, out_w, fc_w, fc_b, proj_w, gains, shifts = weights
    head_count = D // HS
    column_start = layer_index * 3 * D
    feature_start = layer_index * D
    hidden_start = layer_index * FF
    feature_end = feature_start + D
    normed = low(layer_norm(values, gains[0, feature_start:feature_end], shifts[0, feature_start:feature_end]))
    projected = product(normed, qkv_w[:, column_start:column_start + 3 * D]) + qkv_b[column_start:column_start + 3 * D]
    projected = low(low_back(projected)).reshape(LEN, head_count, 3, HS)
    query_rows = projected[:, :, 0]
    key_rows = projected[:, :, 1]
    value_rows = projected[:, :, 2]
    raw = low_back(jnp.einsum('qhc,khc->hqk', query_rows, key_rows, precision=lax.Precision.HIGHEST))
    row_ids = lax.broadcasted_iota(jnp.int32, raw.shape, 1)
    col_ids = lax.broadcasted_iota(jnp.int32, raw.shape, 2)
    scores = jnp.where(col_ids <= row_ids, raw * (1.0 / math.sqrt(HS)), MASKED_SCORE)
    row_max = lax.optimization_barrier(jnp.max(scores, axis=2, keepdims=True))
    log_total = row_max + jnp.log(lax.optimization_barrier(jnp.sum(jnp.exp(scores - row_max), axis=2, keepdims=True)))
    probability = jnp.exp(scores - log_total)
    mixed_out = jnp.einsum('hqk,khc->qhc', low(probability), value_rows, precision=lax.Precision.HIGHEST)
    mixed_out = low(low_back(mixed_out.reshape(LEN, D)))
    branch = low_back(product(mixed_out, out_w[feature_start:feature_end]) + shifts[1, feature_start:feature_end])
    middle = values + branch
    normed_two = low(layer_norm(middle, gains[1, feature_start:feature_end], shifts[2, feature_start:feature_end]))
    pre_act = low_back(product(normed_two, fc_w[:, hidden_start:hidden_start + FF]) + fc_b[hidden_start:hidden_start + FF])
    activated = low(jax.nn.gelu(pre_act, approximate=True))
    branch_two = low_back(product(activated, proj_w[hidden_start:hidden_start + FF]) + shifts[3, feature_start:feature_end])
    return middle + branch_two

def spread_noise(noise):
    pieces = noise.astype(jnp.float32).reshape(N_SECTION, PARAMS_SECTION)
    layouts = (((D, 3 * D // 2), 1), ((3 * D // 2,), 0), ((D // 2, D), 0), ((D, FF // 2), 1), ((FF // 2,), 0), ((FF // 2, D), 0), ((2, D // 2), 1), ((4, D // 2), 1))
    offset = 0
    result = []
    for local_shape, axis_number in layouts:
        entry_count = math.prod(local_shape)
        section_block = pieces[:, offset:offset + entry_count].reshape((N_SECTION,) + local_shape)
        result.append(jnp.concatenate([section_block[section_number] for section_number in range(N_SECTION)], axis_number))
        offset = offset + entry_count
    return result

def reference(inputs, cotangent, included, qkv_weight, qkv_bias, out_weight, fc_weight, fc_bias, proj_weight, norm_gains, shifts, noise):
    clip_norm = CLIP_FRACTION * math.sqrt(LEN * FF * D)
    params = (qkv_weight.astype(jnp.float32), qkv_bias.astype(jnp.float32), out_weight.astype(jnp.float32), fc_weight.astype(jnp.float32), fc_bias.astype(jnp.float32), proj_weight.astype(jnp.float32), norm_gains.astype(jnp.float32), shifts.astype(jnp.float32))

    def two_layers(weights, values):
        first_out = low(low_back(apply_layer(weights, 0, values)))
        return (first_out, apply_layer(weights, 1, first_out))

    def per_sequence(totals, seq_items):
        seq_in, seq_cot, keep_flag = seq_items
        outputs_pair, pull_back = jax.vjp(two_layers, params, seq_in.astype(jnp.float32))
        first_out, second_out = outputs_pair
        param_grads, input_grad = pull_back((jnp.zeros_like(first_out), seq_cot.astype(jnp.float32)))
        squares = jnp.zeros((), jnp.float32)
        for grad_part in param_grads:
            squares = squares + jnp.sum(grad_part * grad_part)
        factor = jnp.minimum(1.0, clip_norm / jnp.sqrt(squares))
        weight = keep_flag.astype(jnp.float32) * factor
        totals = tuple((total_part + weight * grad_part for total_part, grad_part in zip(totals, param_grads)))
        return (totals, (first_out.astype(jnp.bfloat16), second_out.astype(jnp.bfloat16), input_grad.astype(jnp.bfloat16)))
    initial = tuple((jnp.zeros_like(part) for part in params))
    totals, outputs_all = lax.scan(per_sequence, initial, (inputs, cotangent, included))
    first_all, second_all, grad_all = outputs_all
    noise_parts = spread_noise(noise)
    denominator = SAMPLE_RATE * NSEQ
    finished = [(total_part + NOISE_MULT * clip_norm * noise_part) / denominator for total_part, noise_part in zip(totals, noise_parts)]
    layer_outputs = jnp.concatenate([first_all, second_all], axis=2)
    return (layer_outputs, grad_all, finished[0], finished[1], finished[2], finished[3], finished[4], finished[5], finished[6], finished[7])
```

```python
import functools
import math

import jax
import jax.numpy as jnp
from jax import lax
from jax.experimental import pallas as pl
from jax.experimental.pallas import tpu as pltpu
from jax.sharding import PartitionSpec as P

D = 768
FF = 3072
HS = 64
LEN = 1024
HALF = D // 2
QW = 3 * HALF
FW = FF // 2
PAIRS = HALF // 128
BT = 256
NB = LEN // BT

CLIP_FRACTION = 0.05
NOISE_MULT = 0.001
SAMPLE_RATE = 0.5
NORM_EPS = 1e-05
MASKED_SCORE = -1e30
VMEM_BYTES = 56 * 1024 * 1024

BF = jnp.bfloat16
F32 = jnp.float32


def mm(left, right):
    return lax.dot_general(left, right, (((1,), (0,)), ((), ())), preferred_element_type=F32)


def mm_nt(left, right):
    return lax.dot_general(left, right, (((1,), (1,)), ((), ())), preferred_element_type=F32)


def mm_tn(left, right):
    return lax.dot_general(left, right, (((0,), (0,)), ((), ())), preferred_element_type=F32)


def normalize(values):
    center = values - jnp.mean(values, axis=-1, keepdims=True)
    spread = jnp.mean(center * center, axis=-1, keepdims=True)
    scale = lax.rsqrt(spread + NORM_EPS)
    return center * scale, scale


def normalize_back(grad, unit, scale, gain):
    inner = grad * gain
    mean_inner = jnp.mean(inner, axis=-1, keepdims=True)
    mean_cross = jnp.mean(inner * unit, axis=-1, keepdims=True)
    return scale * (inner - mean_inner - unit * mean_cross)


def column_sum(values):
    return jnp.sum(values, axis=0, keepdims=True)


def block_rows(index):
    return pl.ds(pl.multiple_of(index * BT, BT), BT)


def lane_group(index, width=128):
    return pl.ds(pl.multiple_of(index * 128, 128), width)


def lower_lanes(rows=BT):
    return lax.broadcasted_iota(jnp.int32, (rows, 128), 1) < HS


def to_pairs(block, group):
    low = lower_lanes()
    start = 3 * 128 * group
    one, two, three = (block[:, start + 128 * i : start + 128 * (i + 1)] for i in range(3))
    query = jnp.where(low, one, two)
    key = pltpu.roll(jnp.where(low, three, one), HS, 1)
    value = jnp.where(low, two, three)
    return query, key, value


def from_pairs(query, key, value):
    low = lower_lanes()
    turned = pltpu.roll(key, HS, 1)
    return jnp.where(low, query, turned), jnp.where(low, value, query), jnp.where(low, turned, value)


def attention_forward_kernel(first, *refs):
    if first:
        (x_ref, gain_ref, shift_ref, wqkv_ref, bqkv_ref, wout_ref, a_ref, qkv_ref, o_ref, lse_ref, part_ref) = refs
    else:
        (h_ref, own_ref, recv_ref, last_ref, gain_ref, shift_ref, wqkv_ref, bqkv_ref, wout_ref) = refs[:9]
        (a_ref, qkv_ref, o_ref, lse_ref, part_ref, x_ref) = refs[9:]

    def project(index, carry):
        rows = block_rows(index)
        if first:
            values = x_ref[rows, :].astype(F32)
        else:
            total = h_ref[rows, :] + (own_ref[rows, :].astype(F32) + recv_ref[rows, :].astype(F32)) + last_ref[...]
            x_ref[rows, :] = total.astype(BF)
            values = total.astype(BF).astype(F32)
        unit, _ = normalize(values)
        a = (unit * gain_ref[...] + shift_ref[...]).astype(BF)
        a_ref[rows, :] = a
        projected = mm(a, wqkv_ref[...]) + bqkv_ref[...]
        for group in range(PAIRS):
            query, key, value = to_pairs(projected, group)
            start = 3 * 128 * group
            qkv_ref[rows, start : start + 128] = query.astype(BF) * 0.125
            qkv_ref[rows, start + 128 : start + 256] = key.astype(BF)
            qkv_ref[rows, start + 256 : start + 384] = value.astype(BF)
        return carry

    lax.fori_loop(0, NB, project, 0)

    def attend(group, carry):
        low = lower_lanes()
        keep_diag = lax.broadcasted_iota(jnp.int32, (BT, BT), 1) <= lax.broadcasted_iota(jnp.int32, (BT, BT), 0)
        for i in range(NB):
            past, here = i * BT, (i + 1) * BT
            query = qkv_ref[past:here, lane_group(3 * group)]
            mixed, largest = [], []
            for head in range(2):
                keep = low if head == 0 else jnp.logical_not(low)
                query_one = jnp.where(keep, query, jnp.zeros_like(query))
                diag = mm_nt(query_one, qkv_ref[past:here, lane_group(3 * group + 1)])
                diag = jnp.where(keep_diag, diag, MASKED_SCORE)
                top = jnp.max(diag, axis=1, keepdims=True)
                if i > 0:
                    left = mm_nt(query_one, qkv_ref[0:past, lane_group(3 * group + 1)])
                    top = jnp.maximum(top, jnp.max(left, axis=1, keepdims=True))
                value = qkv_ref[past:here, lane_group(3 * group + 2)]
                value = jnp.where(keep, value, jnp.ones_like(value))
                total = mm(jnp.exp(diag - top).astype(BF), value)
                if i > 0:
                    value = qkv_ref[0:past, lane_group(3 * group + 2)]
                    keep_left = lower_lanes(past) if head == 0 else jnp.logical_not(lower_lanes(past))
                    value = jnp.where(keep_left, value, jnp.ones_like(value))
                    total = total + mm(jnp.exp(left - top).astype(BF), value)
                mixed.append(total)
                largest.append(top)
            sums = pltpu.roll(jnp.where(low, mixed[1], mixed[0]), HS, 1)
            o_ref[past:here, lane_group(group)] = (jnp.where(low, mixed[0], mixed[1]) / sums).astype(BF)
            lse_ref[past:here, lane_group(group)] = jnp.where(low, largest[0], largest[1]) + jnp.log(sums)
        return carry

    lax.fori_loop(0, PAIRS, attend, 0)

    def leave(index, carry):
        rows = block_rows(index)
        part_ref[rows, :] = mm(o_ref[rows, :], wout_ref[...]).astype(BF)
        return carry

    lax.fori_loop(0, NB, leave, 0)


def params():
    return pltpu.CompilerParams(vmem_limit_bytes=VMEM_BYTES)


def shape(dims, kind):
    return jax.ShapeDtypeStruct(dims, kind)


def cost(flops, moved, transcendentals=0):
    return pl.CostEstimate(flops=int(flops), bytes_accessed=int(moved), transcendentals=int(transcendentals))


def attention_forward(first, args, weights):
    vmem = pl.BlockSpec(memory_space=pltpu.VMEM)
    outs = [
        shape((LEN, D), BF),
        shape((LEN, QW), BF),
        shape((LEN, HALF), BF),
        shape((LEN, HALF), F32),
        shape((LEN, D), BF),
    ]
    if not first:
        outs.append(shape((LEN, D), BF))
    operands = list(args) + list(weights)
    return pl.pallas_call(
        functools.partial(attention_forward_kernel, first),
        out_shape=outs,
        in_specs=[vmem] * len(operands),
        out_specs=[vmem] * len(outs),
        compiler_params=params(),
        cost_estimate=cost(1.2e10, 1.6e7, 4e6),
        name="attention_forward",
    )(*operands)


def gelu_parts(u):
    slope = math.sqrt(2.0 / math.pi)
    square = u * u
    t = jnp.tanh(u * (slope + (slope * 0.044715) * square))
    half = 0.5 + 0.5 * t
    derivative = half + (0.5 * u) * (1.0 - t * t) * (slope + (3.0 * slope * 0.044715) * square)
    return u * half, derivative


def feed_forward_kernel(both, *refs):
    if both:
        (x_ref, own_ref, recv_ref, dm_ref, row1_ref, gain_ref, shift_ref, wfc_ref, bfc_ref, wproj_ref) = refs[:10]
        (h_ref, c_ref, g_ref, part_ref, du_ref, dc_ref) = refs[10:]
    else:
        (x_ref, own_ref, recv_ref, row1_ref, gain_ref, shift_ref, wfc_ref, bfc_ref, wproj_ref) = refs[:9]
        (h_ref, c_ref, g_ref, part_ref, slope_ref) = refs[9:]
    h = x_ref[...].astype(F32) + (own_ref[...].astype(F32) + recv_ref[...].astype(F32) + row1_ref[...])
    h_ref[...] = h
    unit, _ = normalize(h)
    c = (unit * gain_ref[...] + shift_ref[...]).astype(BF)
    c_ref[...] = c
    width = 512
    part = jnp.zeros((BT, D), F32)
    dc = jnp.zeros((BT, D), F32)
    for start in range(0, FW, width):
        cols = slice(start, start + width)
        u = mm(c, wfc_ref[:, cols]) + bfc_ref[:, cols]
        g, slope = gelu_parts(u)
        g = g.astype(BF)
        g_ref[:, cols] = g
        part = part + mm(g, wproj_ref[cols, :])
        if both:
            du = (mm_nt(dm_ref[...], wproj_ref[cols, :]) * slope).astype(BF)
            du_ref[:, cols] = du
            dc = dc + mm_nt(du, wfc_ref[:, cols])
        else:
            slope_ref[:, cols] = slope.astype(BF)
    part_ref[...] = part.astype(BF)
    if both:
        dc_ref[...] = dc.astype(BF)


def rows_spec(width):
    return pl.BlockSpec((BT, width), lambda i: (i, 0))


def whole_spec(dims):
    return pl.BlockSpec(dims, lambda i: (0,) * len(dims))


def feed_forward(x, own, recv, weights, dm=None):
    both = dm is not None
    acts = [x, own, recv] + ([dm] if both else [])
    outs = [shape((LEN, D), F32), shape((LEN, D), BF), shape((LEN, FW), BF), shape((LEN, D), BF), shape((LEN, FW), BF)]
    out_specs = [rows_spec(D), rows_spec(D), rows_spec(FW), rows_spec(D), rows_spec(FW)]
    if both:
        outs.append(shape((LEN, D), BF))
        out_specs.append(rows_spec(D))
    return pl.pallas_call(
        functools.partial(feed_forward_kernel, both),
        grid=(NB,),
        out_shape=outs,
        in_specs=[rows_spec(D)] * len(acts) + [whole_spec(w.shape) for w in weights],
        out_specs=out_specs,
        compiler_params=params(),
        cost_estimate=cost(1e10 if both else 5e9, 2e7, 2e6),
        name="feed_forward",
    )(*acts, *weights)


def feed_back_kernel(
    dh_ref, own_ref, recv_ref, x_ref, gain_ref, slope_ref, wfc_ref, wproj_ref, dm_ref, du_ref, dc_ref, sums_ref
):
    unit, scale = normalize(x_ref[...].astype(F32))
    da = own_ref[...].astype(F32) + recv_ref[...].astype(F32)

    @pl.when(pl.program_id(0) == 0)
    def _():
        sums_ref[...] = jnp.zeros_like(sums_ref)

    sums_ref[0:1, :] += column_sum(da * unit)
    sums_ref[1:2, :] += column_sum(da)
    dm = (dh_ref[...] + normalize_back(da, unit, scale, gain_ref[...])).astype(BF)
    dm_ref[...] = dm
    width = 512
    dc = jnp.zeros((BT, D), F32)
    for start in range(0, FW, width):
        cols = slice(start, start + width)
        du = (mm_nt(dm, wproj_ref[cols, :]) * slope_ref[:, cols].astype(F32)).astype(BF)
        du_ref[:, cols] = du
        dc = dc + mm_nt(du, wfc_ref[:, cols])
    dc_ref[...] = dc.astype(BF)


def feed_back(dh, own, recv, x, gain, slope, wfc, wproj):
    return pl.pallas_call(
        feed_back_kernel,
        grid=(NB,),
        out_shape=[shape((LEN, D), BF), shape((LEN, FW), BF), shape((LEN, D), BF), shape((8, D), F32)],
        in_specs=[rows_spec(D)] * 4
        + [whole_spec((1, D)), rows_spec(FW), whole_spec((D, FW)), whole_spec((FW, D))],
        out_specs=[rows_spec(D), rows_spec(FW), rows_spec(D), whole_spec((8, D))],
        compiler_params=params(),
        cost_estimate=cost(5e9, 2e7),
        name="feed_back",
    )(dh, own, recv, x, gain, slope, wfc, wproj)


def input_back_kernel(dh_ref, own_ref, recv_ref, x_ref, gain_ref, dx_ref, sums_ref):
    unit, scale = normalize(x_ref[...].astype(F32))
    da = own_ref[...].astype(F32) + recv_ref[...].astype(F32)

    @pl.when(pl.program_id(0) == 0)
    def _():
        sums_ref[...] = jnp.zeros_like(sums_ref)

    sums_ref[0:1, :] += column_sum(da * unit)
    sums_ref[1:2, :] += column_sum(da)
    dx_ref[...] = (dh_ref[...] + normalize_back(da, unit, scale, gain_ref[...])).astype(BF)


def input_back(dh, own, recv, x, gain):
    return pl.pallas_call(
        input_back_kernel,
        grid=(NB,),
        out_shape=[shape((LEN, D), BF), shape((8, D), F32)],
        in_specs=[rows_spec(D)] * 4 + [whole_spec((1, D))],
        out_specs=[rows_spec(D), whole_spec((8, D))],
        compiler_params=params(),
        cost_estimate=cost(1e7, 1e7),
        name="input_back",
    )(dh, own, recv, x, gain)


def in_three(values, spots):
    high = values.astype(BF)
    rest = values - high.astype(F32)
    middle = rest.astype(BF)
    low = (rest - middle.astype(F32)).astype(BF)
    return jnp.where(spots == 0, high, jnp.where(spots == 1, middle, jnp.where(spots == 2, low, jnp.zeros_like(low))))


def attention_back_kernel(
    dm_ref, own_ref, recv_ref, h_ref, gain_ref, wout_ref, qkv_ref, o_ref, lse_ref, wqkv_ref,
    dh_ref, dz_ref, dqkv_ref, da_ref, sums_ref, bias_ref,
    do_ref, dk_ref, dv_ref,
):
    sums_ref[...] = jnp.zeros_like(sums_ref)
    bias_ref[...] = jnp.zeros_like(bias_ref)

    def enter(index, carry):
        rows = block_rows(index)
        unit, scale = normalize(h_ref[rows, :])
        dc = own_ref[rows, :].astype(F32) + recv_ref[rows, :].astype(F32)
        sums_ref[0:1, :] += column_sum(dc * unit)
        sums_ref[1:2, :] += column_sum(dc)
        dh = dm_ref[rows, :].astype(F32) + normalize_back(dc, unit, scale, gain_ref[...])
        dh_ref[rows, :] = dh
        dz = dh.astype(BF)
        dz_ref[rows, :] = dz
        sums_ref[2:3, :] += column_sum(dz.astype(F32))
        sums_ref[3:4, :] += column_sum(dm_ref[rows, :].astype(F32))
        do_ref[rows, :] = mm_nt(dz, wout_ref[...]).astype(BF)
        return carry

    lax.fori_loop(0, NB, enter, 0)

    def attend(group, carry):
        low = lower_lanes()
        spots = lax.broadcasted_iota(jnp.int32, (BT, 128), 1) % HS
        ones = jnp.where(spots < 3, jnp.ones((BT, 128), BF), jnp.zeros((BT, 128), BF))
        keep_diag = lax.broadcasted_iota(jnp.int32, (BT, BT), 0) <= lax.broadcasted_iota(jnp.int32, (BT, BT), 1)
        nothing = jnp.zeros((BT, 128), BF)
        dk_ref[...] = jnp.zeros_like(dk_ref)
        dv_ref[...] = jnp.zeros_like(dv_ref)
        for i in range(NB):
            mine = slice(i * BT, (i + 1) * BT)
            query = qkv_ref[mine, lane_group(3 * group)]
            do = do_ref[mine, lane_group(group)]
            lse = in_three(-pltpu.roll(lse_ref[mine, lane_group(group)], HS, 1), spots)
            inner = do.astype(F32) * o_ref[mine, lane_group(group)].astype(F32)
            t_low = jnp.sum(jnp.where(low, inner, 0.0), axis=1, keepdims=True)
            t_high = jnp.sum(jnp.where(low, 0.0, inner), axis=1, keepdims=True)
            t = in_three(-jnp.where(low, t_high, t_low), spots)
            query_with = (jnp.where(low, query, lse), jnp.where(low, lse, query))
            do_with = (jnp.where(low, do, t), jnp.where(low, t, do))
            query_one = (jnp.where(low, query, nothing), jnp.where(low, nothing, query))
            do_one = (jnp.where(low, do, nothing), jnp.where(low, nothing, do))
            dq = jnp.zeros((BT, 128), F32)
            for j in range(i + 1):
                theirs = slice(j * BT, (j + 1) * BT)
                key = qkv_ref[theirs, lane_group(3 * group + 1)]
                value = qkv_ref[theirs, lane_group(3 * group + 2)]
                dv = jnp.zeros((BT, 128), F32)
                dk = jnp.zeros((BT, 128), F32)
                for head in range(2):
                    key_with = jnp.where(low, key, ones) if head == 0 else jnp.where(low, ones, key)
                    value_with = jnp.where(low, value, ones) if head == 0 else jnp.where(low, ones, value)
                    key_one = jnp.where(low, key, nothing) if head == 0 else jnp.where(low, nothing, key)
                    score = mm_nt(key_with, query_with[head])
                    if i == j:
                        score = jnp.where(keep_diag, score, MASKED_SCORE)
                    p = jnp.exp(score)
                    ds = (p * mm_nt(value_with, do_with[head])).astype(BF)
                    dv = dv + mm(p.astype(BF), do_one[head])
                    dk = dk + mm(ds, query_one[head])
                    dq = dq + mm_tn(ds, key_one)
                dv_ref[theirs, :] += dv
                dk_ref[theirs, :] += dk
            dq = dq * 0.125
            dqkv_ref[mine, lane_group(3 * group)] = dq.astype(BF)
        for i in range(NB):
            mine = slice(i * BT, (i + 1) * BT)
            one, two, three = from_pairs(
                dqkv_ref[mine, lane_group(3 * group)].astype(F32), dk_ref[mine, :], dv_ref[mine, :]
            )
            dqkv_ref[mine, lane_group(3 * group)] = one.astype(BF)
            dqkv_ref[mine, lane_group(3 * group + 1)] = two.astype(BF)
            dqkv_ref[mine, lane_group(3 * group + 2)] = three.astype(BF)
        return carry

    lax.fori_loop(0, PAIRS, attend, 0)

    def leave(index, carry):
        rows = block_rows(index)
        dqkv = dqkv_ref[rows, :]
        bias_ref[0:1, :] += column_sum(dqkv.astype(F32))
        da_ref[rows, :] = mm_nt(dqkv, wqkv_ref[...]).astype(BF)
        return carry

    lax.fori_loop(0, NB, leave, 0)


def attention_back(dm, own, recv, h, gain, wout, qkv, o, lse, wqkv):
    vmem = pl.BlockSpec(memory_space=pltpu.VMEM)
    outs = [
        shape((LEN, D), F32),
        shape((LEN, D), BF),
        shape((LEN, QW), BF),
        shape((LEN, D), BF),
        shape((8, D), F32),
        shape((8, QW), F32),
    ]
    return pl.pallas_call(
        attention_back_kernel,
        out_shape=outs,
        in_specs=[vmem] * 10,
        out_specs=[vmem] * len(outs),
        scratch_shapes=[pltpu.VMEM((LEN, HALF), BF), pltpu.VMEM((LEN, 128), F32), pltpu.VMEM((LEN, 128), F32)],
        compiler_params=params(),
        cost_estimate=cost(2.2e10, 2.2e7, 4e6),
        name="attention_back",
    )(dm, own, recv, h, gain, wout, qkv, o, lse, wqkv)


def weight_grad_kernel(left_ref, right_ref, grad_ref, square_ref, sums_ref):
    @pl.when(pl.program_id(0) == 0)
    def _():
        square_ref[...] = jnp.zeros_like(square_ref)
        sums_ref[...] = jnp.zeros_like(sums_ref)
        sums_ref[0:1, :] = column_sum(right_ref[...].astype(F32))

    grad = mm_tn(left_ref[...], right_ref[...])
    grad_ref[...] = grad.astype(BF)
    square_ref[0:1, :] += column_sum(grad * grad)


def weight_grad(left, right, rows):
    tall, wide = left.shape[1], right.shape[1]
    return pl.pallas_call(
        weight_grad_kernel,
        grid=(tall // rows,),
        out_shape=[shape((tall, wide), BF), shape((8, wide), F32), shape((8, wide), F32)],
        in_specs=[pl.BlockSpec((LEN, rows), lambda i: (0, i)), whole_spec((LEN, wide))],
        out_specs=[pl.BlockSpec((rows, wide), lambda i: (i, 0)), whole_spec((8, wide)), whole_spec((8, wide))],
        compiler_params=params(),
        cost_estimate=cost(2 * LEN * tall * wide, 2 * (LEN * (tall + wide) + tall * wide)),
        name="weight_grad",
    )(left, right)


def send(values, route):
    sections, ranks = lax.axis_size("section"), lax.axis_size("dp")
    pairs = []
    for section in range(sections):
        for rank in range(ranks):
            target = route(section, rank // 2, rank % 2)
            if target is not None:
                to_section, to_pair, to_core = target
                pairs.append((section * ranks + rank, to_section * ranks + to_pair * 2 + to_core))
    return lax.ppermute(values, ("section", "dp"), pairs)


def swap_cores(values):
    return send(values, lambda s, z, c: (s, z, 1 - c))


def is_home(s, c):
    return s % 2 == c


def local(
    inputs,
    cotangent,
    included,
    qkv_weight,
    qkv_bias,
    out_weight,
    fc_weight,
    fc_bias,
    proj_weight,
    norm_gains,
    shifts,
    noise,
):
    clip_norm = CLIP_FRACTION * math.sqrt(LEN * FF * D)
    section = lax.axis_index("section")
    rank = lax.axis_index("dp")
    ranks = lax.axis_size("dp")
    row, half = section // 2, section % 2
    place, core = rank // 2, rank % 2
    home = half == core
    on_top = row == 0

    small = jnp.concatenate([qkv_bias, fc_bias, norm_gains.reshape(-1), shifts.reshape(-1)])
    small_all = lax.all_gather(small, "section")

    def own_sequence(values):
        mine = lax.dynamic_index_in_dim(values, half, 0, keepdims=False)
        theirs = swap_cores(mine)
        return jnp.where(core == row, mine, theirs)

    x0 = own_sequence(inputs)
    cot = own_sequence(cotangent)
    drawn = own_sequence(jnp.broadcast_to(included.astype(F32)[:, None, None], (2, 8, 128)))[0, 0]

    def near(s, z, c):
        return (s, z, c) if is_home(s, c) else (s ^ 1, z, 1 - c)

    def far(s, z, c):
        return (s ^ 2, z, c) if is_home(s, c) else (s ^ 3, z, 1 - c)

    def both_layers(weight):
        here, there = send(weight, near), send(weight, far)
        return jnp.where(on_top, here, there), jnp.where(on_top, there, here)

    wqkv = both_layers(qkv_weight)
    wout = both_layers(out_weight)
    wfc = both_layers(fc_weight)
    wproj = both_layers(proj_weight)

    def small_of(layer):
        lower, upper = small_all[2 * layer], small_all[2 * layer + 1]
        mine = jnp.where(core == 0, lower, upper)
        bqkv = mine[:QW].reshape(1, QW)
        bfc = mine[QW : QW + FW].reshape(1, FW)
        start = QW + FW
        rows = [
            jnp.concatenate(
                [part[start + i * HALF : start + (i + 1) * HALF] for part in (lower, upper)]
            ).reshape(1, D)
            for i in range(6)
        ]
        return bqkv, bfc, rows[:2], rows[2:]

    bqkv0, bfc0, gains0, shifts0 = small_of(0)
    bqkv1, bfc1, gains1, shifts1 = small_of(1)

    a0, qkv0, o0, lse0, part = attention_forward(
        True, (x0,), (gains0[0], shifts0[0], wqkv[0], bqkv0, wout[0])
    )
    h0, c0, g0, part_two, slope0 = feed_forward(
        x0, part, swap_cores(part), (shifts0[1], gains0[1], shifts0[2], wfc[0], bfc0, wproj[0])
    )
    a1, qkv1, o1, lse1, part, x1 = attention_forward(
        False, (h0, part_two, swap_cores(part_two), shifts0[3]), (gains1[0], shifts1[0], wqkv[1], bqkv1, wout[1])
    )
    h1, c1, g1, part_two, du1, dc = feed_forward(
        x1, part, swap_cores(part), (shifts1[1], gains1[1], shifts1[2], wfc[1], bfc1, wproj[1]), cot
    )
    dc_theirs = swap_cores(dc)
    y1 = (h1 + (part_two.astype(F32) + swap_cores(part_two).astype(F32)) + shifts1[3]).astype(BF)

    def cross(values):
        return send(values, lambda s, z, c: None if is_home(s, c) else (s ^ 1, z, c))

    def weight_grads_one(g, dm, c, du):
        proj, proj_squares, proj_sums = weight_grad(g, dm, 256)
        proj_there = cross(proj)
        fc, fc_squares, fc_sums = weight_grad(c, du, 256)
        fc_there = cross(fc)
        return (proj, proj_there), (fc, fc_there), fc_sums[0], jnp.sum(proj_squares) + jnp.sum(fc_squares)

    def weight_grads_two(o, dz, a, dqkv):
        out, out_squares, _ = weight_grad(o, dz, 128)
        out_there = cross(out)
        qkv, qkv_squares, _ = weight_grad(a, dqkv, 256)
        qkv_there = cross(qkv)
        return (out, out_there), (qkv, qkv_there), jnp.sum(out_squares) + jnp.sum(qkv_squares)

    def small_grads(bias_qkv, bias_fc, first_sums, second_sums):
        rows = jnp.stack([first_sums[0], second_sums[0], first_sums[1], second_sums[2], second_sums[1], second_sums[3]])
        rows = lax.dynamic_slice_in_dim(rows, core * HALF, HALF, 1)
        return jnp.concatenate([bias_qkv, bias_fc, rows.reshape(-1)])

    proj1, fc1, bias_fc1, squares_one1 = weight_grads_one(g1, cot, c1, du1)
    dh1, dz1, dqkv1, da, sums1, bias_qkv1 = attention_back(
        cot, dc, dc_theirs, h1, gains1[1], wout[1], qkv1, o1, lse1, wqkv[1]
    )
    da_theirs = swap_cores(da)
    out1, qkvg1, squares_two1 = weight_grads_two(o1, dz1, a1, dqkv1)
    dm0, du0, dc, first_sums1 = feed_back(dh1, da, da_theirs, x1, gains1[0], slope0, wfc[0], wproj[0])
    dc_theirs = swap_cores(dc)
    proj0, fc0, bias_fc0, squares_one0 = weight_grads_one(g0, dm0, c0, du0)
    dh0, dz0, dqkv0, da, sums0, bias_qkv0 = attention_back(
        dm0, dc, dc_theirs, h0, gains0[1], wout[0], qkv0, o0, lse0, wqkv[0]
    )
    da_theirs = swap_cores(da)
    out0, qkvg0, squares_two0 = weight_grads_two(o0, dz0, a0, dqkv0)
    dx0, first_sums0 = input_back(dh0, da, da_theirs, x0, gains0[0])

    small0 = small_grads(bias_qkv0[0], bias_fc0, first_sums0, sums0)
    small1 = small_grads(bias_qkv1[0], bias_fc1, first_sums1, sums1)
    small_pair = jnp.stack([small0, small1])
    small_there = cross(small_pair)

    squares = squares_one0 + squares_two0 + squares_one1 + squares_two1 + jnp.sum(small_pair * small_pair)
    squares = jnp.broadcast_to(squares, (8, 128))
    squares = squares + swap_cores(squares)
    factor = drawn * jnp.minimum(1.0, clip_norm / jnp.sqrt(squares))
    factor_there = cross(factor)
    mine, theirs = factor[0, 0], factor_there[0, 0]

    def spread(block_for):
        received = []
        for step in range(2):
            block = block_for(2 * core + (step ^ half))
            received.append(send(block, lambda s, z, c, step=step: (2 * c + (step ^ (s % 2)), z, s // 2)))
        first, second = received
        return jnp.where(half == 0, jnp.stack([first, second]), jnp.stack([second, first]))

    both_out = jnp.concatenate([x1, y1], axis=1)
    layer_out = spread(lambda block: lax.dynamic_slice_in_dim(both_out, block * HALF, HALF, 1))
    token_rows = LEN // 4
    input_grad = spread(lambda block: lax.dynamic_slice_in_dim(dx0, block * token_rows, token_rows, 0))

    places = ranks // 2
    middle = places // 2
    denominator = SAMPLE_RATE * inputs.shape[0] * ranks

    def to_middle(step):
        def route(s, z, c):
            if not is_home(s, c):
                return None
            if z == step:
                return (s, z + 1, c)
            if z == places - 1 - step:
                return (s, z - 1, c)
            return None

        return route

    def at_middle(s, z, c):
        if not is_home(s, c):
            return None
        return (s, places - 1 - z, c) if z in (middle - 1, middle) else None

    def from_middle(step):
        def route(s, z, c):
            if not is_home(s, c):
                return None
            if z == middle - 1 - step:
                return (s, z - 1, c)
            if z == middle + step:
                return (s, z + 1, c)
            return None

        return route

    def summed(top, bottom):
        top_here, top_there = top
        bottom_here, bottom_there = bottom

        def weighted(here, there):
            return mine * here.astype(F32) + theirs * there.astype(F32)

        other = weighted(
            jnp.where(on_top, bottom_here, top_here), jnp.where(on_top, bottom_there, top_there)
        ).astype(BF)
        keep = weighted(jnp.where(on_top, top_here, bottom_here), jnp.where(on_top, top_there, bottom_there))
        arrived = send(other, lambda s, z, c: (s ^ 2, z, c) if is_home(s, c) else None)
        total = (keep + arrived.astype(F32)).astype(BF)
        for step in range(middle - 1):
            total = (total.astype(F32) + send(total, to_middle(step)).astype(F32)).astype(BF)
        if places > 1:
            total = (total.astype(F32) + send(total, at_middle).astype(F32)).astype(BF)
        for step in range(middle - 1):
            arrived = send(total, from_middle(step))
            takes = (place == middle - 2 - step) | (place == middle + 1 + step)
            total = jnp.where(takes, arrived, total)
        across = send(total, lambda s, z, c: (s, z, 1 - c) if is_home(s, c) else None)
        return jnp.where(home, total, across).astype(F32)

    noise_values = noise.astype(F32)

    def finish(total, offset):
        part = noise_values[offset : offset + total.size].reshape(total.shape)
        return (total + NOISE_MULT * clip_norm * part) / denominator

    shapes = ((D, QW), (QW,), (HALF, D), (D, FW), (FW,), (FW, D), (2, HALF), (4, HALF))
    offsets = [0]
    for dims in shapes:
        offsets.append(offsets[-1] + math.prod(dims))

    proj_sum = summed(proj0, proj1)
    fc_sum = summed(fc0, fc1)
    out_sum = summed(out0, out1)
    qkv_sum = summed(qkvg0, qkvg1)
    small_sum = summed((small_pair[0], small_there[0]), (small_pair[1], small_there[1]))
    bounds = [0, QW, QW + FW, QW + FW + 2 * HALF, QW + FW + 6 * HALF]
    small_parts = [small_sum[a:b] for a, b in zip(bounds[:-1], bounds[1:])]
    return (
        layer_out,
        input_grad,
        finish(qkv_sum, offsets[0]),
        finish(small_parts[0], offsets[1]),
        finish(out_sum, offsets[2]),
        finish(fc_sum, offsets[3]),
        finish(small_parts[1], offsets[4]),
        finish(proj_sum, offsets[5]),
        finish(small_parts[2].reshape(2, HALF), offsets[6]),
        finish(small_parts[3].reshape(4, HALF), offsets[7]),
    )


def solution(mesh):
    return jax.shard_map(
        local,
        mesh=mesh,
        in_specs=(
            P("dp", None, None),
            P("dp", None, None),
            P("dp"),
            P(None, "section"),
            P("section"),
            P("section", None),
            P(None, "section"),
            P("section"),
            P("section", None),
            P(None, "section"),
            P(None, "section"),
            P("section"),
        ),
        out_specs=(
            P("dp", None, "section"),
            P("dp", "section", None),
            P(None, "section"),
            P("section"),
            P("section", None),
            P(None, "section"),
            P("section"),
            P("section", None),
            P(None, "section"),
            P(None, "section"),
        ),
        check_vma=False,
    )
```

```python
import functools
import math

import jax
import jax.numpy as jnp
from jax import lax
from jax.experimental import pallas as pl
from jax.experimental.pallas import tpu as pltpu
from jax.sharding import PartitionSpec as P

D = 768
FF = 3072
HS = 64
LEN = 1024
HALF = D // 2
QW = 3 * HALF
FW = FF // 2
PAIRS = HALF // 128
BT = 256
NB = LEN // BT

CLIP_FRACTION = 0.05
NOISE_MULT = 0.001
SAMPLE_RATE = 0.5
NORM_EPS = 1e-05
MASKED_SCORE = -1e30
VMEM_BYTES = 56 * 1024 * 1024

BF = jnp.bfloat16
F32 = jnp.float32


def mm(left, right):
    return lax.dot_general(left, right, (((1,), (0,)), ((), ())), preferred_element_type=F32)


def mm_nt(left, right):
    return lax.dot_general(left, right, (((1,), (1,)), ((), ())), preferred_element_type=F32)


def mm_tn(left, right):
    return lax.dot_general(left, right, (((0,), (0,)), ((), ())), preferred_element_type=F32)


def normalize(values):
    center = values - jnp.mean(values, axis=-1, keepdims=True)
    spread = jnp.mean(center * center, axis=-1, keepdims=True)
    scale = lax.rsqrt(spread + NORM_EPS)
    return center * scale, scale


def normalize_back(grad, unit, scale, gain):
    inner = grad * gain
    mean_inner = jnp.mean(inner, axis=-1, keepdims=True)
    mean_cross = jnp.mean(inner * unit, axis=-1, keepdims=True)
    return scale * (inner - mean_inner - unit * mean_cross)


def column_sum(values):
    return jnp.sum(values, axis=0, keepdims=True)


def block_rows(index):
    return pl.ds(pl.multiple_of(index * BT, BT), BT)


def lane_group(index, width=128):
    return pl.ds(pl.multiple_of(index * 128, 128), width)


def lower_lanes(rows=BT):
    return lax.broadcasted_iota(jnp.int32, (rows, 128), 1) < HS


def to_pairs(block, group):
    low = lower_lanes()
    start = 3 * 128 * group
    one, two, three = (block[:, start + 128 * i : start + 128 * (i + 1)] for i in range(3))
    query = jnp.where(low, one, two)
    key = pltpu.roll(jnp.where(low, three, one), HS, 1)
    value = jnp.where(low, two, three)
    return query, key, value


def from_pairs(query, key, value):
    low = lower_lanes()
    turned = pltpu.roll(key, HS, 1)
    return jnp.where(low, query, turned), jnp.where(low, value, query), jnp.where(low, turned, value)


def start_fetch(which_ref, sources, target, sem):
    half = target.shape[0] // 2

    @pl.when(which_ref[0] == 0)
    def _():
        pltpu.make_async_copy(sources[0], target, sem).start()

    for number in (1, 2):
        for side in range(2):

            @pl.when((which_ref[0] == number) & (which_ref[1] == side))
            def _(number=number, side=side):
                one, two = sources[2 * number - 1 : 2 * number + 1]
                pltpu.make_async_copy(one, target.at[pl.ds(side * half, half)], sem).start()
                pltpu.make_async_copy(two, target.at[pl.ds((1 - side) * half, half)], sem).start()


def end_fetch(sources, target, sem):
    pltpu.make_async_copy(sources[0], target, sem).wait()


def attention_forward_kernel(layer, *refs):
    which_ref, wqkv_from, wout_from, refs = refs[0], refs[1:6], refs[6:11], refs[11:]
    vec_ref, bqkv_ref, refs = refs[0], refs[1], refs[2:]
    first = layer == 0
    if first:
        (x_ref, a_ref, qkv_ref, o_ref, lse_ref, part_ref, wqkv_ref, wout_ref, sems) = refs
    else:
        (h_ref, own_ref, recv_ref, a_ref, qkv_ref, o_ref, lse_ref, part_ref, x_ref, wqkv_ref, wout_ref, sems) = refs
    start_fetch(which_ref, wqkv_from, wqkv_ref, sems.at[0])
    start_fetch(which_ref, wout_from, wout_ref, sems.at[1])
    end_fetch(wqkv_from, wqkv_ref, sems.at[0])

    def project(index, carry):
        rows = block_rows(index)
        if first:
            values = x_ref[rows, :].astype(F32)
        else:
            total = h_ref[rows, :] + (own_ref[rows, :].astype(F32) + recv_ref[rows, :].astype(F32)) + vec_ref[5:6, :]
            x_ref[rows, :] = total.astype(BF)
            values = total.astype(BF).astype(F32)
        unit, _ = normalize(values)
        a = (unit * vec_ref[8 * layer : 8 * layer + 1, :] + vec_ref[8 * layer + 2 : 8 * layer + 3, :]).astype(BF)
        a_ref[rows, :] = a
        projected = mm(a, wqkv_ref[...]) + bqkv_ref[layer : layer + 1, :]
        for group in range(PAIRS):
            query, key, value = to_pairs(projected, group)
            start = 3 * 128 * group
            qkv_ref[rows, start : start + 128] = query.astype(BF) * 0.125
            qkv_ref[rows, start + 128 : start + 256] = key.astype(BF)
            qkv_ref[rows, start + 256 : start + 384] = value.astype(BF)
        return carry

    lax.fori_loop(0, NB, project, 0)

    def attend(group, carry):
        low = lower_lanes()
        keep_diag = lax.broadcasted_iota(jnp.int32, (BT, BT), 1) <= lax.broadcasted_iota(jnp.int32, (BT, BT), 0)
        for i in range(NB):
            past, here = i * BT, (i + 1) * BT
            query = qkv_ref[past:here, lane_group(3 * group)]
            mixed, largest = [], []
            for head in range(2):
                keep = low if head == 0 else jnp.logical_not(low)
                query_one = jnp.where(keep, query, jnp.zeros_like(query))
                diag = mm_nt(query_one, qkv_ref[past:here, lane_group(3 * group + 1)])
                diag = jnp.where(keep_diag, diag, MASKED_SCORE)
                top = jnp.max(diag, axis=1, keepdims=True)
                if i > 0:
                    left = mm_nt(query_one, qkv_ref[0:past, lane_group(3 * group + 1)])
                    top = jnp.maximum(top, jnp.max(left, axis=1, keepdims=True))
                value = qkv_ref[past:here, lane_group(3 * group + 2)]
                value = jnp.where(keep, value, jnp.ones_like(value))
                total = mm(jnp.exp(diag - top).astype(BF), value)
                if i > 0:
                    value = qkv_ref[0:past, lane_group(3 * group + 2)]
                    keep_left = lower_lanes(past) if head == 0 else jnp.logical_not(lower_lanes(past))
                    value = jnp.where(keep_left, value, jnp.ones_like(value))
                    total = total + mm(jnp.exp(left - top).astype(BF), value)
                mixed.append(total)
                largest.append(top)
            sums = pltpu.roll(jnp.where(low, mixed[1], mixed[0]), HS, 1)
            o_ref[past:here, lane_group(group)] = (jnp.where(low, mixed[0], mixed[1]) / sums).astype(BF)
            lse_ref[past:here, lane_group(group)] = jnp.where(low, largest[0], largest[1]) + jnp.log(sums)
        return carry

    lax.fori_loop(0, PAIRS, attend, 0)

    end_fetch(wout_from, wout_ref, sems.at[1])

    def leave(index, carry):
        rows = block_rows(index)
        part_ref[rows, :] = mm(o_ref[rows, :], wout_ref[...]).astype(BF)
        return carry

    lax.fori_loop(0, NB, leave, 0)


def params():
    return pltpu.CompilerParams(vmem_limit_bytes=VMEM_BYTES)


def shape(dims, kind):
    return jax.ShapeDtypeStruct(dims, kind)


def cost(flops, moved, transcendentals=0):
    return pl.CostEstimate(flops=int(flops) // 1000, bytes_accessed=int(moved) // 1000, transcendentals=0)


def specs(*counts):
    return (
        [pl.BlockSpec(memory_space=pltpu.SMEM)]
        + [pl.BlockSpec(memory_space=pl.ANY)] * counts[0]
        + [pl.BlockSpec(memory_space=pltpu.VMEM)] * counts[1]
    )


def attention_forward(layer, which, wqkv, wout, vecs, bqkv, *acts):
    outs = [
        shape((LEN, D), BF),
        shape((LEN, QW), BF),
        shape((LEN, HALF), BF),
        shape((LEN, HALF), F32),
        shape((LEN, D), BF),
    ]
    if layer:
        outs.append(shape((LEN, D), BF))
    return pl.pallas_call(
        functools.partial(attention_forward_kernel, layer),
        out_shape=outs,
        in_specs=specs(10, 2 + len(acts)),
        out_specs=[pl.BlockSpec(memory_space=pltpu.VMEM)] * len(outs),
        scratch_shapes=[pltpu.VMEM((D, QW), BF), pltpu.VMEM((HALF, D), BF), pltpu.SemaphoreType.DMA((2,))],
        compiler_params=params(),
        cost_estimate=cost(1.2e10, 1.6e7, 4e6),
        name="attention_forward",
    )(which, *wqkv, *wout, vecs, bqkv, *acts)


def gelu_parts(u):
    slope = math.sqrt(2.0 / math.pi)
    square = u * u
    t = jnp.tanh(u * (slope + (slope * 0.044715) * square))
    half = 0.5 + 0.5 * t
    derivative = half + (0.5 * u) * (1.0 - t * t) * (slope + (3.0 * slope * 0.044715) * square)
    return u * half, derivative


def feed_forward_kernel(layer, *refs):
    both = layer == 1
    which_ref, wfc_from, wproj_from, refs = refs[0], refs[1:6], refs[6:11], refs[11:]
    vec_ref, bfc_ref, refs = refs[0], refs[1], refs[2:]
    if both:
        (x_ref, own_ref, recv_ref, dm_ref, h_ref, c_ref, g_ref, part_ref, du_ref, dc_ref) = refs[:10]
    else:
        (x_ref, own_ref, recv_ref, h_ref, c_ref, g_ref, part_ref, slope_ref) = refs[:8]
    wfc_ref, wproj_ref, sems = refs[-3:]
    base = 8 * layer

    @pl.when(pl.program_id(0) == 0)
    def _():
        start_fetch(which_ref, wfc_from, wfc_ref, sems.at[0])
        start_fetch(which_ref, wproj_from, wproj_ref, sems.at[1])

    h = x_ref[...].astype(F32) + (
        own_ref[...].astype(F32) + recv_ref[...].astype(F32) + vec_ref[base + 3 : base + 4, :]
    )
    h_ref[...] = h
    unit, _ = normalize(h)
    c = (unit * vec_ref[base + 1 : base + 2, :] + vec_ref[base + 4 : base + 5, :]).astype(BF)
    c_ref[...] = c

    @pl.when(pl.program_id(0) == 0)
    def _():
        end_fetch(wfc_from, wfc_ref, sems.at[0])
        end_fetch(wproj_from, wproj_ref, sems.at[1])

    width = 512
    part = jnp.zeros((BT, D), F32)
    dc = jnp.zeros((BT, D), F32)
    for start in range(0, FW, width):
        cols = slice(start, start + width)
        u = mm(c, wfc_ref[:, cols]) + bfc_ref[layer : layer + 1, cols]
        g, slope = gelu_parts(u)
        g = g.astype(BF)
        g_ref[:, cols] = g
        part = part + mm(g, wproj_ref[cols, :])
        if both:
            du = (mm_nt(dm_ref[...], wproj_ref[cols, :]) * slope).astype(BF)
            du_ref[:, cols] = du
            dc = dc + mm_nt(du, wfc_ref[:, cols])
        else:
            slope_ref[:, cols] = slope.astype(BF)
    part_ref[...] = part.astype(BF)
    if both:
        dc_ref[...] = dc.astype(BF)


def rows_spec(width):
    return pl.BlockSpec((BT, width), lambda i: (i, 0))


def whole_spec(dims):
    return pl.BlockSpec(dims, lambda *i: (0,) * len(dims))


def feed_weights():
    return [pltpu.VMEM((D, FW), BF), pltpu.VMEM((FW, D), BF), pltpu.SemaphoreType.DMA((2,))]


def feed_forward(layer, which, wfc, wproj, vecs, bfc, *acts):
    both = layer == 1
    outs = [shape((LEN, D), F32), shape((LEN, D), BF), shape((LEN, FW), BF), shape((LEN, D), BF), shape((LEN, FW), BF)]
    out_specs = [rows_spec(D), rows_spec(D), rows_spec(FW), rows_spec(D), rows_spec(FW)]
    if both:
        outs.append(shape((LEN, D), BF))
        out_specs.append(rows_spec(D))
    return pl.pallas_call(
        functools.partial(feed_forward_kernel, layer),
        grid=(NB,),
        out_shape=outs,
        in_specs=specs(10, 0) + [whole_spec(vecs.shape), whole_spec(bfc.shape)] + [rows_spec(D)] * len(acts),
        out_specs=out_specs,
        scratch_shapes=feed_weights(),
        compiler_params=params(),
        cost_estimate=cost(1e10 if both else 5e9, 2e7, 2e6),
        name="feed_forward",
    )(which, *wfc, *wproj, vecs, bfc, *acts)


def feed_back_kernel(*refs):
    which_ref, wfc_from, wproj_from, refs = refs[0], refs[1:6], refs[6:11], refs[11:]
    (vec_ref, dh_ref, own_ref, recv_ref, x_ref, slope_ref, dm_ref, du_ref, dc_ref, sums_ref) = refs[:10]
    wfc_ref, wproj_ref, sems = refs[10:]

    @pl.when(pl.program_id(0) == 0)
    def _():
        start_fetch(which_ref, wproj_from, wproj_ref, sems.at[1])
        start_fetch(which_ref, wfc_from, wfc_ref, sems.at[0])
        sums_ref[...] = jnp.zeros_like(sums_ref)

    unit, scale = normalize(x_ref[...].astype(F32))
    da = own_ref[...].astype(F32) + recv_ref[...].astype(F32)
    sums_ref[0:1, :] += column_sum(da * unit)
    sums_ref[1:2, :] += column_sum(da)
    dm = (dh_ref[...] + normalize_back(da, unit, scale, vec_ref[8:9, :])).astype(BF)
    dm_ref[...] = dm

    @pl.when(pl.program_id(0) == 0)
    def _():
        end_fetch(wproj_from, wproj_ref, sems.at[1])
        end_fetch(wfc_from, wfc_ref, sems.at[0])

    width = 512
    dc = jnp.zeros((BT, D), F32)
    for start in range(0, FW, width):
        cols = slice(start, start + width)
        du = (mm_nt(dm, wproj_ref[cols, :]) * slope_ref[:, cols].astype(F32)).astype(BF)
        du_ref[:, cols] = du
        dc = dc + mm_nt(du, wfc_ref[:, cols])
    dc_ref[...] = dc.astype(BF)


def feed_back(which, wfc, wproj, vecs, dh, own, recv, x, slope):
    return pl.pallas_call(
        feed_back_kernel,
        grid=(NB,),
        out_shape=[shape((LEN, D), BF), shape((LEN, FW), BF), shape((LEN, D), BF), shape((8, D), F32)],
        in_specs=specs(10, 0) + [whole_spec(vecs.shape)] + [rows_spec(D)] * 4 + [rows_spec(FW)],
        out_specs=[rows_spec(D), rows_spec(FW), rows_spec(D), whole_spec((8, D))],
        scratch_shapes=feed_weights(),
        compiler_params=params(),
        cost_estimate=cost(5e9, 2e7),
        name="feed_back",
    )(which, *wfc, *wproj, vecs, dh, own, recv, x, slope)


def input_back_kernel(vec_ref, dh_ref, own_ref, recv_ref, x_ref, dx_ref, sums_ref):
    unit, scale = normalize(x_ref[...].astype(F32))
    da = own_ref[...].astype(F32) + recv_ref[...].astype(F32)

    @pl.when(pl.program_id(0) == 0)
    def _():
        sums_ref[...] = jnp.zeros_like(sums_ref)

    sums_ref[0:1, :] += column_sum(da * unit)
    sums_ref[1:2, :] += column_sum(da)
    dx_ref[...] = (dh_ref[...] + normalize_back(da, unit, scale, vec_ref[0:1, :])).astype(BF)


def input_back(vecs, dh, own, recv, x):
    return pl.pallas_call(
        input_back_kernel,
        grid=(NB,),
        out_shape=[shape((LEN, D), BF), shape((8, D), F32)],
        in_specs=[whole_spec(vecs.shape)] + [rows_spec(D)] * 4,
        out_specs=[rows_spec(D), whole_spec((8, D))],
        compiler_params=params(),
        cost_estimate=cost(1e7, 1e7),
        name="input_back",
    )(vecs, dh, own, recv, x)


def in_three(values, spots):
    high = values.astype(BF)
    rest = values - high.astype(F32)
    middle = rest.astype(BF)
    low = (rest - middle.astype(F32)).astype(BF)
    return jnp.where(spots == 0, high, jnp.where(spots == 1, middle, jnp.where(spots == 2, low, jnp.zeros_like(low))))


def attention_back_kernel(layer, *refs):
    which_ref, wqkv_from, wout_from, refs = refs[0], refs[1:6], refs[6:11], refs[11:]
    (vec_ref, dm_ref, own_ref, recv_ref, h_ref, qkv_ref, o_ref, lse_ref), refs = refs[:8], refs[8:]
    (dh_ref, dz_ref, dqkv_ref, da_ref, sums_ref, bias_ref), refs = refs[:6], refs[6:]
    do_ref, dk_ref, dv_ref, wqkv_ref, wout_ref, sems = refs
    start_fetch(which_ref, wout_from, wout_ref, sems.at[1])
    start_fetch(which_ref, wqkv_from, wqkv_ref, sems.at[0])
    end_fetch(wout_from, wout_ref, sems.at[1])
    gain = vec_ref[8 * layer + 1 : 8 * layer + 2, :]
    sums_ref[...] = jnp.zeros_like(sums_ref)
    bias_ref[...] = jnp.zeros_like(bias_ref)

    def enter(index, carry):
        rows = block_rows(index)
        unit, scale = normalize(h_ref[rows, :])
        dc = own_ref[rows, :].astype(F32) + recv_ref[rows, :].astype(F32)
        sums_ref[0:1, :] += column_sum(dc * unit)
        sums_ref[1:2, :] += column_sum(dc)
        dh = dm_ref[rows, :].astype(F32) + normalize_back(dc, unit, scale, gain)
        dh_ref[rows, :] = dh
        dz = dh.astype(BF)
        dz_ref[rows, :] = dz
        sums_ref[2:3, :] += column_sum(dz.astype(F32))
        sums_ref[3:4, :] += column_sum(dm_ref[rows, :].astype(F32))
        do_ref[rows, :] = mm_nt(dz, wout_ref[...]).astype(BF)
        return carry

    lax.fori_loop(0, NB, enter, 0)

    def attend(group, carry):
        low = lower_lanes()
        spots = lax.broadcasted_iota(jnp.int32, (BT, 128), 1) % HS
        ones = jnp.where(spots < 3, jnp.ones((BT, 128), BF), jnp.zeros((BT, 128), BF))
        keep_diag = lax.broadcasted_iota(jnp.int32, (BT, BT), 0) <= lax.broadcasted_iota(jnp.int32, (BT, BT), 1)
        nothing = jnp.zeros((BT, 128), BF)
        dk_ref[...] = jnp.zeros_like(dk_ref)
        dv_ref[...] = jnp.zeros_like(dv_ref)
        for i in range(NB):
            mine = slice(i * BT, (i + 1) * BT)
            query = qkv_ref[mine, lane_group(3 * group)]
            do = do_ref[mine, lane_group(group)]
            lse = in_three(-pltpu.roll(lse_ref[mine, lane_group(group)], HS, 1), spots)
            inner = do.astype(F32) * o_ref[mine, lane_group(group)].astype(F32)
            t_low = jnp.sum(jnp.where(low, inner, 0.0), axis=1, keepdims=True)
            t_high = jnp.sum(jnp.where(low, 0.0, inner), axis=1, keepdims=True)
            t = in_three(-jnp.where(low, t_high, t_low), spots)
            query_with = (jnp.where(low, query, lse), jnp.where(low, lse, query))
            do_with = (jnp.where(low, do, t), jnp.where(low, t, do))
            query_one = (jnp.where(low, query, nothing), jnp.where(low, nothing, query))
            do_one = (jnp.where(low, do, nothing), jnp.where(low, nothing, do))
            dq = jnp.zeros((BT, 128), F32)
            for j in range(i + 1):
                theirs = slice(j * BT, (j + 1) * BT)
                key = qkv_ref[theirs, lane_group(3 * group + 1)]
                value = qkv_ref[theirs, lane_group(3 * group + 2)]
                dv = jnp.zeros((BT, 128), F32)
                dk = jnp.zeros((BT, 128), F32)
                for head in range(2):
                    key_with = jnp.where(low, key, ones) if head == 0 else jnp.where(low, ones, key)
                    value_with = jnp.where(low, value, ones) if head == 0 else jnp.where(low, ones, value)
                    key_one = jnp.where(low, key, nothing) if head == 0 else jnp.where(low, nothing, key)
                    score = mm_nt(key_with, query_with[head])
                    if i == j:
                        score = jnp.where(keep_diag, score, MASKED_SCORE)
                    p = jnp.exp(score)
                    ds = (p * mm_nt(value_with, do_with[head])).astype(BF)
                    dv = dv + mm(p.astype(BF), do_one[head])
                    dk = dk + mm(ds, query_one[head])
                    dq = dq + mm_tn(ds, key_one)
                dv_ref[theirs, :] += dv
                dk_ref[theirs, :] += dk
            dq = dq * 0.125
            dqkv_ref[mine, lane_group(3 * group)] = dq.astype(BF)
        for i in range(NB):
            mine = slice(i * BT, (i + 1) * BT)
            one, two, three = from_pairs(
                dqkv_ref[mine, lane_group(3 * group)].astype(F32), dk_ref[mine, :], dv_ref[mine, :]
            )
            dqkv_ref[mine, lane_group(3 * group)] = one.astype(BF)
            dqkv_ref[mine, lane_group(3 * group + 1)] = two.astype(BF)
            dqkv_ref[mine, lane_group(3 * group + 2)] = three.astype(BF)
        return carry

    lax.fori_loop(0, PAIRS, attend, 0)

    end_fetch(wqkv_from, wqkv_ref, sems.at[0])

    def leave(index, carry):
        rows = block_rows(index)
        dqkv = dqkv_ref[rows, :]
        bias_ref[0:1, :] += column_sum(dqkv.astype(F32))
        da_ref[rows, :] = mm_nt(dqkv, wqkv_ref[...]).astype(BF)
        return carry

    lax.fori_loop(0, NB, leave, 0)


def attention_back(layer, which, wqkv, wout, vecs, *acts):
    outs = [
        shape((LEN, D), F32),
        shape((LEN, D), BF),
        shape((LEN, QW), BF),
        shape((LEN, D), BF),
        shape((8, D), F32),
        shape((8, QW), F32),
    ]
    return pl.pallas_call(
        functools.partial(attention_back_kernel, layer),
        out_shape=outs,
        in_specs=specs(10, 1 + len(acts)),
        out_specs=[pl.BlockSpec(memory_space=pltpu.VMEM)] * len(outs),
        scratch_shapes=[
            pltpu.VMEM((LEN, HALF), BF),
            pltpu.VMEM((LEN, 128), F32),
            pltpu.VMEM((LEN, 128), F32),
            pltpu.VMEM((D, QW), BF),
            pltpu.VMEM((HALF, D), BF),
            pltpu.SemaphoreType.DMA((2,)),
        ],
        compiler_params=params(),
        cost_estimate=cost(2.2e10, 2.2e7, 4e6),
        name="attention_back",
    )(which, *wqkv, *wout, vecs, *acts)


def feed_grad_kernel(flip_ref, g_ref, dm_ref, c_ref, du_ref, first_ref, second_ref, square_ref, bias_ref):
    step = pl.program_id(0)
    tile = step % 6
    part = jnp.where(step < 6, flip_ref[0], 1 - flip_ref[0])

    @pl.when(step == 0)
    def _():
        square_ref[...] = jnp.zeros_like(square_ref)

    def keep(grad):
        square_ref[0:1, :] += column_sum(grad * grad)

        @pl.when(step < 6)
        def _():
            first_ref[...] = grad.astype(BF)

        @pl.when(step >= 6)
        def _():
            second_ref[...] = grad.astype(BF)

    @pl.when(tile < 3)
    def _():
        keep(mm_tn(g_ref[...], dm_ref[...]))

    @pl.when(tile >= 3)
    def _():
        keep(mm_tn(c_ref[...], du_ref[...]))

    @pl.when(tile == 3)
    def _():
        bias_ref[0:1, pl.ds(pl.multiple_of(part * D, 128), D)] = column_sum(du_ref[...].astype(F32))


def feed_grad(flip, g, dm, c, du):
    def part(step, flip_ref):
        return jnp.where(step < 6, flip_ref[0], 1 - flip_ref[0])

    return pl.pallas_call(
        feed_grad_kernel,
        grid_spec=pltpu.PrefetchScalarGridSpec(
            num_scalar_prefetch=1,
            grid=(12,),
            in_specs=[
                pl.BlockSpec((LEN, 256), lambda t, f: (0, 3 * part(t, f) + jnp.minimum(t % 6, 2))),
                pl.BlockSpec((LEN, D), lambda t, f: (0, 0)),
                pl.BlockSpec((LEN, 256), lambda t, f: (0, jnp.maximum(t % 6 - 3, 0))),
                pl.BlockSpec((LEN, D), lambda t, f: (0, part(t, f))),
            ],
            out_specs=[
                pl.BlockSpec((256, D), lambda t, f: (jnp.minimum(t, 5), 0)),
                pl.BlockSpec((256, D), lambda t, f: (jnp.maximum(t - 6, 0), 0)),
                pl.BlockSpec((8, D), lambda t, f: (0, 0)),
                pl.BlockSpec((8, FW), lambda t, f: (0, 0)),
            ],
        ),
        out_shape=[shape((FW, D), BF), shape((FW, D), BF), shape((8, D), F32), shape((8, FW), F32)],
        compiler_params=params(),
        cost_estimate=cost(4 * LEN * D * FW, 1.4e7),
        name="feed_grad",
    )(flip, g, dm, c, du)


def attention_grad_kernel(flip_ref, o_ref, dz_ref, a_ref, dqkv_ref, first_ref, second_ref, square_ref):
    step = pl.program_id(0)

    @pl.when(step == 0)
    def _():
        square_ref[...] = jnp.zeros_like(square_ref)

    def fill(target):
        def place(grad, rows, cols):
            square_ref[0:1, 0:HALF] += column_sum(grad * grad)
            target[rows, cols] = grad.astype(BF)

        place(mm_tn(a_ref[...], dqkv_ref[:, 0:HALF]), slice(0, HALF), slice(0, HALF))
        place(mm_tn(a_ref[...], dqkv_ref[:, HALF:D]), slice(0, HALF), slice(HALF, D))
        side = HALF // 2
        for top, left, right in ((HALF, a_ref[...], dqkv_ref[:, D:]), (HALF + side, o_ref[...], dz_ref[...])):
            grad = mm_tn(left, right)
            place(grad[:side], slice(top, top + side), slice(0, HALF))
            place(grad[side:], slice(top, top + side), slice(HALF, D))

    @pl.when(step == 0)
    def _():
        fill(first_ref)

    @pl.when(step == 1)
    def _():
        fill(second_ref)


def attention_grad(flip, o, dz, a, dqkv):
    def part(step, flip_ref):
        return jnp.where(step == 0, flip_ref[0], 1 - flip_ref[0])

    return pl.pallas_call(
        attention_grad_kernel,
        grid_spec=pltpu.PrefetchScalarGridSpec(
            num_scalar_prefetch=1,
            grid=(2,),
            in_specs=[
                pl.BlockSpec((LEN, HALF), lambda t, f: (0, 0)),
                pl.BlockSpec((LEN, HALF), lambda t, f: (0, part(t, f))),
                pl.BlockSpec((LEN, HALF), lambda t, f: (0, part(t, f))),
                pl.BlockSpec((LEN, QW), lambda t, f: (0, 0)),
            ],
            out_specs=[pl.BlockSpec((D, D), lambda t, f: (0, 0))] * 2 + [pl.BlockSpec((8, D), lambda t, f: (0, 0))],
        ),
        out_shape=[shape((D, D), BF), shape((D, D), BF), shape((8, D), F32)],
        compiler_params=params(),
        cost_estimate=cost(2 * LEN * D * (QW + HALF), 1e7),
        name="attention_grad",
    )(flip, o, dz, a, dqkv)


def weigh_kernel(rows, roles_ref, weight_ref, *refs):
    sources, refs = refs[:6], refs[6:]
    if len(refs) == 5:
        (small_ref, other_ref, keep_ref, held_ref, sems) = refs
    else:
        (other_ref, keep_ref, held_ref, sems) = refs
        small_ref = None
    mine = roles_ref[0]
    for layer in range(2):
        one, own, there = (source.at[rows] for source in sources[3 * layer : 3 * layer + 3])
        for role in range(2):

            @pl.when((mine == layer) == (role == 1))
            def _(role=role, one=one, own=own, there=there):
                pltpu.make_async_copy(one, held_ref.at[2 * role], sems.at[role]).start()

                @pl.when(roles_ref[1] == 1)
                def _():
                    pltpu.make_async_copy(own, held_ref.at[2 * role + 1], sems.at[role]).start()

                @pl.when(roles_ref[1] == 0)
                def _():
                    pltpu.make_async_copy(there, held_ref.at[2 * role + 1], sems.at[role]).start()

    count = held_ref.shape[1]
    for role, target in ((0, other_ref), (1, keep_ref)):
        both = held_ref.at[pl.ds(2 * role, 2)]
        pltpu.make_async_copy(both, both, sems.at[role]).wait()
        total = weight_ref[0] * held_ref[2 * role].astype(F32) + weight_ref[1] * held_ref[2 * role + 1].astype(F32)
        target[0:count, :] = total.astype(target.dtype)
        if small_ref is not None:
            target[count:, :] = jnp.where(mine == role, small_ref[1], small_ref[0]).astype(target.dtype)


def weigh(rows, roles, weights, layers, small=None):
    count = rows.stop - rows.start
    tall = count + (0 if small is None else 16)
    vmem, smem, hbm = (pl.BlockSpec(memory_space=kind) for kind in (pltpu.VMEM, pltpu.SMEM, pl.ANY))
    return pl.pallas_call(
        functools.partial(weigh_kernel, pl.ds(rows.start, count)),
        out_shape=[shape((tall, D), BF), shape((tall, D), F32)],
        in_specs=[smem, smem] + [hbm] * 6 + ([] if small is None else [vmem]),
        out_specs=[vmem] * 2,
        scratch_shapes=[pltpu.VMEM((4, count, D), BF), pltpu.SemaphoreType.DMA((2,))],
        compiler_params=params(),
        cost_estimate=cost(1e7, 1e7),
        name="weigh",
    )(roles, weights, *layers[0], *layers[1], *(() if small is None else (small,)))


def finish_feed_kernel(denominator, home_ref, *refs):
    own, swapped = refs[0:4], refs[4:8]
    noise_proj_ref, noise_fc_ref, proj_ref, fc_ref = refs[8:]
    scale, step = NOISE_MULT * CLIP_FRACTION * math.sqrt(LEN * FF * D), D // 2

    def run(parts):
        for number, part in enumerate(parts):
            for index in range(2):
                rows = slice(number * D + index * step, number * D + (index + 1) * step)
                noise = noise_proj_ref[rows, :].astype(F32)
                proj_ref[rows, :] = (part[index][...].astype(F32) + scale * noise) / denominator
                rows, cols = slice(index * step, (index + 1) * step), slice(number * D, (number + 1) * D)
                noise = noise_fc_ref[rows, cols].astype(F32)
                fc_ref[rows, cols] = (part[2 + index][...].astype(F32) + scale * noise) / denominator

    @pl.when(home_ref[0] == 1)
    def _():
        run((own, swapped))

    @pl.when(home_ref[0] == 0)
    def _():
        run((swapped, own))


def finish_attention_kernel(denominator, home_ref, *refs):
    own, swapped = refs[0:2], refs[2:4]
    noise_qkv_ref, noise_out_ref, qkv_ref, out_ref = refs[4:]
    scale, side = NOISE_MULT * CLIP_FRACTION * math.sqrt(LEN * FF * D), HALF // 2

    def put(target, noise_ref, rows, cols, block):
        target[rows, cols] = (block.astype(F32) + scale * noise_ref[rows, cols].astype(F32)) / denominator

    def run(parts):
        for number, (one, two) in enumerate(parts):
            start = number * HALF
            put(qkv_ref, noise_qkv_ref, slice(start, start + HALF), slice(0, D), one[...])
            for index in range(2):
                cols = slice(index * HALF, (index + 1) * HALF)
                rows = slice(start + index * side, start + (index + 1) * side)
                put(qkv_ref, noise_qkv_ref, rows, slice(D, QW), two[0:side, cols])
                rows = slice(index * side, (index + 1) * side)
                put(out_ref, noise_out_ref, rows, slice(start, start + HALF), two[side : 2 * side, cols])

    @pl.when(home_ref[0] == 1)
    def _():
        run((own, swapped))

    @pl.when(home_ref[0] == 0)
    def _():
        run((swapped, own))


def finish(kernel, denominator, home, own, swapped, noises, name):
    vmem = pl.BlockSpec(memory_space=pltpu.VMEM)
    return pl.pallas_call(
        functools.partial(kernel, denominator),
        out_shape=[shape(noise.shape, F32) for noise in noises],
        in_specs=[pl.BlockSpec(memory_space=pltpu.SMEM)] + [vmem] * (2 * len(own) + 2),
        out_specs=[vmem] * 2,
        compiler_params=params(),
        cost_estimate=cost(1e7, 1.6e7),
        name=name,
    )(home, *own, *swapped, *noises)


def send(values, route):
    sections, ranks = lax.axis_size("section"), lax.axis_size("dp")
    pairs = []
    for section in range(sections):
        for rank in range(ranks):
            target = route(section, rank // 2, rank % 2)
            if target is not None:
                to_section, to_pair, to_core = target
                pairs.append((section * ranks + rank, to_section * ranks + to_pair * 2 + to_core))
    return lax.ppermute(values, ("section", "dp"), pairs)


def swap_cores(values):
    return send(values, lambda s, z, c: (s, z, 1 - c))


def is_home(s, c):
    return s % 2 == c


def after(values, *others):
    return lax.optimization_barrier((values, *others))[0]


def local(
    inputs,
    cotangent,
    included,
    qkv_weight,
    qkv_bias,
    out_weight,
    fc_weight,
    fc_bias,
    proj_weight,
    norm_gains,
    shifts,
    noise,
):
    clip_norm = CLIP_FRACTION * math.sqrt(LEN * FF * D)
    section = lax.axis_index("section")
    rank = lax.axis_index("dp")
    ranks = lax.axis_size("dp")
    row, half = section // 2, section % 2
    place, core = rank // 2, rank % 2
    home = half == core
    on_top = row == 0
    flip = home.astype(jnp.int32).reshape(1)
    denominator = SAMPLE_RATE * inputs.shape[0] * ranks

    side = place % 2

    def pieces(weight):
        tall = weight.shape[0] // 2
        piece = lax.dynamic_slice_in_dim(weight, side * tall, tall, 0)
        one = send(piece, lambda s, z, c: (s ^ 2, z, c) if is_home(s, c) else (s ^ 1, z, 1 - c))
        two = send(one, lambda s, z, c: (s, z ^ 1, c))
        far_one = send(one, lambda s, z, c: (s ^ 1, z, c) if is_home(s, c) else None)
        far_two = send(two, lambda s, z, c: None if is_home(s, c) else (s ^ 2, z, c))
        return (weight, one, two, far_one, far_two)

    def which_of(layer):
        kind = jnp.where(row == layer, jnp.where(home, 0, 1), jnp.where(home, 1, 2))
        return jnp.stack([kind, side]).astype(jnp.int32)

    which = [which_of(0), which_of(1)]

    def own_sequence(values):
        mine = lax.dynamic_index_in_dim(values, half, 0, keepdims=False)
        theirs = swap_cores(mine)
        return jnp.where(core == row, mine, theirs)

    small = jnp.concatenate([qkv_bias, fc_bias, norm_gains.reshape(-1), shifts.reshape(-1)]).reshape(1, -1)
    others = [send(small, lambda s, z, c, bits=bits: (s ^ bits, z, c)) for bits in (1, 2, 3)]
    wqkv, wout, wfc, wproj = (pieces(weight) for weight in (qkv_weight, out_weight, fc_weight, proj_weight))
    x0 = own_sequence(inputs)
    cot = own_sequence(cotangent)
    drawn = own_sequence(jnp.broadcast_to(included.astype(F32)[:, None, None], (2, 8, 128)))[0, 0]
    small_all = jnp.concatenate([small] + others, axis=0)
    small_all = jnp.where(half == 0, small_all, small_all[jnp.array([1, 0, 3, 2])])
    small_all = jnp.where(on_top, small_all, small_all[jnp.array([2, 3, 0, 1])])
    small_all = small_all.reshape(2, 2, -1)
    bias = jnp.where(core == 0, small_all[:, 0], small_all[:, 1])
    bqkv, bfc = bias[:, :QW], bias[:, QW : QW + FW]
    vecs = small_all[:, :, QW + FW :].reshape(2, 2, 6, HALF).transpose(0, 2, 1, 3).reshape(2, 6, D)
    vecs = jnp.pad(vecs, ((0, 0), (0, 2), (0, 0))).reshape(16, D)

    shapes = ((D, QW), (QW,), (HALF, D), (D, FW), (FW,), (FW, D), (2, HALF), (4, HALF))
    noises, offset = [], 0
    for dims in shapes:
        noises.append(noise[offset : offset + math.prod(dims)].reshape(dims))
        offset += math.prod(dims)
    x0, *noises = lax.optimization_barrier((x0, *noises))

    a0, qkv0, o0, lse0, part = attention_forward(0, which[0], wqkv, wout, vecs, bqkv, x0)
    h0, c0, g0, part_two, slope0 = feed_forward(
        0, which[0], wfc, wproj, vecs, bfc, x0, part, swap_cores(part)
    )
    a1, qkv1, o1, lse1, part, x1 = attention_forward(
        1, which[1], wqkv, wout, vecs, bqkv, h0, part_two, swap_cores(part_two)
    )
    h1, c1, g1, part_two, du1, dc = feed_forward(
        1, which[1], wfc, wproj, vecs, bfc, x1, part, swap_cores(part), cot
    )
    dc_theirs = swap_cores(dc)
    y1 = (h1 + (part_two.astype(F32) + swap_cores(part_two).astype(F32)) + vecs[13:14]).astype(BF)

    def spread(block_for):
        received = []
        for step in range(2):
            block = block_for(2 * core + (step ^ half))
            received.append(send(block, lambda s, z, c, step=step: (2 * c + (step ^ (s % 2)), z, s // 2)))
        first, second = received
        return jnp.where(half == 0, jnp.stack([first, second]), jnp.stack([second, first]))

    both_out = jnp.concatenate([x1, y1], axis=1)
    layer_out = spread(lambda block: lax.dynamic_slice_in_dim(both_out, block * HALF, HALF, 1))

    def gather_parts(first, second):
        one = send(first, lambda s, z, c: (s, z, 1 - c) if is_home(s, c) else (s ^ 1, z, c))
        there = send(second, lambda s, z, c: None if is_home(s, c) else (s ^ 1, z, 1 - c))
        return one, second, there

    first, second, squares_feed1, bias_fc1 = feed_grad(flip, g1, cot, c1, du1)
    feed1 = gather_parts(first, second)
    dc = after(dc, first)
    dh1, dz1, dqkv1, da, sums1, bias_qkv1 = attention_back(
        1, which[1], wqkv, wout, vecs, cot, dc, dc_theirs, h1, qkv1, o1, lse1
    )
    da_theirs = swap_cores(da)
    first, second, squares_attention1 = attention_grad(flip, o1, dz1, a1, dqkv1)
    attention1 = gather_parts(first, second)
    da = after(da, first)
    da = after(da, layer_out)
    dm0, du0, dc, first_sums1 = feed_back(which[0], wfc, wproj, vecs, dh1, da, da_theirs, x1, slope0)
    dc_theirs = swap_cores(dc)
    du0, *feed1 = lax.optimization_barrier((du0, *feed1))
    first, second, squares_feed0, bias_fc0 = feed_grad(flip, g0, dm0, c0, du0)
    feed0 = gather_parts(first, second)
    dc, _, *attention1 = lax.optimization_barrier((dc, first, *attention1))
    dh0, dz0, dqkv0, da, sums0, bias_qkv0 = attention_back(
        0, which[0], wqkv, wout, vecs, dm0, dc, dc_theirs, h0, qkv0, o0, lse0
    )
    da_theirs = swap_cores(da)
    first, second, squares_attention0 = attention_grad(flip, o0, dz0, a0, dqkv0)
    attention0 = gather_parts(first, second)
    dx0, first_sums0 = input_back(vecs, dh0, da, da_theirs, x0)

    def small_grads(bias_qkv, bias_fc, first_sums, second_sums):
        rows = jnp.stack([first_sums[0], second_sums[0], first_sums[1], second_sums[2], second_sums[1], second_sums[3]])
        rows = lax.dynamic_slice_in_dim(rows, core * HALF, HALF, 1)
        return jnp.concatenate([bias_qkv[0], bias_fc[0], rows.reshape(-1)])

    small_pair = jnp.stack(
        [
            small_grads(bias_qkv0, bias_fc0, first_sums0, sums0),
            small_grads(bias_qkv1, bias_fc1, first_sums1, sums1),
        ]
    )

    squares = jnp.sum(squares_feed0 + squares_attention0 + squares_feed1 + squares_attention1)
    squares = jnp.broadcast_to(squares + jnp.sum(small_pair * small_pair), (8, 128))
    squares = squares + swap_cores(squares)
    factor = drawn * jnp.minimum(1.0, clip_norm / jnp.sqrt(squares))
    across = send(factor, lambda s, z, c: (s ^ 1, z, 1 - c) if is_home(s, c) else None)
    factor_there = jnp.where(home, across, swap_cores(across))
    mine, theirs = factor[0, 0], factor_there[0, 0]
    weights = jnp.stack([jnp.where(home, theirs, mine), jnp.where(home, mine, theirs)])
    roles = jnp.stack([row, home]).astype(jnp.int32)

    small_pair = jnp.pad(small_pair, ((0, 0), (0, 16 * D - small_pair.shape[1]))).reshape(2, 16, D)
    small_there = send(small_pair, lambda s, z, c: None if is_home(s, c) else (s ^ 1, z, c))
    small_sum = jnp.where(home, mine * small_pair + theirs * small_there, 0.0)

    token_rows = LEN // lax.axis_size("section")
    input_grad = spread(lambda block: lax.dynamic_slice_in_dim(dx0, block * token_rows, token_rows, 0))

    places = ranks // 2
    middle = places // 2

    def to_middle(step):
        def route(s, z, c):
            if z == step:
                return (s, z + 1, c)
            if z == places - 1 - step:
                return (s, z - 1, c)
            return None

        return route

    def at_middle(s, z, c):
        return (s, places - 1 - z, c) if z in (middle - 1, middle) else None

    def from_middle(step):
        def route(s, z, c):
            if z == middle - 1 - step:
                return (s, z - 1, c)
            if z == middle + step:
                return (s, z + 1, c)
            return None

        return route

    def add(left, right):
        return (left.astype(F32) + right.astype(F32)).astype(BF)

    def weigh_stage(args):
        other, keep = weigh(*args)
        return keep, send(other, lambda s, z, c: (s ^ 2, z, c))

    def chain_stage(hop):
        def stage(held):
            total = add(*held)
            return total, send(total, hop)

        return stage

    def spread_stage(step):
        def stage(held):
            total, arrived = held
            if step == 0:
                total = add(total, arrived)
            else:
                takes = (place == middle - 1 - step) | (place == middle + step)
                total = jnp.where(takes, arrived, total)
            return total, send(total, from_middle(step))

        return stage

    def last_stage(held):
        total, arrived = held
        if middle > 1:
            takes = (place == 0) | (place == places - 1)
            total = jnp.where(takes, arrived, total)
        else:
            total = add(total, arrived)
        return total, swap_cores(total)

    hops = [to_middle(step) for step in range(middle - 1)] + [at_middle]
    stages = [weigh_stage] + [chain_stage(hop) for hop in hops]
    stages += [spread_stage(step) for step in range(middle - 1)] + [last_stage]

    chunk = D // 2
    jobs = [(slice(i * chunk, (i + 1) * chunk), roles, weights, (feed0, feed1)) for i in range(4)]
    jobs.append((slice(0, chunk), roles, weights, (attention0, attention1)))
    jobs.append((slice(chunk, 2 * chunk), roles, weights, (attention0, attention1), small_sum))
    done = None
    for tick in range(len(jobs) + len(stages) - 1):
        for stage in reversed(range(len(stages))):
            index = tick - stage
            if 0 <= index < len(jobs):
                held = jobs[index]
                if stage == 0:
                    if done is not None:
                        held = (held[0], held[1], after(held[2], done)) + held[3:]
                elif done is not None:
                    held = (after(held[0], done), held[1])
                jobs[index] = stages[stage](held)
                done = jobs[index][0]
    feed, attention = jobs[:4], jobs[4:]
    own, swapped = zip(*feed)
    proj_grad, fc_grad = finish(
        finish_feed_kernel, denominator, flip, own, swapped, (noises[5], noises[3]), "finish_feed"
    )
    own, swapped = zip(*attention)
    small_sum = jnp.where(home, own[1][chunk:], swapped[1][chunk:]).astype(F32).reshape(-1)
    qkv_grad, out_grad = finish(
        finish_attention_kernel, denominator, flip, own, swapped, (noises[0], noises[2]), "finish_attention"
    )

    small_noise = jnp.concatenate([noises[i].reshape(-1) for i in (1, 4, 6, 7)]).astype(F32)
    small_done = (small_sum[: small_noise.size] + NOISE_MULT * clip_norm * small_noise) / denominator
    start = QW + FW
    return (
        layer_out,
        input_grad,
        qkv_grad,
        small_done[:QW],
        out_grad,
        fc_grad,
        small_done[QW:start],
        proj_grad,
        small_done[start : start + 2 * HALF].reshape(2, HALF),
        small_done[start + 2 * HALF :].reshape(4, HALF),
    )


def solution(mesh):
    return jax.shard_map(
        local,
        mesh=mesh,
        in_specs=(
            P("dp", None, None),
            P("dp", None, None),
            P("dp"),
            P(None, "section"),
            P("section"),
            P("section", None),
            P(None, "section"),
            P("section"),
            P("section", None),
            P(None, "section"),
            P(None, "section"),
            P("section"),
        ),
        out_specs=(
            P("dp", None, "section"),
            P("dp", "section", None),
            P(None, "section"),
            P("section"),
            P("section", None),
            P(None, "section"),
            P("section"),
            P("section", None),
            P(None, "section"),
            P(None, "section"),
        ),
        check_vma=False,
    )
```

```python
import functools
import math

import jax
import jax.numpy as jnp
from jax import lax
from jax.experimental import pallas as pl
from jax.experimental.pallas import tpu as pltpu
from jax.sharding import PartitionSpec as P

D = 768
FF = 3072
HS = 64
LEN = 1024
HALF = D // 2
QW = 3 * HALF
FW = FF // 2
PAIRS = HALF // 128
BT = 256
NB = LEN // BT
BQ = 256
BR = 512
BK = 256

CLIP_FRACTION = 0.05
NOISE_MULT = 0.001
SAMPLE_RATE = 0.5
NORM_EPS = 1e-05
MASKED_SCORE = -1e30
VMEM_BYTES = 36 * 1024 * 1024

BF = jnp.bfloat16
F32 = jnp.float32


def mm(left, right):
    return lax.dot_general(left, right, (((1,), (0,)), ((), ())), preferred_element_type=F32)


def mm_nt(left, right):
    return lax.dot_general(left, right, (((1,), (1,)), ((), ())), preferred_element_type=F32)


def mm_tn(left, right):
    return lax.dot_general(left, right, (((0,), (0,)), ((), ())), preferred_element_type=F32)


def normalize(values):
    center = values - jnp.mean(values, axis=-1, keepdims=True)
    spread = jnp.mean(center * center, axis=-1, keepdims=True)
    scale = lax.rsqrt(spread + NORM_EPS)
    return center * scale, scale


def normalize_back(grad, unit, scale, gain):
    inner = grad * gain
    mean_inner = jnp.mean(inner, axis=-1, keepdims=True)
    mean_cross = jnp.mean(inner * unit, axis=-1, keepdims=True)
    return scale * (inner - mean_inner - unit * mean_cross)


def column_sum(values):
    return jnp.sum(values, axis=0, keepdims=True)


def block_rows(index):
    return pl.ds(pl.multiple_of(index * BT, BT), BT)


def lane_group(index, width=128):
    return pl.ds(pl.multiple_of(index * 128, 128), width)


def lower_lanes(rows=BT):
    return lax.broadcasted_iota(jnp.int32, (rows, 128), 1) < HS


def to_pairs(block, group):
    low = lower_lanes()
    start = 3 * 128 * group
    one, two, three = (block[:, start + 128 * i : start + 128 * (i + 1)] for i in range(3))
    query = jnp.where(low, one, two)
    key = pltpu.roll(jnp.where(low, three, one), HS, 1)
    value = jnp.where(low, two, three)
    return query, key, value


def from_pairs(query, key, value):
    low = lower_lanes()
    turned = pltpu.roll(key, HS, 1)
    return jnp.where(low, query, turned), jnp.where(low, value, query), jnp.where(low, turned, value)


def start_fetch(which_ref, own, pieces, parts, sems):
    @pl.when(which_ref[0] == 0)
    def _():
        for number, (target, _) in enumerate(parts):
            pltpu.make_async_copy(own[number], target, sems.at[number]).start()

    for kind in (1, 2):

        @pl.when(which_ref[0] == kind)
        def _(kind=kind):
            for order in range(2):
                piece = pieces[2 * kind - 2 + order]
                side = which_ref[1] if order == 0 else 1 - which_ref[1]
                for number, (target, blocks) in enumerate(parts):
                    base = pl.multiple_of(side * (target.shape[0] // 2), 64)
                    for (top, left), (tall, wide), (down, right) in blocks:
                        pltpu.make_async_copy(
                            piece.at[pl.ds(top, tall), pl.ds(left, wide)],
                            target.at[pl.ds(base + down, tall), pl.ds(right, wide)],
                            sems.at[number],
                        ).start()


def end_fetch(own, target, sem):
    pltpu.make_async_copy(own, target, sem).wait()


SIDE = HALF // 2
QKV_BLOCKS = (
    ((0, 0), (HALF, D), (0, 0)),
    ((HALF, 0), (SIDE, HALF), (0, D)),
    ((HALF, HALF), (SIDE, HALF), (SIDE, D)),
)
OUT_BLOCKS = (((HALF + SIDE, 0), (SIDE, D), (0, 0)),)
FC_BLOCKS = (((0, 0), (HALF, D), (0, 0)), ((HALF, 0), (HALF, D), (0, D)))
PROJ_BLOCKS = (((0, 0), (D, D), (0, 0)),)


def attention_forward_kernel(layer, *refs):
    which_ref, own, pieces, refs = refs[0], refs[1:3], refs[3:7], refs[7:]
    vec_ref, bqkv_ref, refs = refs[0], refs[1], refs[2:]
    first = layer == 0
    if first:
        (x_ref, a_ref, qkv_ref, o_ref, lse_ref, part_ref, wqkv_ref, wout_ref, sems) = refs
    else:
        (h_ref, own_ref, recv_ref, a_ref, qkv_ref, o_ref, lse_ref, part_ref, x_ref, wqkv_ref, wout_ref, sems) = refs
    start_fetch(which_ref, own, pieces, ((wqkv_ref, QKV_BLOCKS), (wout_ref, OUT_BLOCKS)), sems)
    end_fetch(own[0], wqkv_ref, sems.at[0])

    def project(index, carry):
        rows = block_rows(index)
        if first:
            values = x_ref[rows, :].astype(F32)
        else:
            total = h_ref[rows, :] + (own_ref[rows, :].astype(F32) + recv_ref[rows, :].astype(F32)) + vec_ref[5:6, :]
            x_ref[rows, :] = total.astype(BF)
            values = total.astype(BF).astype(F32)
        unit, _ = normalize(values)
        a = (unit * vec_ref[8 * layer : 8 * layer + 1, :] + vec_ref[8 * layer + 2 : 8 * layer + 3, :]).astype(BF)
        a_ref[rows, :] = a
        projected = mm(a, wqkv_ref[...]) + bqkv_ref[layer : layer + 1, :]
        for group in range(PAIRS):
            query, key, value = to_pairs(projected, group)
            start = 3 * 128 * group
            qkv_ref[rows, start : start + 128] = query.astype(BF) * 0.125
            qkv_ref[rows, start + 128 : start + 256] = key.astype(BF)
            qkv_ref[rows, start + 256 : start + 384] = value.astype(BF)
        return carry

    lax.fori_loop(0, NB, project, 0)

    def attend(group, carry):
        low = lower_lanes(BQ)
        keep_diag = lax.broadcasted_iota(jnp.int32, (BQ, BQ), 1) <= lax.broadcasted_iota(jnp.int32, (BQ, BQ), 0)
        value = qkv_ref[:, lane_group(3 * group + 2)]
        low_all = lower_lanes(LEN)
        one = jnp.ones_like(value)
        values = (jnp.where(low_all, value, one), jnp.where(low_all, one, value))

        def scores(i, head):
            past, here = i * BQ, (i + 1) * BQ
            query = qkv_ref[past:here, lane_group(3 * group)]
            nothing = jnp.zeros_like(query)
            query = jnp.where(low, query, nothing) if head == 0 else jnp.where(low, nothing, query)
            diag = jnp.where(keep_diag, mm_nt(query, qkv_ref[past:here, lane_group(3 * group + 1)]), MASKED_SCORE)
            left = mm_nt(query, qkv_ref[0:past, lane_group(3 * group + 1)]) if i else None
            return diag, left

        units = [(i, head) for i in range(LEN // BQ) for head in range(2)]
        ahead = scores(*units[0])
        mixed, largest = [], []
        for number, (i, head) in enumerate(units):
            past, here = i * BQ, (i + 1) * BQ
            diag, left = ahead
            if number + 1 < len(units):
                ahead = scores(*units[number + 1])
            top = jnp.max(diag, axis=1, keepdims=True)
            if i:
                top = jnp.maximum(top, jnp.max(left, axis=1, keepdims=True))
            total = mm(jnp.exp(diag - top).astype(BF), values[head][past:here])
            if i:
                total = total + mm(jnp.exp(left - top).astype(BF), values[head][:past])
            mixed.append(total)
            largest.append(top)
            if head == 1:
                sums = pltpu.roll(jnp.where(low, mixed[1], mixed[0]), HS, 1)
                o_ref[past:here, lane_group(group)] = (jnp.where(low, mixed[0], mixed[1]) / sums).astype(BF)
                lse_ref[past:here, lane_group(group)] = jnp.where(low, largest[0], largest[1]) + jnp.log(sums)
                mixed, largest = [], []
        return carry

    lax.fori_loop(0, PAIRS, attend, 0)

    end_fetch(own[1], wout_ref, sems.at[1])

    def leave(index, carry):
        rows = block_rows(index)
        part_ref[rows, :] = mm(o_ref[rows, :], wout_ref[...]).astype(BF)
        return carry

    lax.fori_loop(0, NB, leave, 0)


def params(limit=VMEM_BYTES):
    return pltpu.CompilerParams(vmem_limit_bytes=limit)


def shape(dims, kind):
    return jax.ShapeDtypeStruct(dims, kind)


def cost(flops, moved, transcendentals=0):
    return pl.CostEstimate(flops=int(flops) // 1000, bytes_accessed=int(moved) // 1000, transcendentals=0)


def specs(*counts):
    return (
        [pl.BlockSpec(memory_space=pltpu.SMEM)]
        + [pl.BlockSpec(memory_space=pl.ANY)] * counts[0]
        + [pl.BlockSpec(memory_space=pltpu.VMEM)] * counts[1]
    )


def attention_forward(layer, which, weights, vecs, bqkv, *acts):
    outs = [
        shape((LEN, D), BF),
        shape((LEN, QW), BF),
        shape((LEN, HALF), BF),
        shape((LEN, HALF), F32),
        shape((LEN, D), BF),
    ]
    if layer:
        outs.append(shape((LEN, D), BF))
    return pl.pallas_call(
        functools.partial(attention_forward_kernel, layer),
        out_shape=outs,
        in_specs=specs(6, 2 + len(acts)),
        out_specs=[pl.BlockSpec(memory_space=pltpu.VMEM)] * len(outs),
        scratch_shapes=[pltpu.VMEM((D, QW), BF), pltpu.VMEM((HALF, D), BF), pltpu.SemaphoreType.DMA((2,))],
        compiler_params=params(),
        cost_estimate=cost(1.2e10, 1.6e7, 4e6),
        name="attention_forward",
    )(which, *weights, vecs, bqkv, *acts)


def gelu_parts(u):
    slope = math.sqrt(2.0 / math.pi)
    square = u * u
    half = 0.5 + 0.5 * jnp.tanh(u * (slope + (slope * 0.044715) * square))
    value = u * half
    return value, half + (value - value * half) * (2.0 * slope + (6.0 * slope * 0.044715) * square)


def feed_forward_kernel(layer, *refs):
    both = layer == 1
    which_ref, own, fc_pieces, proj_pieces, refs = refs[0], refs[1:3], refs[3:7], refs[7:11], refs[11:]
    vec_ref, bfc_ref, refs = refs[0], refs[1], refs[2:]
    if both:
        (x_ref, own_ref, recv_ref, dm_ref, h_ref, c_ref, g_ref, part_ref, du_ref, dc_ref) = refs[:10]
    else:
        (x_ref, own_ref, recv_ref, h_ref, c_ref, g_ref, part_ref, slope_ref) = refs[:8]
    wfc_ref, wproj_ref, sems = refs[-3:]
    base = 8 * layer

    @pl.when(pl.program_id(0) == 0)
    def _():
        start_fetch(which_ref, own[0:1], fc_pieces, ((wfc_ref, FC_BLOCKS),), sems.at[pl.ds(0, 1)])
        start_fetch(which_ref, own[1:2], proj_pieces, ((wproj_ref, PROJ_BLOCKS),), sems.at[pl.ds(1, 1)])

    h = x_ref[...].astype(F32) + (
        own_ref[...].astype(F32) + recv_ref[...].astype(F32) + vec_ref[base + 3 : base + 4, :]
    )
    h_ref[...] = h
    unit, _ = normalize(h)
    c = (unit * vec_ref[base + 1 : base + 2, :] + vec_ref[base + 4 : base + 5, :]).astype(BF)
    c_ref[...] = c

    @pl.when(pl.program_id(0) == 0)
    def _():
        end_fetch(own[0], wfc_ref, sems.at[0])
        end_fetch(own[1], wproj_ref, sems.at[1])

    width = 512
    starts = list(range(0, FW, width))

    def up(start):
        cols = slice(start, start + width)
        u = mm(c, wfc_ref[:, cols]) + bfc_ref[layer : layer + 1, cols]
        return u, (mm_nt(dm_ref[...], wproj_ref[cols, :]) if both else None)

    part, dc = None, None
    ahead = up(starts[0])
    for number, start in enumerate(starts):
        cols = slice(start, start + width)
        u, dg = ahead
        if number + 1 < len(starts):
            ahead = up(starts[number + 1])
        g, slope = gelu_parts(u)
        g = g.astype(BF)
        g_ref[:, cols] = g
        more = mm(g, wproj_ref[cols, :])
        part = more if part is None else part + more
        if both:
            du = (dg * slope).astype(BF)
            du_ref[:, cols] = du
            more = mm_nt(du, wfc_ref[:, cols])
            dc = more if dc is None else dc + more
        else:
            slope_ref[:, cols] = slope.astype(BF)
    part_ref[...] = part.astype(BF)
    if both:
        dc_ref[...] = dc.astype(BF)


def rows_spec(width):
    return pl.BlockSpec((BR, width), lambda i: (i, 0))


def whole_spec(dims):
    return pl.BlockSpec(dims, lambda *i: (0,) * len(dims))


def feed_weights():
    return [pltpu.VMEM((D, FW), BF), pltpu.VMEM((FW, D), BF), pltpu.SemaphoreType.DMA((2,))]


def feed_forward(layer, which, weights, vecs, bfc, *acts):
    both = layer == 1
    outs = [shape((LEN, D), F32), shape((LEN, D), BF), shape((LEN, FW), BF), shape((LEN, D), BF), shape((LEN, FW), BF)]
    out_specs = [rows_spec(D), rows_spec(D), rows_spec(FW), rows_spec(D), rows_spec(FW)]
    if both:
        outs.append(shape((LEN, D), BF))
        out_specs.append(rows_spec(D))
    return pl.pallas_call(
        functools.partial(feed_forward_kernel, layer),
        grid=(LEN // BR,),
        out_shape=outs,
        in_specs=specs(10, 0) + [whole_spec(vecs.shape), whole_spec(bfc.shape)] + [rows_spec(D)] * len(acts),
        out_specs=out_specs,
        scratch_shapes=feed_weights(),
        compiler_params=params(),
        cost_estimate=cost(1e10 if both else 5e9, 2e7, 2e6),
        name="feed_forward",
    )(which, *weights, vecs, bfc, *acts)


def feed_back_kernel(*refs):
    which_ref, own, fc_pieces, proj_pieces, refs = refs[0], refs[1:3], refs[3:7], refs[7:11], refs[11:]
    (vec_ref, dh_ref, own_ref, recv_ref, x_ref, slope_ref, dm_ref, du_ref, dc_ref, sums_ref) = refs[:10]
    wfc_ref, wproj_ref, sems = refs[10:]

    @pl.when(pl.program_id(0) == 0)
    def _():
        start_fetch(which_ref, own[0:1], fc_pieces, ((wfc_ref, FC_BLOCKS),), sems.at[pl.ds(0, 1)])
        start_fetch(which_ref, own[1:2], proj_pieces, ((wproj_ref, PROJ_BLOCKS),), sems.at[pl.ds(1, 1)])
        sums_ref[...] = jnp.zeros_like(sums_ref)

    unit, scale = normalize(x_ref[...].astype(F32))
    da = own_ref[...].astype(F32) + recv_ref[...].astype(F32)
    sums_ref[0:1, :] += column_sum(da * unit)
    sums_ref[1:2, :] += column_sum(da)
    dm = (dh_ref[...] + normalize_back(da, unit, scale, vec_ref[8:9, :])).astype(BF)
    dm_ref[...] = dm

    @pl.when(pl.program_id(0) == 0)
    def _():
        end_fetch(own[1], wproj_ref, sems.at[1])
        end_fetch(own[0], wfc_ref, sems.at[0])

    width = 512
    starts = list(range(0, FW, width))

    def up(start):
        return mm_nt(dm, wproj_ref[start : start + width, :])

    dc = None
    ahead = up(starts[0])
    for number, start in enumerate(starts):
        cols = slice(start, start + width)
        dg = ahead
        if number + 1 < len(starts):
            ahead = up(starts[number + 1])
        du = (dg * slope_ref[:, cols].astype(F32)).astype(BF)
        du_ref[:, cols] = du
        more = mm_nt(du, wfc_ref[:, cols])
        dc = more if dc is None else dc + more
    dc_ref[...] = dc.astype(BF)


def feed_back(which, weights, vecs, dh, own, recv, x, slope):
    return pl.pallas_call(
        feed_back_kernel,
        grid=(LEN // BR,),
        out_shape=[shape((LEN, D), BF), shape((LEN, FW), BF), shape((LEN, D), BF), shape((8, D), F32)],
        in_specs=specs(10, 0) + [whole_spec(vecs.shape)] + [rows_spec(D)] * 4 + [rows_spec(FW)],
        out_specs=[rows_spec(D), rows_spec(FW), rows_spec(D), whole_spec((8, D))],
        scratch_shapes=feed_weights(),
        compiler_params=params(),
        cost_estimate=cost(5e9, 2e7),
        name="feed_back",
    )(which, *weights, vecs, dh, own, recv, x, slope)


def input_back_kernel(vec_ref, dh_ref, own_ref, recv_ref, x_ref, dx_ref, sums_ref):
    unit, scale = normalize(x_ref[...].astype(F32))
    da = own_ref[...].astype(F32) + recv_ref[...].astype(F32)

    @pl.when(pl.program_id(0) == 0)
    def _():
        sums_ref[...] = jnp.zeros_like(sums_ref)

    sums_ref[0:1, :] += column_sum(da * unit)
    sums_ref[1:2, :] += column_sum(da)
    dx_ref[...] = (dh_ref[...] + normalize_back(da, unit, scale, vec_ref[0:1, :])).astype(BF)


def input_back(vecs, dh, own, recv, x):
    return pl.pallas_call(
        input_back_kernel,
        grid=(LEN // BR,),
        out_shape=[shape((LEN, D), BF), shape((8, D), F32)],
        in_specs=[whole_spec(vecs.shape)] + [rows_spec(D)] * 4,
        out_specs=[rows_spec(D), whole_spec((8, D))],
        compiler_params=params(),
        cost_estimate=cost(1e7, 1e7),
        name="input_back",
    )(vecs, dh, own, recv, x)


def in_three(values, spots):
    high = values.astype(BF)
    rest = values - high.astype(F32)
    middle = rest.astype(BF)
    low = (rest - middle.astype(F32)).astype(BF)
    return jnp.where(spots == 0, high, jnp.where(spots == 1, middle, jnp.where(spots == 2, low, jnp.zeros_like(low))))


def attention_back_kernel(layer, *refs):
    which_ref, own, pieces, refs = refs[0], refs[1:3], refs[3:7], refs[7:]
    (vec_ref, dm_ref, own_ref, recv_ref, h_ref, qkv_ref, o_ref, lse_ref), refs = refs[:8], refs[8:]
    (dh_ref, dz_ref, dqkv_ref, da_ref, sums_ref, bias_ref), refs = refs[:6], refs[6:]
    do_ref, dk_ref, dv_ref, wqkv_ref, wout_ref, sems = refs
    start_fetch(which_ref, own, pieces, ((wqkv_ref, QKV_BLOCKS), (wout_ref, OUT_BLOCKS)), sems)
    end_fetch(own[1], wout_ref, sems.at[1])
    gain = vec_ref[8 * layer + 1 : 8 * layer + 2, :]
    sums_ref[...] = jnp.zeros_like(sums_ref)
    bias_ref[...] = jnp.zeros_like(bias_ref)

    def enter(index, carry):
        rows = block_rows(index)
        unit, scale = normalize(h_ref[rows, :])
        dc = own_ref[rows, :].astype(F32) + recv_ref[rows, :].astype(F32)
        sums_ref[0:1, :] += column_sum(dc * unit)
        sums_ref[1:2, :] += column_sum(dc)
        dh = dm_ref[rows, :].astype(F32) + normalize_back(dc, unit, scale, gain)
        dh_ref[rows, :] = dh
        dz = dh.astype(BF)
        dz_ref[rows, :] = dz
        sums_ref[2:3, :] += column_sum(dz.astype(F32))
        sums_ref[3:4, :] += column_sum(dm_ref[rows, :].astype(F32))
        do_ref[rows, :] = mm_nt(dz, wout_ref[...]).astype(BF)
        return carry

    lax.fori_loop(0, NB, enter, 0)

    def attend(group, carry):
        low = lower_lanes(BK)
        low_all = lower_lanes(LEN)
        spots = lax.broadcasted_iota(jnp.int32, (BK, 128), 1) % HS
        ones = jnp.where(lax.broadcasted_iota(jnp.int32, (LEN, 128), 1) % HS < 3, 1.0, 0.0).astype(BF)
        keep_diag = lax.broadcasted_iota(jnp.int32, (BK, BK), 0) <= lax.broadcasted_iota(jnp.int32, (BK, BK), 1)
        nothing = jnp.zeros((BK, 128), BF)
        key = qkv_ref[:, lane_group(3 * group + 1)]
        value = qkv_ref[:, lane_group(3 * group + 2)]
        blank = jnp.zeros_like(key)
        keys_with = (jnp.where(low_all, key, ones), jnp.where(low_all, ones, key))
        values_with = (jnp.where(low_all, value, ones), jnp.where(low_all, ones, value))
        keys_one = (jnp.where(low_all, key, blank), jnp.where(low_all, blank, key))

        def prepare(i):
            mine = slice(i * BK, (i + 1) * BK)
            query = qkv_ref[mine, lane_group(3 * group)]
            do = do_ref[mine, lane_group(group)]
            lse = in_three(-pltpu.roll(lse_ref[mine, lane_group(group)], HS, 1), spots)
            inner = do.astype(F32) * o_ref[mine, lane_group(group)].astype(F32)
            t_low = jnp.sum(jnp.where(low, inner, 0.0), axis=1, keepdims=True)
            t_high = jnp.sum(jnp.where(low, 0.0, inner), axis=1, keepdims=True)
            t = in_three(-jnp.where(low, t_high, t_low), spots)
            return (
                (jnp.where(low, query, lse), jnp.where(low, lse, query)),
                (jnp.where(low, do, t), jnp.where(low, t, do)),
                (jnp.where(low, query, nothing), jnp.where(low, nothing, query)),
                (jnp.where(low, do, nothing), jnp.where(low, nothing, do)),
            )

        def products(i, head, prepared):
            past, here = i * BK, (i + 1) * BK
            query_with, do_with = prepared[0][head], prepared[1][head]
            diag = jnp.where(keep_diag, mm_nt(keys_with[head][past:here], query_with), MASKED_SCORE)
            out = [(diag, mm_nt(values_with[head][past:here], do_with))]
            if i:
                out.append((mm_nt(keys_with[head][:past], query_with), mm_nt(values_with[head][:past], do_with)))
            return out

        units = [(i, head) for i in range(LEN // BK) for head in range(2)]
        prepared = prepare(0)
        ahead = products(0, 0, prepared)
        dq = None
        for number, (i, head) in enumerate(units):
            past, here = i * BK, (i + 1) * BK
            now, now_prepared = ahead, prepared
            if number + 1 < len(units):
                if head == 1:
                    prepared = prepare(i + 1)
                ahead = products(*units[number + 1], prepared)
            query_one, do_one = now_prepared[2][head], now_prepared[3][head]
            for rows, (score, inner) in zip((slice(past, here), slice(0, past)), now):
                p = jnp.exp(score)
                ds = (p * inner).astype(BF)
                dv = mm(p.astype(BF), do_one)
                dk = mm(ds, query_one)
                part = mm_tn(ds, keys_one[head][rows])
                dq = part if dq is None else dq + part
                if head == 0 and rows.start == past:
                    dv_ref[rows, :] = dv
                    dk_ref[rows, :] = dk
                else:
                    dv_ref[rows, :] += dv
                    dk_ref[rows, :] += dk
            if head == 1:
                dqkv_ref[past:here, lane_group(3 * group)] = (dq * 0.125).astype(BF)
                dq = None
        for i in range(NB):
            mine = slice(i * BT, (i + 1) * BT)
            one, two, three = from_pairs(
                dqkv_ref[mine, lane_group(3 * group)].astype(F32), dk_ref[mine, :], dv_ref[mine, :]
            )
            dqkv_ref[mine, lane_group(3 * group)] = one.astype(BF)
            dqkv_ref[mine, lane_group(3 * group + 1)] = two.astype(BF)
            dqkv_ref[mine, lane_group(3 * group + 2)] = three.astype(BF)
        return carry

    lax.fori_loop(0, PAIRS, attend, 0)

    end_fetch(own[0], wqkv_ref, sems.at[0])

    def leave(index, carry):
        rows = block_rows(index)
        dqkv = dqkv_ref[rows, :]
        bias_ref[0:1, :] += column_sum(dqkv.astype(F32))
        da_ref[rows, :] = mm_nt(dqkv, wqkv_ref[...]).astype(BF)
        return carry

    lax.fori_loop(0, NB, leave, 0)


def attention_back(layer, which, weights, vecs, *acts):
    outs = [
        shape((LEN, D), F32),
        shape((LEN, D), BF),
        shape((LEN, QW), BF),
        shape((LEN, D), BF),
        shape((8, D), F32),
        shape((8, QW), F32),
    ]
    return pl.pallas_call(
        functools.partial(attention_back_kernel, layer),
        out_shape=outs,
        in_specs=specs(6, 1 + len(acts)),
        out_specs=[pl.BlockSpec(memory_space=pltpu.VMEM)] * len(outs),
        scratch_shapes=[
            pltpu.VMEM((LEN, HALF), BF),
            pltpu.VMEM((LEN, 128), F32),
            pltpu.VMEM((LEN, 128), F32),
            pltpu.VMEM((D, QW), BF),
            pltpu.VMEM((HALF, D), BF),
            pltpu.SemaphoreType.DMA((2,)),
        ],
        compiler_params=params(),
        cost_estimate=cost(2.2e10, 2.2e7, 4e6),
        name="attention_back",
    )(which, *weights, vecs, *acts)


def feed_grad_kernel(g_ref, dm_ref, c_ref, du_ref, *outs):
    grads, (square_ref, bias_ref) = outs[:4], outs[4:]
    step = pl.program_id(0)

    @pl.when(step == 0)
    def _():
        square_ref[...] = jnp.zeros_like(square_ref)

    def keep(grad, number):
        square_ref[0:1, :] += column_sum(grad * grad)
        for half in range(2):

            @pl.when(step // 2 == half)
            def _(half=half):
                grads[number + 2 * half][...] = grad.astype(BF)

    @pl.when(step % 2 == 0)
    def _():
        keep(mm_tn(g_ref[...], dm_ref[...]), 0)

    @pl.when(step % 2 == 1)
    def _():
        keep(mm_tn(c_ref[...], du_ref[...]), 1)
        bias_ref[0:1, pl.ds(pl.multiple_of(step // 2 * D, 128), D)] = column_sum(du_ref[...].astype(F32))


def feed_grad(g, dm, c, du):
    return pl.pallas_call(
        feed_grad_kernel,
        grid=(4,),
        in_specs=[
            pl.BlockSpec((LEN, D), lambda t: (0, t // 2)),
            pl.BlockSpec((LEN, D), lambda t: (0, 0)),
            pl.BlockSpec((LEN, D), lambda t: (0, 0)),
            pl.BlockSpec((LEN, D), lambda t: (0, t // 2)),
        ],
        out_specs=[pl.BlockSpec((D, D), lambda t: (0, 0))] * 4
        + [pl.BlockSpec((8, D), lambda t: (0, 0)), pl.BlockSpec((8, FW), lambda t: (0, 0))],
        out_shape=[shape((D, D), BF)] * 4 + [shape((8, D), F32), shape((8, FW), F32)],
        compiler_params=params(56 * 1024 * 1024),
        cost_estimate=cost(4 * LEN * D * FW, 1.4e7),
        name="feed_grad",
    )(g, dm, c, du)


def attention_grad_kernel(o_ref, dz_ref, a_ref, dqkv_ref, first_ref, second_ref, square_ref):
    square_ref[...] = jnp.zeros_like(square_ref)
    for part, target in enumerate((first_ref, second_ref)):
        half = slice(part * HALF, (part + 1) * HALF)

        def place(grad, rows, cols):
            square_ref[0:1, 0:HALF] += column_sum(grad * grad)
            target[rows, cols] = grad.astype(BF)

        top = mm_tn(a_ref[:, half], dqkv_ref[...])
        out = mm_tn(o_ref[...], dz_ref[:, half])
        place(top[:, 0:HALF], slice(0, HALF), slice(0, HALF))
        place(top[:, HALF:D], slice(0, HALF), slice(HALF, D))
        for start, grad in ((HALF, top[:, D:]), (HALF + SIDE, out)):
            place(grad[:SIDE], slice(start, start + SIDE), slice(0, HALF))
            place(grad[SIDE:], slice(start, start + SIDE), slice(HALF, D))


def attention_grad(o, dz, a, dqkv):
    vmem = pl.BlockSpec(memory_space=pltpu.VMEM)
    return pl.pallas_call(
        attention_grad_kernel,
        in_specs=[vmem] * 4,
        out_specs=[vmem] * 3,
        out_shape=[shape((D, D), BF), shape((D, D), BF), shape((8, D), F32)],
        compiler_params=params(),
        cost_estimate=cost(2 * LEN * D * (QW + HALF), 1e7),
        name="attention_grad",
    )(o, dz, a, dqkv)


def pack_small_kernel(core_ref, *refs):
    ins, (small_ref, square_ref) = refs[:12], refs[12:]
    small_ref[...] = jnp.zeros_like(small_ref)
    lower = core_ref[0] == 0
    total = jnp.zeros((8, D), F32)
    for layer in range(2):
        bias_qkv, bias_fc, first, second, squares_feed, squares_attention = (ref[...] for ref in ins[6 * layer : 6 * layer + 6])

        def side(values):
            return jnp.where(lower, values[:, :HALF], values[:, HALF:])

        small_ref[layer, 0:1, :] = bias_fc[0:1, 0:D]
        small_ref[layer, 1:2, :] = bias_fc[0:1, D:]
        small_ref[layer, 2:3, :] = bias_qkv[0:1, 0:D]
        small_ref[layer, 3:4, 0:HALF] = bias_qkv[0:1, D:]
        rows = (first[0:1], second[0:1], first[1:2], second[2:3], second[1:2], second[3:4])
        for number, row in enumerate(rows):
            line, right = divmod(number + 1, 2)
            small_ref[layer, 3 + line : 4 + line, right * HALF : (right + 1) * HALF] = side(row)
        total = total + squares_feed + squares_attention
        total = total + small_ref[layer, 0:8, :] * small_ref[layer, 0:8, :]
    square_ref[...] = jnp.broadcast_to(jnp.sum(total, keepdims=True), (8, 128))


def pack_small(core, *parts):
    vmem = pl.BlockSpec(memory_space=pltpu.VMEM)
    return pl.pallas_call(
        pack_small_kernel,
        in_specs=[pl.BlockSpec(memory_space=pltpu.SMEM)] + [vmem] * 12,
        out_specs=[vmem] * 2,
        out_shape=[shape((2, 16, D), F32), shape((8, 128), F32)],
        compiler_params=params(),
        cost_estimate=cost(1e5, 1e5),
        name="pack_small",
    )(core, *parts)


def unpack_small(rows):
    tail = rows[3:7].reshape(8, HALF)
    bias = jnp.concatenate([rows[2], tail[0]])
    return bias, rows[0:2].reshape(FW), tail[1:3], tail[3:7]


def weigh_kernel(rows, roles_ref, weight_ref, *refs):
    sources, refs = refs[:8], refs[8:]
    if len(refs) == 6:
        (small_ref, other_ref, keep_ref, aside_ref, held_ref, sems) = refs
    else:
        (other_ref, keep_ref, aside_ref, held_ref, sems) = refs
        small_ref = None
    mine, home = roles_ref[0], roles_ref[1]

    def bring(slot, one, two):
        for number, source in enumerate((one, two)):
            pltpu.make_async_copy(source.at[rows], held_ref.at[2 * slot + number], sems.at[slot]).start()

    for layer in range(2):
        first, first_there, second, second_there = sources[4 * layer : 4 * layer + 4]

        @pl.when(mine == layer)
        def _(second=second, second_there=second_there):
            bring(2, second, second_there)

        for role in range(2):

            @pl.when((home == 1) & ((mine == layer) == (role == 1)))
            def _(role=role, first=first, first_there=first_there):
                bring(role, first, first_there)

    count = held_ref.shape[1]

    def total(slot, weight):
        both = held_ref.at[pl.ds(2 * slot, 2)]
        pltpu.make_async_copy(both, both, sems.at[slot]).wait()
        return weight_ref[0] * held_ref[2 * slot].astype(F32) + weight * held_ref[2 * slot + 1].astype(F32)

    @pl.when(home == 1)
    def _():
        for slot, target in ((0, other_ref), (1, keep_ref)):
            target[0:count, :] = total(slot, weight_ref[1]).astype(target.dtype)
            if small_ref is not None:
                target[count:, :] = jnp.where(mine == slot, small_ref[1], small_ref[0]).astype(target.dtype)
        aside_ref[0:count, :] = total(2, weight_ref[2]).astype(BF)
        if small_ref is not None:
            aside_ref[count:, :] = jnp.zeros((16, D), BF)

    @pl.when(home == 0)
    def _():
        other_ref[0:count, :] = total(2, weight_ref[2]).astype(BF)
        if small_ref is not None:
            other_ref[count:, :] = jnp.zeros((16, D), BF)


def weigh(rows, roles, weights, layers, small=None):
    count = rows.stop - rows.start
    tall = count + (0 if small is None else 16)
    vmem, smem, hbm = (pl.BlockSpec(memory_space=kind) for kind in (pltpu.VMEM, pltpu.SMEM, pl.ANY))
    return pl.pallas_call(
        functools.partial(weigh_kernel, pl.ds(rows.start, count)),
        out_shape=[shape((tall, D), BF), shape((tall, D), F32), shape((tall, D), BF)],
        in_specs=[smem, smem] + [hbm] * 8 + ([] if small is None else [vmem]),
        out_specs=[vmem] * 3,
        scratch_shapes=[pltpu.VMEM((6, count, D), BF), pltpu.SemaphoreType.DMA((3,))],
        compiler_params=params(),
        cost_estimate=cost(1e7, 1e7),
        name="weigh",
    )(roles, weights, *layers[0], *layers[1], *(() if small is None else (small,)))


def finish_feed_kernel(columns, denominator, home_ref, *refs):
    own, swapped = refs[0:2], refs[2:4]
    noise_ref, grad_ref = refs[4:]
    scale, step = NOISE_MULT * CLIP_FRACTION * math.sqrt(LEN * FF * D), D // 2

    def run(parts):
        for number, part in enumerate(parts):
            for index in range(2):
                if columns:
                    where = (slice(index * step, (index + 1) * step), slice(number * D, (number + 1) * D))
                else:
                    where = (slice(number * D + index * step, number * D + (index + 1) * step), slice(0, D))
                noise = noise_ref[where].astype(F32)
                grad_ref[where] = (part[index][0:step, :].astype(F32) + scale * noise) / denominator

    @pl.when(home_ref[0] == 1)
    def _():
        run((own, swapped))

    @pl.when(home_ref[0] == 0)
    def _():
        run((swapped, own))


def finish_attention_kernel(denominator, home_ref, *refs):
    own, swapped = refs[0:2], refs[2:4]
    noise_qkv_ref, noise_out_ref, qkv_ref, out_ref = refs[4:]
    scale, side = NOISE_MULT * CLIP_FRACTION * math.sqrt(LEN * FF * D), HALF // 2

    def put(target, noise_ref, rows, cols, block):
        target[rows, cols] = (block.astype(F32) + scale * noise_ref[rows, cols].astype(F32)) / denominator

    def run(parts):
        for number, (one, two) in enumerate(parts):
            start = number * HALF
            put(qkv_ref, noise_qkv_ref, slice(start, start + HALF), slice(0, D), one[...])
            for index in range(2):
                cols = slice(index * HALF, (index + 1) * HALF)
                rows = slice(start + index * side, start + (index + 1) * side)
                put(qkv_ref, noise_qkv_ref, rows, slice(D, QW), two[0:side, cols])
                rows = slice(index * side, (index + 1) * side)
                put(out_ref, noise_out_ref, rows, slice(start, start + HALF), two[side : 2 * side, cols])

    @pl.when(home_ref[0] == 1)
    def _():
        run((own, swapped))

    @pl.when(home_ref[0] == 0)
    def _():
        run((swapped, own))


def finish(kernel, denominator, home, own, swapped, noises, name):
    vmem = pl.BlockSpec(memory_space=pltpu.VMEM)
    return pl.pallas_call(
        functools.partial(kernel, denominator),
        out_shape=[shape(noise.shape, F32) for noise in noises],
        in_specs=[pl.BlockSpec(memory_space=pltpu.SMEM)] + [vmem] * (2 * len(own) + len(noises)),
        out_specs=[vmem] * len(noises),
        compiler_params=params(),
        cost_estimate=cost(1e7, 1.6e7),
        name=name,
    )(home, *own, *swapped, *noises)


def send(values, route):
    sections, ranks = lax.axis_size("section"), lax.axis_size("dp")
    pairs = []
    for section in range(sections):
        for rank in range(ranks):
            target = route(section, rank // 2, rank % 2)
            if target is not None:
                to_section, to_pair, to_core = target
                pairs.append((section * ranks + rank, to_section * ranks + to_pair * 2 + to_core))
    return lax.ppermute(values, ("section", "dp"), pairs)


def swap_cores(values):
    return send(values, lambda s, z, c: (s, z, 1 - c))


def is_home(s, c):
    return s % 2 == c


def after(values, *others):
    return lax.optimization_barrier((values, *others))[0]


def local(
    inputs,
    cotangent,
    included,
    qkv_weight,
    qkv_bias,
    out_weight,
    fc_weight,
    fc_bias,
    proj_weight,
    norm_gains,
    shifts,
    noise,
):
    clip_norm = CLIP_FRACTION * math.sqrt(LEN * FF * D)
    section = lax.axis_index("section")
    rank = lax.axis_index("dp")
    ranks = lax.axis_size("dp")
    row, half = section // 2, section % 2
    place, core = rank // 2, rank % 2
    home = half == core
    on_top = row == 0
    flip = home.astype(jnp.int32).reshape(1)
    denominator = SAMPLE_RATE * inputs.shape[0] * ranks

    side = place % 2

    def piece_of(weight, number):
        tall = weight.shape[0] // 2
        if number is None:
            return lax.dynamic_slice_in_dim(weight, side * tall, tall, 0)
        return weight[number * tall : (number + 1) * tall]

    def attention_piece(number):
        qkv = piece_of(qkv_weight, number)
        tail = jnp.concatenate([qkv[:SIDE, D:], qkv[SIDE:, D:]], axis=1)
        return jnp.concatenate([qkv[:, :D], tail, piece_of(out_weight, number)])

    fc_piece = piece_of(fc_weight, None)
    fc_piece = jnp.concatenate([fc_piece[:, :D], fc_piece[:, D:]])

    def near(piece):
        return send(piece, lambda s, z, c: (s ^ 2, z, c) if is_home(s, c) else (s ^ 1, z, 1 - c))

    def far(one, two):
        far_one = send(one, lambda s, z, c: (s ^ 1, z, c) if is_home(s, c) else None)
        return far_one, send(two, lambda s, z, c: None if is_home(s, c) else (s ^ 2, z, c))

    def next_plane(one):
        return send(one, lambda s, z, c: (s, z ^ 1, c))

    fc_one = near(fc_piece)
    proj_piece, fc_one = lax.optimization_barrier((piece_of(proj_weight, None), fc_one))
    proj_one = near(proj_piece)
    *parts, proj_one = lax.optimization_barrier((attention_piece(0), attention_piece(1), proj_one))
    attention_pieces = tuple(near(part) for part in parts)
    fc_two = next_plane(fc_one)
    later, fc_two = lax.optimization_barrier((proj_one, fc_two))
    proj_two = next_plane(later)
    shapes = ((D, QW), (QW,), (HALF, D), (D, FW), (FW,), (FW, D), (2, HALF), (4, HALF))
    noise, fc_one = lax.optimization_barrier((noise, fc_one))
    noises, offset = [], 0
    for dims in shapes:
        noises.append(noise[offset : offset + math.prod(dims)].reshape(dims))
        offset += math.prod(dims)
    held = lax.optimization_barrier((*attention_pieces, *noises))
    attention_pieces, noises = held[:2], held[2:]
    attention_pieces += far(*attention_pieces)
    fc_pieces = (fc_one, fc_two, *far(fc_one, fc_two))
    proj_pieces = (proj_one, proj_two, *far(proj_one, proj_two))
    attention_weights = (qkv_weight, out_weight, *attention_pieces)
    feed_weights_all = (fc_weight, proj_weight, *fc_pieces, *proj_pieces)

    def which_of(layer):
        kind = jnp.where(row == layer, jnp.where(home, 0, 1), jnp.where(home, 1, 2))
        return [jnp.stack([kind, first]).astype(jnp.int32) for first in (jnp.zeros_like(side), side)]

    which_attention, which_feed = zip(which_of(0), which_of(1))

    def own_sequence(values):
        mine = lax.dynamic_index_in_dim(values, half, 0, keepdims=False)
        theirs = swap_cores(mine)
        return jnp.where(core == row, mine, theirs)

    small = jnp.concatenate([qkv_bias, fc_bias, norm_gains.reshape(-1), shifts.reshape(-1)]).reshape(1, -1)
    others = [send(small, lambda s, z, c, bits=bits: (s ^ bits, z, c)) for bits in (1, 2, 3)]
    x0 = own_sequence(inputs)
    cot = own_sequence(cotangent)
    drawn = own_sequence(jnp.broadcast_to(included.astype(F32)[:, None, None], (2, 8, 128)))[0, 0]
    small_all = jnp.concatenate([small] + others, axis=0)
    small_all = jnp.where(half == 0, small_all, small_all[jnp.array([1, 0, 3, 2])])
    small_all = jnp.where(on_top, small_all, small_all[jnp.array([2, 3, 0, 1])])
    small_all = small_all.reshape(2, 2, -1)
    bias = jnp.where(core == 0, small_all[:, 0], small_all[:, 1])
    bqkv, bfc = bias[:, :QW], bias[:, QW : QW + FW]
    vecs = small_all[:, :, QW + FW :].reshape(2, 2, 6, HALF).transpose(0, 2, 1, 3).reshape(2, 6, D)
    vecs = jnp.pad(vecs, ((0, 0), (0, 2), (0, 0))).reshape(16, D)

    shapes = ((D, QW), (QW,), (HALF, D), (D, FW), (FW,), (FW, D), (2, HALF), (4, HALF))
    a0, qkv0, o0, lse0, part = attention_forward(0, which_attention[0], attention_weights, vecs, bqkv, x0)
    part_theirs = swap_cores(part)
    h0, c0, g0, part_two, slope0 = feed_forward(
        0, which_feed[0], feed_weights_all, vecs, bfc, x0, part, part_theirs
    )
    a1, qkv1, o1, lse1, part, x1 = attention_forward(
        1, which_attention[1], attention_weights, vecs, bqkv, h0, part_two, swap_cores(part_two)
    )
    h1, c1, g1, part_two, du1, dc = feed_forward(
        1, which_feed[1], feed_weights_all, vecs, bfc, x1, part, swap_cores(part), cot
    )
    dc_theirs = swap_cores(dc)
    y1 = (h1 + (part_two.astype(F32) + swap_cores(part_two).astype(F32)) + vecs[13:14]).astype(BF)

    def spread(block_for):
        received = []
        for step in range(2):
            block = block_for(2 * core + (step ^ half))
            received.append(send(block, lambda s, z, c, step=step: (2 * c + (step ^ (s % 2)), z, s // 2)))
        first, second = received
        return jnp.where(half == 0, jnp.stack([first, second]), jnp.stack([second, first]))

    both_out = jnp.concatenate([x1, y1], axis=1)
    def over_x(values):
        return send(values, lambda s, z, c: None if is_home(s, c) else (s ^ 1, z, c))

    def over_y(layer, values):
        return send(values, lambda s, z, c: None if s // 2 == layer else (s ^ 2, z, c))

    *grads1, squares_feed1, bias_fc1 = feed_grad(g1, cot, c1, du1)
    dc, dc_theirs, *grads1 = lax.optimization_barrier((dc, dc_theirs, *grads1))
    proj_x1, fc_x1, proj_y1 = over_x(grads1[0]), over_x(grads1[1]), over_y(1, grads1[2])
    dh1, dz1, dqkv1, da, sums1, bias_qkv1 = attention_back(
        1, which_attention[1], attention_weights, vecs, cot, dc, dc_theirs, h1, qkv1, o1, lse1
    )
    da, proj_x1, fc_x1, proj_y1 = lax.optimization_barrier((da, proj_x1, fc_x1, proj_y1))
    da_theirs = swap_cores(da)
    fc_y1 = over_y(1, grads1[3])
    first1, second1, squares_attention1 = attention_grad(o1, dz1, a1, dqkv1)
    da, da_theirs, first1 = lax.optimization_barrier((da, da_theirs, first1))
    dm0, du0, dc, first_sums1 = feed_back(which_feed[0], feed_weights_all, vecs, dh1, da, da_theirs, x1, slope0)
    dc, fc_y1 = lax.optimization_barrier((dc, fc_y1))
    dc_theirs = swap_cores(dc)
    attention_x1 = over_x(first1)
    *grads0, squares_feed0, bias_fc0 = feed_grad(g0, dm0, c0, du0)
    dc, dc_theirs, attention_x1, *grads0 = lax.optimization_barrier((dc, dc_theirs, attention_x1, *grads0))
    proj_x0, fc_x0, proj_y0 = over_x(grads0[0]), over_x(grads0[1]), over_y(0, grads0[2])
    attention_y1 = over_y(1, second1)
    dh0, dz0, dqkv0, da, sums0, bias_qkv0 = attention_back(
        0, which_attention[0], attention_weights, vecs, dm0, dc, dc_theirs, h0, qkv0, o0, lse0
    )
    da, proj_x0, fc_x0, proj_y0, attention_y1 = lax.optimization_barrier((da, proj_x0, fc_x0, proj_y0, attention_y1))
    da_theirs = swap_cores(da)
    fc_y0 = over_y(0, grads0[3])
    first0, second0, squares_attention0 = attention_grad(o0, dz0, a0, dqkv0)
    attention_x0, attention_y0 = over_x(first0), over_y(0, second0)
    dx0, first_sums0 = input_back(vecs, dh0, da, da_theirs, x0)
    small_pair, squares = pack_small(
        core.astype(jnp.int32).reshape(1),
        *(bias_qkv0, bias_fc0, first_sums0, sums0, squares_feed0, squares_attention0),
        *(bias_qkv1, bias_fc1, first_sums1, sums1, squares_feed1, squares_attention1),
    )
    small_there = send(small_pair, lambda s, z, c: None if is_home(s, c) else (s ^ 1, z, c))

    squares = squares + swap_cores(squares)
    factor = drawn * jnp.minimum(1.0, clip_norm / jnp.sqrt(squares))
    across = send(factor, lambda s, z, c: (s ^ 1, z, 1 - c) if is_home(s, c) else None)
    above = send(factor, lambda s, z, c: (s ^ 2, z, c))
    weights = jnp.stack([factor[0, 0], across[0, 0], above[0, 0]])
    weights, fc_y0 = lax.optimization_barrier((weights, fc_y0))
    roles = jnp.stack([row, home]).astype(jnp.int32)
    small_sum = jnp.where(home, weights[0] * small_pair + weights[1] * small_there, 0.0)

    proj0, proj1 = (grads0[0], proj_x0, grads0[2], proj_y0), (grads1[0], proj_x1, grads1[2], proj_y1)
    fc0, fc1 = (grads0[1], fc_x0, grads0[3], fc_y0), (grads1[1], fc_x1, grads1[3], fc_y1)
    attention0 = (first0, attention_x0, second0, attention_y0)
    attention1 = (first1, attention_x1, second1, attention_y1)

    token_rows = LEN // lax.axis_size("section")

    def exchange_outputs(both_out, dx0):
        layer_out = spread(lambda block: lax.dynamic_slice_in_dim(both_out, block * HALF, HALF, 1))
        return layer_out, spread(lambda block: lax.dynamic_slice_in_dim(dx0, block * token_rows, token_rows, 0))

    places = ranks // 2
    middle = places // 2

    def to_middle(step):
        def route(s, z, c):
            if z == step:
                return (s, z + 1, c)
            if z == places - 1 - step:
                return (s, z - 1, c)
            return None

        return route

    def at_middle(s, z, c):
        return (s, places - 1 - z, c) if z in (middle - 1, middle) else None

    def from_middle(step):
        def route(s, z, c):
            if z == middle - 1 - step:
                return (s, z - 1, c)
            if z == middle + step:
                return (s, z + 1, c)
            return None

        return route

    def add(left, right):
        return (left.astype(F32) + right.astype(F32)).astype(BF)

    def weigh_stage(args):
        other, keep, aside = weigh(*args)
        arrived = send(other, lambda s, z, c: (s ^ 2, z, c) if is_home(s, c) else (s ^ 1, z, 1 - c))
        aside = send(aside, lambda s, z, c: (s, z, 1 - c) if is_home(s, c) else None)
        return keep, aside, arrived

    def weigh_end(held):
        keep, aside, arrived = held
        return (jnp.where(home, keep, aside.astype(F32)) + arrived.astype(F32)).astype(BF)

    def chain_stage(hop):
        def stage(held):
            total = add(*held) if len(held) == 2 else weigh_end(held)
            return total, send(total, hop)

        return stage

    def spread_stage(step):
        def stage(held):
            total, arrived = held
            if step == 0:
                total = add(total, arrived)
            else:
                takes = (place == middle - 1 - step) | (place == middle + step)
                total = jnp.where(takes, arrived, total)
            return total, send(total, from_middle(step))

        return stage

    def last_stage(held):
        total, arrived = held
        if middle > 1:
            takes = (place == 0) | (place == places - 1)
            total = jnp.where(takes, arrived, total)
        else:
            total = add(total, arrived)
        return total, swap_cores(total)

    hops = [to_middle(step) for step in range(middle - 1)] + [at_middle]
    stages = [weigh_stage] + [chain_stage(hop) for hop in hops]
    stages += [spread_stage(step) for step in range(middle - 1)] + [last_stage]

    chunk = D // 2
    jobs = []
    for pair in ((proj0, proj1), (fc0, fc1)):
        jobs += [(slice(i * chunk, (i + 1) * chunk), roles, weights, pair) for i in range(2)]
    jobs[2] += (small_sum,)

    def finish_proj(one, two):
        return finish(
            functools.partial(finish_feed_kernel, False), denominator, flip, *zip(one, two), (noises[5],), "finish_feed"
        )[0]

    def finish_fc(one, two):
        return finish(
            functools.partial(finish_feed_kernel, True), denominator, flip, *zip(one, two), (noises[3],), "finish_feed"
        )[0]

    if middle == 2:
        edge = (place == 0) | (place == places - 1)

        def to_next(s, z, c):
            return (s, z ^ 1, c)

        count = len(jobs) + 2
        kept, passing, arriving, sums, lows, totals, ready = {}, {}, {}, {}, {}, {}, {}
        inner, outer, last = None, None, None

        def tie(*values):
            if last is None:
                return values if len(values) > 1 else values[0]
            store, name = last
            *values, store[name] = lax.optimization_barrier((*values, store[name]))
            return values if len(values) > 1 else values[0]

        for tick in range(count + 4):
            old_inner, old_outer = inner, outer
            if tick == 2:
                attention_x0, attention_y0 = tie(attention_x0, attention_y0)
                attention0 = (first0, attention_x0, second0, attention_y0)
                jobs += [(slice(i * chunk, (i + 1) * chunk), roles, weights, (attention0, attention1)) for i in range(2)]
            if tick == count:
                layer_out, input_grad = exchange_outputs(*tie(both_out, dx0))
            if tick < count:
                held = jobs[tick]
                held = (held[0], held[1], tie(held[2])) + held[3:]
                kept[tick], passing[tick], arriving[tick] = weigh_stage(held)
                last = kept, tick
            if 0 <= tick - 1 < count:
                keep = tie(kept.pop(tick - 1)) if tick < count else kept.pop(tick - 1)
                sums[tick - 1] = weigh_end((keep, passing.pop(tick - 1), arriving.pop(tick - 1)))
                last = sums, tick - 1
            if 0 <= tick - 3 < count:
                totals[tick - 3] = add(tie(lows.pop(tick - 3)), old_inner)
                last = totals, tick - 3
            inward, outward = sums.get(tick - 1), totals.get(tick - 3)
            if inward is not None and outward is not None:
                tall = [inward.shape[0], outward.shape[0]]
                padded = [jnp.pad(part, ((0, max(tall) - part.shape[0]), (0, 0))) for part in (inward, outward)]
                outer = send(jnp.where(edge, *padded), to_next)
                outer = (outer[: tall[0]], outer[: tall[1]])
            else:
                outer = (
                    None if inward is None else send(inward, to_middle(0)),
                    None if outward is None else send(outward, from_middle(0)),
                )
            if 0 <= tick - 2 < count:
                low = sums.pop(tick - 2)
                if last[0] is not sums or last[1] != tick - 2:
                    low = tie(low)
                lows[tick - 2] = add(low, old_outer[0])
                last = lows, tick - 2
                inner = send(lows[tick - 2], at_middle)
            if 0 <= tick - 4 < count:
                total = totals.pop(tick - 4)
                if last[0] is not totals or last[1] != tick - 4:
                    total = tie(total)
                ready[tick - 4] = jnp.where(edge, old_outer[1], total)
                last = ready, tick - 4
                if tick == 6:
                    proj_grad = finish_proj(*((ready[i], swap_cores(ready[i])) for i in (0, 1)))
                if tick == 8:
                    proj_grad = tie(proj_grad)
                    pairs = [(ready[i], swap_cores(ready[i])) for i in (2, 3)]
                    fc_grad = finish_fc(*pairs)
                    small_own, small_swapped = pairs[0]
                if tick == count + 2:
                    layer_out, input_grad = tie(layer_out, input_grad)
        jobs = [None] * 4 + [(ready[i], swap_cores(ready[i])) for i in (4, 5)]
        stages = []
    else:
        jobs += [(slice(i * chunk, (i + 1) * chunk), roles, weights, (attention0, attention1)) for i in range(2)]
        layer_out, input_grad = exchange_outputs(both_out, dx0)
    done = None
    for tick in range(len(jobs) + len(stages) - 1 if stages else 0):
        for stage in reversed(range(len(stages))):
            index = tick - stage
            if 0 <= index < len(jobs):
                held = jobs[index]
                if stage == 0:
                    if done is not None:
                        held = (held[0], held[1], after(held[2], done)) + held[3:]
                elif done is not None:
                    held = (after(held[0], done), *held[1:])
                jobs[index] = stages[stage](held)
                done = jobs[index][0]
    if stages:
        proj_grad, fc_grad = finish_proj(*jobs[0:2]), finish_fc(*jobs[2:4])
        small_own, small_swapped = jobs[2]
    attention = jobs[4:]
    own, swapped = zip(*attention)
    qkv_grad, out_grad = finish(
        finish_attention_kernel, denominator, flip, own, swapped, (noises[0], noises[2]), "finish_attention"
    )
    small_sum = jnp.where(home, small_own[chunk:], small_swapped[chunk:]).astype(F32)
    small_done = [
        (part + NOISE_MULT * clip_norm * noises[number].astype(F32)) / denominator
        for part, number in zip(unpack_small(small_sum), (1, 4, 6, 7))
    ]
    return (
        layer_out,
        input_grad,
        qkv_grad,
        small_done[0],
        out_grad,
        fc_grad,
        small_done[1],
        proj_grad,
        small_done[2],
        small_done[3],
    )


def solution(mesh):
    return jax.shard_map(
        local,
        mesh=mesh,
        in_specs=(
            P("dp", None, None),
            P("dp", None, None),
            P("dp"),
            P(None, "section"),
            P("section"),
            P("section", None),
            P(None, "section"),
            P("section"),
            P("section", None),
            P(None, "section"),
            P(None, "section"),
            P("section"),
        ),
        out_specs=(
            P("dp", None, "section"),
            P("dp", "section", None),
            P(None, "section"),
            P("section"),
            P("section", None),
            P(None, "section"),
            P("section"),
            P("section", None),
            P(None, "section"),
            P(None, "section"),
        ),
        check_vma=False,
    )
```

```python
import functools
import math

import jax
import jax.numpy as jnp
from jax import lax
from jax.experimental import pallas as pl
from jax.experimental.pallas import tpu as pltpu
from jax.sharding import PartitionSpec as P

D = 768
FF = 3072
HS = 64
LEN = 1024
HALF = D // 2
QW = 3 * HALF
FW = FF // 2
PAIRS = HALF // 128
BT = 256
NB = LEN // BT
BQ = 256
BR = 512
BK = 256

CLIP_FRACTION = 0.05
NOISE_MULT = 0.001
SAMPLE_RATE = 0.5
NORM_EPS = 1e-05
MASKED_SCORE = -1e30
VMEM_BYTES = 58 * 1024 * 1024
SMALL_VMEM_BYTES = 36 * 1024 * 1024

BF = jnp.bfloat16
F32 = jnp.float32


def mm(left, right):
    return lax.dot_general(left, right, (((1,), (0,)), ((), ())), preferred_element_type=F32)


def mm_nt(left, right):
    return lax.dot_general(left, right, (((1,), (1,)), ((), ())), preferred_element_type=F32)


def mm_tn(left, right):
    return lax.dot_general(left, right, (((0,), (0,)), ((), ())), preferred_element_type=F32)


def normalize(values):
    center = values - jnp.mean(values, axis=-1, keepdims=True)
    spread = jnp.mean(center * center, axis=-1, keepdims=True)
    scale = lax.rsqrt(spread + NORM_EPS)
    return center * scale, scale


def normalize_back(grad, unit, scale, gain):
    inner = grad * gain
    mean_inner = jnp.mean(inner, axis=-1, keepdims=True)
    mean_cross = jnp.mean(inner * unit, axis=-1, keepdims=True)
    return scale * (inner - mean_inner - unit * mean_cross)


def column_sum(values):
    return jnp.sum(values, axis=0, keepdims=True)


def block_rows(index):
    return pl.ds(pl.multiple_of(index * BT, BT), BT)


def lane_group(index, width=128):
    return pl.ds(pl.multiple_of(index * 128, 128), width)


def lower_lanes(rows=BT):
    return lax.broadcasted_iota(jnp.int32, (rows, 128), 1) < HS


def to_pairs(block, group):
    low = lower_lanes()
    start = 3 * 128 * group
    one, two, three = (block[:, start + 128 * i : start + 128 * (i + 1)] for i in range(3))
    query = jnp.where(low, one, two)
    key = pltpu.roll(jnp.where(low, three, one), HS, 1)
    value = jnp.where(low, two, three)
    return query, key, value


def from_pairs(query, key, value):
    low = lower_lanes()
    turned = pltpu.roll(key, HS, 1)
    return jnp.where(low, query, turned), jnp.where(low, value, query), jnp.where(low, turned, value)


class Copies:
    def __init__(self, sems):
        self.sems, self.used, self.left = sems, 0, []

    def begin(self, source, target):
        copy = pltpu.make_async_copy(source, target, self.sems.at[self.used])
        self.used += 1
        copy.start()
        return copy

    def leave(self, source, target):
        self.left.append(self.begin(source, target))

    def finish(self):
        for copy in self.left:
            copy.wait()


COPIES = 64


def row_slices(tall):
    return [slice(start, start + tall) for start in range(0, LEN, tall)]


def part_of(ref, rows):
    return ref.at[pl.ds(rows.start, rows.stop - rows.start)]


def start_fetch(which_ref, own, pieces, parts, sems):
    @pl.when(which_ref[0] == 0)
    def _():
        for number, (target, _) in enumerate(parts):
            pltpu.make_async_copy(own[number], target, sems.at[number]).start()

    for kind in (1, 2):

        @pl.when(which_ref[0] == kind)
        def _(kind=kind):
            for order in range(2):
                piece = pieces[2 * kind - 2 + order]
                side = which_ref[1] if order == 0 else 1 - which_ref[1]
                for number, (target, blocks) in enumerate(parts):
                    base = pl.multiple_of(side * (target.shape[0] // 2), 64)
                    for (top, left), (tall, wide), (down, right) in blocks:
                        pltpu.make_async_copy(
                            piece.at[pl.ds(top, tall), pl.ds(left, wide)],
                            target.at[pl.ds(base + down, tall), pl.ds(right, wide)],
                            sems.at[number],
                        ).start()


def end_fetch(own, target, sem):
    pltpu.make_async_copy(own, target, sem).wait()


SIDE = HALF // 2
QKV_BLOCKS = (
    ((0, 0), (HALF, D), (0, 0)),
    ((HALF, 0), (SIDE, HALF), (0, D)),
    ((HALF, HALF), (SIDE, HALF), (SIDE, D)),
)
OUT_BLOCKS = (((HALF + SIDE, 0), (SIDE, D), (0, 0)),)
FC_BLOCKS = (((0, 0), (HALF, D), (0, 0)), ((HALF, 0), (HALF, D), (0, D)))
PROJ_BLOCKS = (((0, 0), (D, D), (0, 0)),)


def attention_forward_kernel(layer, *refs):
    which_ref, own, pieces, refs = refs[0], refs[1:3], refs[3:7], refs[7:]
    vec_ref, bqkv_ref, refs = refs[0], refs[1], refs[2:]
    first = layer == 0
    count = 1 if first else 3
    ins, refs = refs[:count], refs[count:]
    outs, refs = refs[: 5 if first else 6], refs[5 if first else 6 :]
    held, refs = refs[:count], refs[count:]
    (a_ref, qkv_ref, o_ref, lse_ref, part_ref), refs = refs[:5], refs[5:]
    if not first:
        x_ref, refs = refs[0], refs[1:]
    wqkv_ref, wout_ref, sems, copy_sems = refs
    copies = Copies(copy_sems)
    blocks = row_slices(BT)
    arriving = [[copies.begin(part_of(src, rows), part_of(dst, rows)) for src, dst in zip(ins, held)] for rows in blocks]
    start_fetch(which_ref, own, pieces, ((wqkv_ref, QKV_BLOCKS), (wout_ref, OUT_BLOCKS)), sems)

    for number, rows in enumerate(blocks):
        for copy in arriving[number]:
            copy.wait()
        if first:
            values = held[0][rows, :].astype(F32)
        else:
            total = held[0][rows, :] + (held[1][rows, :].astype(F32) + held[2][rows, :].astype(F32)) + vec_ref[5:6, :]
            x_ref[rows, :] = total.astype(BF)
            copies.leave(part_of(x_ref, rows), part_of(outs[5], rows))
            values = total.astype(BF).astype(F32)
        unit, _ = normalize(values)
        a = (unit * vec_ref[8 * layer : 8 * layer + 1, :] + vec_ref[8 * layer + 2 : 8 * layer + 3, :]).astype(BF)
        a_ref[rows, :] = a
        copies.leave(part_of(a_ref, rows), part_of(outs[0], rows))
        if number == 0:
            end_fetch(own[0], wqkv_ref, sems.at[0])
        projected = mm(a, wqkv_ref[...]) + bqkv_ref[layer : layer + 1, :]
        for group in range(PAIRS):
            query, key, value = to_pairs(projected, group)
            start = 3 * 128 * group
            qkv_ref[rows, start : start + 128] = query.astype(BF) * 0.125
            qkv_ref[rows, start + 128 : start + 256] = key.astype(BF)
            qkv_ref[rows, start + 256 : start + 384] = value.astype(BF)
        copies.leave(part_of(qkv_ref, rows), part_of(outs[1], rows))

    def attend(group, carry):
        low = lower_lanes(BQ)
        keep_diag = lax.broadcasted_iota(jnp.int32, (BQ, BQ), 1) <= lax.broadcasted_iota(jnp.int32, (BQ, BQ), 0)
        value = qkv_ref[:, lane_group(3 * group + 2)]
        low_all = lower_lanes(LEN)
        one = jnp.ones_like(value)
        values = (jnp.where(low_all, value, one), jnp.where(low_all, one, value))

        def scores(i, head):
            past, here = i * BQ, (i + 1) * BQ
            query = qkv_ref[past:here, lane_group(3 * group)]
            nothing = jnp.zeros_like(query)
            query = jnp.where(low, query, nothing) if head == 0 else jnp.where(low, nothing, query)
            diag = jnp.where(keep_diag, mm_nt(query, qkv_ref[past:here, lane_group(3 * group + 1)]), MASKED_SCORE)
            left = mm_nt(query, qkv_ref[0:past, lane_group(3 * group + 1)]) if i else None
            return diag, left

        units = [(i, head) for i in range(LEN // BQ) for head in range(2)]
        ahead = scores(*units[0])
        mixed, largest = [], []
        for number, (i, head) in enumerate(units):
            past, here = i * BQ, (i + 1) * BQ
            diag, left = ahead
            if number + 1 < len(units):
                ahead = scores(*units[number + 1])
            top = jnp.max(diag, axis=1, keepdims=True)
            if i:
                top = jnp.maximum(top, jnp.max(left, axis=1, keepdims=True))
            total = mm(jnp.exp(diag - top).astype(BF), values[head][past:here])
            if i:
                total = total + mm(jnp.exp(left - top).astype(BF), values[head][:past])
            mixed.append(total)
            largest.append(top)
            if head == 1:
                sums = pltpu.roll(jnp.where(low, mixed[1], mixed[0]), HS, 1)
                o_ref[past:here, lane_group(group)] = (jnp.where(low, mixed[0], mixed[1]) / sums).astype(BF)
                lse_ref[past:here, lane_group(group)] = jnp.where(low, largest[0], largest[1]) + jnp.log(sums)
                mixed, largest = [], []
        return carry

    lax.fori_loop(0, PAIRS, attend, 0)

    copies.leave(o_ref, outs[2])
    copies.leave(lse_ref, outs[3])
    end_fetch(own[1], wout_ref, sems.at[1])
    for rows in row_slices(512):
        part_ref[rows, :] = mm(o_ref[rows, :], wout_ref[...]).astype(BF)
        copies.leave(part_of(part_ref, rows), part_of(outs[4], rows))
    copies.finish()


def params(limit=VMEM_BYTES):
    return pltpu.CompilerParams(vmem_limit_bytes=limit)


def shape(dims, kind):
    return jax.ShapeDtypeStruct(dims, kind)


def cost(flops, moved, transcendentals=0):
    return pl.CostEstimate(flops=int(flops) // 1000, bytes_accessed=int(moved) // 1000, transcendentals=0)


def buffers(values):
    return [pltpu.VMEM(value.shape, value.dtype) for value in values]


def run_kernel(kernel, name, smem, weights, rows, acts, outs, scratch, flops):
    smem_spec, vmem, hbm = (pl.BlockSpec(memory_space=kind) for kind in (pltpu.SMEM, pltpu.VMEM, pl.ANY))
    return pl.pallas_call(
        kernel,
        out_shape=outs,
        in_specs=[smem_spec] * len(smem) + [hbm] * len(weights) + [vmem] * len(rows) + [hbm] * len(acts),
        out_specs=[hbm] * len(outs),
        scratch_shapes=buffers(acts) + buffers(outs) + list(scratch) + [pltpu.SemaphoreType.DMA((COPIES,))],
        compiler_params=params(),
        cost_estimate=cost(flops, 2e7),
        name=name,
    )(*smem, *weights, *rows, *acts)


def attention_forward(layer, which, weights, vecs, bqkv, *acts):
    outs = [
        shape((LEN, D), BF),
        shape((LEN, QW), BF),
        shape((LEN, HALF), BF),
        shape((LEN, HALF), F32),
        shape((LEN, D), BF),
    ]
    if layer:
        outs.append(shape((LEN, D), BF))
    scratch = [pltpu.VMEM((D, QW), BF), pltpu.VMEM((HALF, D), BF), pltpu.SemaphoreType.DMA((2,))]
    kernel = functools.partial(attention_forward_kernel, layer)
    return run_kernel(kernel, "attention_forward", (which,), weights, (vecs, bqkv), acts, outs, scratch, 1.2e10)


def gelu_parts(u):
    slope = math.sqrt(2.0 / math.pi)
    square = u * u
    half = 0.5 + 0.5 * jnp.tanh(u * (slope + (slope * 0.044715) * square))
    value = u * half
    return value, half + (value - value * half) * (2.0 * slope + (6.0 * slope * 0.044715) * square)


def feed_forward_kernel(layer, *refs):
    both = layer == 1
    which_ref, own, fc_pieces, proj_pieces, refs = refs[0], refs[1:3], refs[3:7], refs[7:11], refs[11:]
    vec_ref, bfc_ref, refs = refs[0], refs[1], refs[2:]
    count = 4 if both else 3
    ins, refs = refs[:count], refs[count:]
    outs, refs = refs[: 6 if both else 5], refs[6 if both else 5 :]
    held, refs = refs[:count], refs[count:]
    (h_ref, c_ref, g_ref, part_ref, slope_ref), refs = refs[:5], refs[5:]
    if both:
        dc_ref, refs = refs[0], refs[1:]
    wfc_ref, wproj_ref, sems, copy_sems = refs
    base = 8 * layer
    copies = Copies(copy_sems)
    blocks = row_slices(BR)
    arriving = [[copies.begin(part_of(src, rows), part_of(dst, rows)) for src, dst in zip(ins, held)] for rows in blocks]
    start_fetch(which_ref, own[0:1], fc_pieces, ((wfc_ref, FC_BLOCKS),), sems.at[pl.ds(0, 1)])
    start_fetch(which_ref, own[1:2], proj_pieces, ((wproj_ref, PROJ_BLOCKS),), sems.at[pl.ds(1, 1)])

    for number, rows in enumerate(blocks):
        for copy in arriving[number]:
            copy.wait()
        h = held[0][rows, :].astype(F32) + (
            held[1][rows, :].astype(F32) + held[2][rows, :].astype(F32) + vec_ref[base + 3 : base + 4, :]
        )
        h_ref[rows, :] = h
        copies.leave(part_of(h_ref, rows), part_of(outs[0], rows))
        unit, _ = normalize(h)
        c = (unit * vec_ref[base + 1 : base + 2, :] + vec_ref[base + 4 : base + 5, :]).astype(BF)
        c_ref[rows, :] = c
        copies.leave(part_of(c_ref, rows), part_of(outs[1], rows))
        if number == 0:
            end_fetch(own[0], wfc_ref, sems.at[0])
            end_fetch(own[1], wproj_ref, sems.at[1])

        width = 512
        starts = list(range(0, FW, width))

        def up(start):
            cols = slice(start, start + width)
            u = mm(c, wfc_ref[:, cols]) + bfc_ref[layer : layer + 1, cols]
            return u, (mm_nt(held[3][rows, :], wproj_ref[cols, :]) if both else None)

        part, dc = None, None
        ahead = up(starts[0])
        for position, start in enumerate(starts):
            cols = slice(start, start + width)
            u, dg = ahead
            if position + 1 < len(starts):
                ahead = up(starts[position + 1])
            g, slope = gelu_parts(u)
            g = g.astype(BF)
            g_ref[rows, cols] = g
            more = mm(g, wproj_ref[cols, :])
            part = more if part is None else part + more
            if both:
                du = (dg * slope).astype(BF)
                slope_ref[rows, cols] = du
                more = mm_nt(du, wfc_ref[:, cols])
                dc = more if dc is None else dc + more
            else:
                slope_ref[rows, cols] = slope.astype(BF)
        copies.leave(part_of(g_ref, rows), part_of(outs[2], rows))
        copies.leave(part_of(slope_ref, rows), part_of(outs[4], rows))
        if both:
            dc_ref[rows, :] = dc.astype(BF)
            copies.leave(part_of(dc_ref, rows), part_of(outs[5], rows))
        part_ref[rows, :] = part.astype(BF)
        copies.leave(part_of(part_ref, rows), part_of(outs[3], rows))
    copies.finish()


def whole_spec(dims):
    return pl.BlockSpec(dims, lambda *i: (0,) * len(dims))


def feed_weights():
    return [pltpu.VMEM((D, FW), BF), pltpu.VMEM((FW, D), BF), pltpu.SemaphoreType.DMA((2,))]


def feed_forward(layer, which, weights, vecs, bfc, *acts):
    outs = [shape((LEN, D), F32), shape((LEN, D), BF), shape((LEN, FW), BF), shape((LEN, D), BF), shape((LEN, FW), BF)]
    if layer == 1:
        outs.append(shape((LEN, D), BF))
    kernel = functools.partial(feed_forward_kernel, layer)
    return run_kernel(kernel, "feed_forward", (which,), weights, (vecs, bfc), acts, outs, feed_weights(), 1e10)


def norm_back(vec, da, unit, scale, sums_ref):
    sums_ref[0:1, :] += column_sum(da * unit)
    sums_ref[1:2, :] += column_sum(da)
    return normalize_back(da, unit, scale, vec)


def feed_back_kernel(*refs):
    which_ref, own, fc_pieces, proj_pieces, refs = refs[0], refs[1:3], refs[3:7], refs[7:11], refs[11:]
    vec_ref, ins, outs, held, refs = refs[0], refs[1:6], refs[6:10], refs[10:15], refs[15:]
    (dm_ref, du_ref, dc_ref, sums_ref), (wfc_ref, wproj_ref, sems, copy_sems) = refs[:4], refs[4:]
    dh_ref, own_ref, recv_ref, x_ref, slope_ref = held
    copies = Copies(copy_sems)
    blocks = row_slices(BR)
    arriving = []
    for rows in blocks:
        arriving.append([copies.begin(part_of(src, rows), part_of(dst, rows)) for src, dst in zip(ins, held)])
        if len(arriving) == 1:
            start_fetch(which_ref, own[1:2], proj_pieces, ((wproj_ref, PROJ_BLOCKS),), sems.at[pl.ds(1, 1)])
            start_fetch(which_ref, own[0:1], fc_pieces, ((wfc_ref, FC_BLOCKS),), sems.at[pl.ds(0, 1)])
    sums_ref[...] = jnp.zeros_like(sums_ref)

    for number, rows in enumerate(blocks):
        for copy in arriving[number]:
            copy.wait()
        unit, scale = normalize(x_ref[rows, :].astype(F32))
        da = own_ref[rows, :].astype(F32) + recv_ref[rows, :].astype(F32)
        dm = (dh_ref[rows, :] + norm_back(vec_ref[8:9, :], da, unit, scale, sums_ref)).astype(BF)
        dm_ref[rows, :] = dm
        copies.leave(part_of(dm_ref, rows), part_of(outs[0], rows))
        if number == 0:
            end_fetch(own[1], wproj_ref, sems.at[1])
            end_fetch(own[0], wfc_ref, sems.at[0])
        width = 512
        starts = list(range(0, FW, width))

        def up(start):
            return mm_nt(dm, wproj_ref[start : start + width, :])

        dc = None
        ahead = up(starts[0])
        for position, start in enumerate(starts):
            cols = slice(start, start + width)
            dg = ahead
            if position + 1 < len(starts):
                ahead = up(starts[position + 1])
            du = (dg * slope_ref[rows, cols].astype(F32)).astype(BF)
            du_ref[rows, cols] = du
            more = mm_nt(du, wfc_ref[:, cols])
            dc = more if dc is None else dc + more
        copies.leave(part_of(du_ref, rows), part_of(outs[1], rows))
        dc_ref[rows, :] = dc.astype(BF)
        copies.leave(part_of(dc_ref, rows), part_of(outs[2], rows))
    copies.leave(sums_ref, outs[3])
    copies.finish()


def feed_back(which, weights, vecs, *acts):
    outs = [shape((LEN, D), BF), shape((LEN, FW), BF), shape((LEN, D), BF), shape((8, D), F32)]
    return run_kernel(feed_back_kernel, "feed_back", (which,), weights, (vecs,), acts, outs, feed_weights(), 5e9)


def input_back_kernel(vec_ref, *refs):
    ins, outs, held, (dx_ref, sums_ref, copy_sems) = refs[:4], refs[4:6], refs[6:10], refs[10:]
    dh_ref, own_ref, recv_ref, x_ref = held
    copies = Copies(copy_sems)
    blocks = row_slices(BT)
    arriving = [[copies.begin(part_of(src, rows), part_of(dst, rows)) for src, dst in zip(ins, held)] for rows in blocks]
    sums_ref[...] = jnp.zeros_like(sums_ref)
    for number, rows in enumerate(blocks):
        for copy in arriving[number]:
            copy.wait()
        unit, scale = normalize(x_ref[rows, :].astype(F32))
        da = own_ref[rows, :].astype(F32) + recv_ref[rows, :].astype(F32)
        dx_ref[rows, :] = (dh_ref[rows, :] + norm_back(vec_ref[0:1, :], da, unit, scale, sums_ref)).astype(BF)
        copies.leave(part_of(dx_ref, rows), part_of(outs[0], rows))
    copies.leave(sums_ref, outs[1])
    copies.finish()


def input_back(vecs, *acts):
    outs = [shape((LEN, D), BF), shape((8, D), F32)]
    return run_kernel(input_back_kernel, "input_back", (), (), (vecs,), acts, outs, (), 1e7)


def in_three(values, spots):
    high = values.astype(BF)
    rest = values - high.astype(F32)
    middle = rest.astype(BF)
    low = (rest - middle.astype(F32)).astype(BF)
    return jnp.where(spots == 0, high, jnp.where(spots == 1, middle, jnp.where(spots == 2, low, jnp.zeros_like(low))))


def attention_back_kernel(layer, *refs):
    which_ref, own, pieces, refs = refs[0], refs[1:3], refs[3:7], refs[7:]
    vec_ref, ins, outs, held, refs = refs[0], refs[1:8], refs[8:14], refs[14:21], refs[21:]
    (dh_ref, dz_ref, dqkv_ref, da_ref, sums_ref, bias_ref), refs = refs[:6], refs[6:]
    do_ref, dk_ref, dv_ref, wqkv_ref, wout_ref, sems, copy_sems = refs
    dm_ref, own_ref, recv_ref, h_ref, qkv_ref, o_ref, lse_ref = held
    copies = Copies(copy_sems)
    blocks = row_slices(BT)
    arriving = []
    for rows in blocks:
        arriving.append([copies.begin(part_of(src, rows), part_of(dst, rows)) for src, dst in zip(ins[:4], held[:4])])
        if len(arriving) == 1:
            start_fetch(which_ref, own, pieces, ((wqkv_ref, QKV_BLOCKS), (wout_ref, OUT_BLOCKS)), sems)
    later = [copies.begin(src, dst) for src, dst in zip(ins[4:], held[4:])]
    gain = vec_ref[8 * layer + 1 : 8 * layer + 2, :]
    sums_ref[...] = jnp.zeros_like(sums_ref)
    bias_ref[...] = jnp.zeros_like(bias_ref)

    for number, rows in enumerate(blocks):
        for copy in arriving[number]:
            copy.wait()
        unit, scale = normalize(h_ref[rows, :])
        dc = own_ref[rows, :].astype(F32) + recv_ref[rows, :].astype(F32)
        dm = dm_ref[rows, :].astype(F32)
        dh = dm + norm_back(gain, dc, unit, scale, sums_ref)
        dh_ref[rows, :] = dh
        copies.leave(part_of(dh_ref, rows), part_of(outs[0], rows))
        dz = dh.astype(BF)
        dz_ref[rows, :] = dz
        copies.leave(part_of(dz_ref, rows), part_of(outs[1], rows))
        sums_ref[2:3, :] += column_sum(dz.astype(F32))
        sums_ref[3:4, :] += column_sum(dm)
        if number == 0:
            end_fetch(own[1], wout_ref, sems.at[1])
        do_ref[rows, :] = mm_nt(dz, wout_ref[...]).astype(BF)
    copies.leave(sums_ref, outs[4])
    for copy in later:
        copy.wait()

    def attend(group, carry):
        low = lower_lanes(BK)
        low_all = lower_lanes(LEN)
        spots = lax.broadcasted_iota(jnp.int32, (BK, 128), 1) % HS
        ones = jnp.where(lax.broadcasted_iota(jnp.int32, (LEN, 128), 1) % HS < 3, 1.0, 0.0).astype(BF)
        keep_diag = lax.broadcasted_iota(jnp.int32, (BK, BK), 0) <= lax.broadcasted_iota(jnp.int32, (BK, BK), 1)
        nothing = jnp.zeros((BK, 128), BF)
        key = qkv_ref[:, lane_group(3 * group + 1)]
        value = qkv_ref[:, lane_group(3 * group + 2)]
        blank = jnp.zeros_like(key)
        keys_with = (jnp.where(low_all, key, ones), jnp.where(low_all, ones, key))
        values_with = (jnp.where(low_all, value, ones), jnp.where(low_all, ones, value))
        keys_one = (jnp.where(low_all, key, blank), jnp.where(low_all, blank, key))

        def prepare(i):
            mine = slice(i * BK, (i + 1) * BK)
            query = qkv_ref[mine, lane_group(3 * group)]
            do = do_ref[mine, lane_group(group)]
            lse = in_three(-pltpu.roll(lse_ref[mine, lane_group(group)], HS, 1), spots)
            inner = do.astype(F32) * o_ref[mine, lane_group(group)].astype(F32)
            t_low = jnp.sum(jnp.where(low, inner, 0.0), axis=1, keepdims=True)
            t_high = jnp.sum(jnp.where(low, 0.0, inner), axis=1, keepdims=True)
            t = in_three(-jnp.where(low, t_high, t_low), spots)
            return (
                (jnp.where(low, query, lse), jnp.where(low, lse, query)),
                (jnp.where(low, do, t), jnp.where(low, t, do)),
                (jnp.where(low, query, nothing), jnp.where(low, nothing, query)),
                (jnp.where(low, do, nothing), jnp.where(low, nothing, do)),
            )

        def products(i, head, prepared):
            past, here = i * BK, (i + 1) * BK
            query_with, do_with = prepared[0][head], prepared[1][head]
            diag = jnp.where(keep_diag, mm_nt(keys_with[head][past:here], query_with), MASKED_SCORE)
            out = [(diag, mm_nt(values_with[head][past:here], do_with))]
            if i:
                out.append((mm_nt(keys_with[head][:past], query_with), mm_nt(values_with[head][:past], do_with)))
            return out

        units = [(i, head) for i in range(LEN // BK) for head in range(2)]
        prepared = prepare(0)
        ahead = products(0, 0, prepared)
        dq = None
        for number, (i, head) in enumerate(units):
            past, here = i * BK, (i + 1) * BK
            now, now_prepared = ahead, prepared
            if number + 1 < len(units):
                if head == 1:
                    prepared = prepare(i + 1)
                ahead = products(*units[number + 1], prepared)
            query_one, do_one = now_prepared[2][head], now_prepared[3][head]
            for rows, (score, inner) in zip((slice(past, here), slice(0, past)), now):
                p = jnp.exp(score)
                ds = (p * inner).astype(BF)
                dv = mm(p.astype(BF), do_one)
                dk = mm(ds, query_one)
                part = mm_tn(ds, keys_one[head][rows])
                dq = part if dq is None else dq + part
                if head == 0 and rows.start == past:
                    dv_ref[rows, :] = dv
                    dk_ref[rows, :] = dk
                else:
                    dv_ref[rows, :] += dv
                    dk_ref[rows, :] += dk
            if head == 1:
                dqkv_ref[past:here, lane_group(3 * group)] = (dq * 0.125).astype(BF)
                dq = None
        for i in range(NB):
            mine = slice(i * BT, (i + 1) * BT)
            one, two, three = from_pairs(
                dqkv_ref[mine, lane_group(3 * group)].astype(F32), dk_ref[mine, :], dv_ref[mine, :]
            )
            dqkv_ref[mine, lane_group(3 * group)] = one.astype(BF)
            dqkv_ref[mine, lane_group(3 * group + 1)] = two.astype(BF)
            dqkv_ref[mine, lane_group(3 * group + 2)] = three.astype(BF)
        return carry

    lax.fori_loop(0, PAIRS, attend, 0)

    copies.leave(dqkv_ref, outs[2])
    end_fetch(own[0], wqkv_ref, sems.at[0])
    for rows in row_slices(512):
        da_ref[rows, :] = mm_nt(dqkv_ref[rows, :], wqkv_ref[...]).astype(BF)
        copies.leave(part_of(da_ref, rows), part_of(outs[3], rows))
        bias_ref[0:1, :] += column_sum(dqkv_ref[rows, :].astype(F32))
    copies.leave(bias_ref, outs[5])
    copies.finish()


def attention_back(layer, which, weights, vecs, *acts):
    outs = [
        shape((LEN, D), F32),
        shape((LEN, D), BF),
        shape((LEN, QW), BF),
        shape((LEN, D), BF),
        shape((8, D), F32),
        shape((8, QW), F32),
    ]
    scratch = [
        pltpu.VMEM((LEN, HALF), BF),
        pltpu.VMEM((LEN, 128), F32),
        pltpu.VMEM((LEN, 128), F32),
        pltpu.VMEM((D, QW), BF),
        pltpu.VMEM((HALF, D), BF),
        pltpu.SemaphoreType.DMA((2,)),
    ]
    kernel = functools.partial(attention_back_kernel, layer)
    return run_kernel(kernel, "attention_back", (which,), weights, (vecs,), acts, outs, scratch, 2.2e10)


def feed_grad_kernel(*refs):
    ins, outs, held, refs = refs[:4], refs[4:10], refs[10:14], refs[14:]
    grads, (square_ref, bias_ref, copy_sems) = refs[:4], refs[4:]
    copies = Copies(copy_sems)
    g_ref, dm_ref, c_ref, du_ref = held
    bias_ref[...] = jnp.zeros_like(bias_ref)
    halves = [pl.ds(0, D), pl.ds(D, D)]
    arriving = []
    for half in range(2):
        arriving.append(copies.begin(ins[0].at[:, halves[half]], g_ref.at[:, halves[half]]))
        if half == 0:
            arriving.append(copies.begin(ins[1], dm_ref))
        arriving.append(copies.begin(ins[3].at[:, halves[half]], du_ref.at[:, halves[half]]))
        if half == 0:
            arriving.append(copies.begin(ins[2], c_ref))
    total = None
    for number in range(4):
        for copy in (arriving[0:2], arriving[2:4], arriving[4:5], arriving[5:6])[number]:
            copy.wait()
        cols = slice(number // 2 * D, (number // 2 + 1) * D)
        if number % 2 == 0:
            grad = mm_tn(g_ref[:, cols], dm_ref[...])
        else:
            grad = mm_tn(c_ref[...], du_ref[:, cols])
            bias_ref[0:1, cols] = column_sum(du_ref[:, cols].astype(F32))
        grads[number][...] = grad.astype(BF)
        copies.leave(grads[number], outs[number])
        square = column_sum(grad * grad)
        total = square if total is None else total + square
    square_ref[...] = jnp.zeros_like(square_ref)
    square_ref[0:1, :] = total
    copies.leave(square_ref, outs[4])
    copies.leave(bias_ref, outs[5])
    copies.finish()


def feed_grad(*acts):
    outs = [shape((D, D), BF)] * 4 + [shape((8, D), F32), shape((8, FW), F32)]
    return run_kernel(feed_grad_kernel, "feed_grad", (), (), (), acts, outs, (), 1e10)


def attention_grad_kernel(*refs):
    ins, outs, held, refs = refs[:4], refs[4:7], refs[7:11], refs[11:]
    targets, square_ref, copy_sems = refs[:2], refs[2], refs[3]
    copies = Copies(copy_sems)
    o_ref, dz_ref, a_ref, dqkv_ref = held
    arriving = [copies.begin(ins[number], held[number]) for number in (2, 3, 0, 1)]
    square_ref[...] = jnp.zeros_like(square_ref)
    for part, target in enumerate(targets):
        half = slice(part * HALF, (part + 1) * HALF)

        def place(grad, rows, cols):
            square_ref[0:1, 0:HALF] += column_sum(grad * grad)
            target[rows, cols] = grad.astype(BF)

        if part == 0:
            arriving[0].wait()
            arriving[1].wait()
        top = mm_tn(a_ref[:, half], dqkv_ref[...])
        if part == 0:
            arriving[2].wait()
            arriving[3].wait()
        out = mm_tn(o_ref[...], dz_ref[:, half])
        place(top[:, 0:HALF], slice(0, HALF), slice(0, HALF))
        place(top[:, HALF:D], slice(0, HALF), slice(HALF, D))
        for start, grad in ((HALF, top[:, D:]), (HALF + SIDE, out)):
            place(grad[:SIDE], slice(start, start + SIDE), slice(0, HALF))
            place(grad[SIDE:], slice(start, start + SIDE), slice(HALF, D))
        copies.leave(target, outs[part])
    copies.leave(square_ref, outs[2])
    copies.finish()


def attention_grad(*acts):
    outs = [shape((D, D), BF), shape((D, D), BF), shape((8, D), F32)]
    return run_kernel(attention_grad_kernel, "attention_grad", (), (), (), acts, outs, (), 5e9)


def pack_small_kernel(core_ref, *refs):
    ins, (small_ref, square_ref) = refs[:12], refs[12:]
    small_ref[...] = jnp.zeros_like(small_ref)
    lower = core_ref[0] == 0
    total = jnp.zeros((8, D), F32)
    for layer in range(2):
        bias_qkv, bias_fc, first, second, squares_feed, squares_attention = (ref[...] for ref in ins[6 * layer : 6 * layer + 6])

        def side(values):
            return jnp.where(lower, values[:, :HALF], values[:, HALF:])

        small_ref[layer, 0:1, :] = bias_fc[0:1, 0:D]
        small_ref[layer, 1:2, :] = bias_fc[0:1, D:]
        small_ref[layer, 2:3, :] = bias_qkv[0:1, 0:D]
        small_ref[layer, 3:4, 0:HALF] = bias_qkv[0:1, D:]
        rows = (first[0:1], second[0:1], first[1:2], second[2:3], second[1:2], second[3:4])
        for number, row in enumerate(rows):
            line, right = divmod(number + 1, 2)
            small_ref[layer, 3 + line : 4 + line, right * HALF : (right + 1) * HALF] = side(row)
        total = total + squares_feed + squares_attention
        total = total + small_ref[layer, 0:8, :] * small_ref[layer, 0:8, :]
    square_ref[...] = jnp.broadcast_to(jnp.sum(total, keepdims=True), (8, 128))


def pack_small(core, *parts):
    vmem = pl.BlockSpec(memory_space=pltpu.VMEM)
    return pl.pallas_call(
        pack_small_kernel,
        in_specs=[pl.BlockSpec(memory_space=pltpu.SMEM)] + [vmem] * 12,
        out_specs=[vmem] * 2,
        out_shape=[shape((2, 16, D), F32), shape((8, 128), F32)],
        compiler_params=params(SMALL_VMEM_BYTES),
        cost_estimate=cost(1e5, 1e5),
        name="pack_small",
    )(core, *parts)


def unpack_small(rows):
    tail = rows[3:7].reshape(8, HALF)
    bias = jnp.concatenate([rows[2], tail[0]])
    return bias, rows[0:2].reshape(FW), tail[1:3], tail[3:7]


def weigh_kernel(rows, roles_ref, mine_ref, across_ref, above_ref, *refs):
    sources, refs = refs[:8], refs[8:]
    if len(refs) == 6:
        (small_ref, other_ref, keep_ref, aside_ref, held_ref, sems) = refs
    else:
        (other_ref, keep_ref, aside_ref, held_ref, sems) = refs
        small_ref = None
    mine, home = roles_ref[0], roles_ref[1]

    def bring(slot, one, two):
        for number, source in enumerate((one, two)):
            pltpu.make_async_copy(source.at[rows], held_ref.at[2 * slot + number], sems.at[slot]).start()

    for layer in range(2):
        first, first_there, second, second_there = sources[4 * layer : 4 * layer + 4]

        @pl.when(mine == layer)
        def _(second=second, second_there=second_there):
            bring(2, second, second_there)

        for role in range(2):

            @pl.when((home == 1) & ((mine == layer) == (role == 1)))
            def _(role=role, first=first, first_there=first_there):
                bring(role, first, first_there)

    count = held_ref.shape[1]

    def total(slot, weight_ref):
        both = held_ref.at[pl.ds(2 * slot, 2)]
        pltpu.make_async_copy(both, both, sems.at[slot]).wait()
        return mine_ref[0:1, 0:1] * held_ref[2 * slot].astype(F32) + weight_ref[0:1, 0:1] * held_ref[
            2 * slot + 1
        ].astype(F32)

    @pl.when(home == 1)
    def _():
        for slot, target in ((0, other_ref), (1, keep_ref)):
            target[0:count, :] = total(slot, across_ref).astype(target.dtype)
            if small_ref is not None:
                target[count:, :] = jnp.where(mine == slot, small_ref[1], small_ref[0]).astype(target.dtype)
        aside_ref[0:count, :] = total(2, above_ref).astype(BF)
        if small_ref is not None:
            aside_ref[count:, :] = jnp.zeros((16, D), BF)

    @pl.when(home == 0)
    def _():
        other_ref[0:count, :] = total(2, above_ref).astype(BF)
        if small_ref is not None:
            other_ref[count:, :] = jnp.zeros((16, D), BF)


def weigh(rows, roles, weights, layers, small=None):
    count = rows.stop - rows.start
    tall = count + (0 if small is None else 16)
    vmem, smem, hbm = (pl.BlockSpec(memory_space=kind) for kind in (pltpu.VMEM, pltpu.SMEM, pl.ANY))
    return pl.pallas_call(
        functools.partial(weigh_kernel, pl.ds(rows.start, count)),
        out_shape=[shape((tall, D), BF), shape((tall, D), F32), shape((tall, D), BF)],
        in_specs=[smem] + [vmem] * 3 + [hbm] * 8 + ([] if small is None else [vmem]),
        out_specs=[vmem] * 3,
        scratch_shapes=[pltpu.VMEM((6, count, D), BF), pltpu.SemaphoreType.DMA((3,))],
        compiler_params=params(SMALL_VMEM_BYTES),
        cost_estimate=cost(1e7, 1e7),
        name="weigh",
    )(roles, *weights, *layers[0], *layers[1], *(() if small is None else (small,)))


def noise_rows():
    sizes = (D * QW, QW, HALF * D, D * FW, FW, FW * D, 2 * HALF, 4 * HALF)
    starts = [0]
    for size in sizes:
        starts.append(starts[-1] + size // 128)
    return starts


NOISE_ROWS = noise_rows()


def bring_noise(noise_ref, begin, raw_ref, sem):
    copy = pltpu.make_async_copy(noise_ref.at[pl.ds(begin, raw_ref.shape[0])], raw_ref, sem)
    copy.start()
    return copy


def put_noised(target, block, rows, col, wide_ref, first, denominator):
    scale = NOISE_MULT * CLIP_FRACTION * math.sqrt(LEN * FF * D)
    per = target.shape[1] // 128
    tall = rows.stop - rows.start
    for tile in range(block.shape[1] // 128):
        place = col // 128 + tile
        noise = wide_ref[pl.ds(first + per * rows.start + place, tall, stride=per), :]
        value = block[:, tile * 128 : (tile + 1) * 128].astype(F32)
        target[rows, place * 128 : (place + 1) * 128] = (value + scale * noise) / denominator


def finish_feed_kernel(columns, denominator, home_ref, *refs):
    own, swapped = refs[:2], refs[2:4]
    noise_ref, grad_ref, raw_ref, wide_ref, sem = refs[4:]
    first = NOISE_ROWS[3 if columns else 5]
    begin = first // 16 * 16
    bring_noise(noise_ref, begin, raw_ref, sem).wait()
    wide_ref[...] = raw_ref[...].astype(F32)
    step = D // 2

    def run(parts):
        for number, part in enumerate(parts):
            for index in range(2):
                row, col = (index * step, number * D) if columns else (number * D + index * step, 0)
                block = part[index][0:step, :]
                put_noised(grad_ref, block, slice(row, row + step), col, wide_ref, first - begin, denominator)

    @pl.when(home_ref[0] == 1)
    def _():
        run((own, swapped))

    @pl.when(home_ref[0] == 0)
    def _():
        run((swapped, own))


def finish_attention_kernel(denominator, home_ref, *refs):
    own, swapped = refs[0:2], refs[2:4]
    noise_ref, qkv_ref, out_ref, raw_ref, wide_ref, sem = refs[4:]
    bring_noise(noise_ref, 0, raw_ref, sem).wait()
    wide_ref[...] = raw_ref[...].astype(F32)

    def run(parts):
        for number, (one, two) in enumerate(parts):
            start = number * HALF
            put_noised(qkv_ref, one[...], slice(start, start + HALF), 0, wide_ref, NOISE_ROWS[0], denominator)
            for index in range(2):
                cols = slice(index * HALF, (index + 1) * HALF)
                rows = slice(start + index * SIDE, start + (index + 1) * SIDE)
                put_noised(qkv_ref, two[0:SIDE, cols], rows, D, wide_ref, NOISE_ROWS[0], denominator)
                rows = slice(index * SIDE, (index + 1) * SIDE)
                put_noised(out_ref, two[SIDE : 2 * SIDE, cols], rows, start, wide_ref, NOISE_ROWS[2], denominator)

    @pl.when(home_ref[0] == 1)
    def _():
        run((own, swapped))

    @pl.when(home_ref[0] == 0)
    def _():
        run((swapped, own))


def finish(kernel, denominator, home, own, swapped, noise, numbers, shapes, name):
    smem, vmem, hbm = (pl.BlockSpec(memory_space=kind) for kind in (pltpu.SMEM, pltpu.VMEM, pl.ANY))
    begin, end = NOISE_ROWS[numbers[0]] // 16 * 16, -(-NOISE_ROWS[numbers[-1] + 1] // 16) * 16
    return pl.pallas_call(
        functools.partial(kernel, denominator),
        out_shape=[shape(dims, F32) for dims in shapes],
        in_specs=[smem] + [vmem] * (2 * len(own)) + [hbm],
        out_specs=[vmem] * len(shapes),
        scratch_shapes=[
            pltpu.VMEM((end - begin, 128), BF),
            pltpu.VMEM((end - begin, 128), F32),
            pltpu.SemaphoreType.DMA,
        ],
        compiler_params=params(SMALL_VMEM_BYTES),
        cost_estimate=cost(1e7, 1.6e7),
        name=name,
    )(home, *own, *swapped, noise)


def send(values, route):
    sections, ranks = lax.axis_size("section"), lax.axis_size("dp")
    pairs = []
    for section in range(sections):
        for rank in range(ranks):
            target = route(section, rank // 2, rank % 2)
            if target is not None:
                to_section, to_pair, to_core = target
                pairs.append((section * ranks + rank, to_section * ranks + to_pair * 2 + to_core))
    return lax.ppermute(values, ("section", "dp"), pairs)


def swap_cores(values):
    return send(values, lambda s, z, c: (s, z, 1 - c))


def is_home(s, c):
    return s % 2 == c


def after(values, *others):
    return lax.optimization_barrier((values, *others))[0]


def local(
    inputs,
    cotangent,
    included,
    qkv_weight,
    qkv_bias,
    out_weight,
    fc_weight,
    fc_bias,
    proj_weight,
    norm_gains,
    shifts,
    noise,
):
    clip_norm = CLIP_FRACTION * math.sqrt(LEN * FF * D)
    section = lax.axis_index("section")
    rank = lax.axis_index("dp")
    ranks = lax.axis_size("dp")
    row, half = section // 2, section % 2
    place, core = rank // 2, rank % 2
    home = half == core
    on_top = row == 0
    flip = home.astype(jnp.int32).reshape(1)
    denominator = SAMPLE_RATE * inputs.shape[0] * ranks

    side = place % 2

    def piece_of(weight, number):
        tall = weight.shape[0] // 2
        if number is None:
            return lax.dynamic_slice_in_dim(weight, side * tall, tall, 0)
        return weight[number * tall : (number + 1) * tall]

    def attention_piece(number):
        qkv = piece_of(qkv_weight, number)
        tail = jnp.concatenate([qkv[:SIDE, D:], qkv[SIDE:, D:]], axis=1)
        return jnp.concatenate([qkv[:, :D], tail, piece_of(out_weight, number)])

    fc_piece = piece_of(fc_weight, None)
    fc_piece = jnp.concatenate([fc_piece[:, :D], fc_piece[:, D:]])

    def near(piece):
        return send(piece, lambda s, z, c: (s ^ 2, z, c) if is_home(s, c) else (s ^ 1, z, 1 - c))

    def far(one, two):
        far_one = send(one, lambda s, z, c: (s ^ 1, z, c) if is_home(s, c) else None)
        return far_one, send(two, lambda s, z, c: None if is_home(s, c) else (s ^ 2, z, c))

    def next_plane(one):
        return send(one, lambda s, z, c: (s, z ^ 1, c))

    fc_one = near(fc_piece)
    *parts, fc_one = lax.optimization_barrier((attention_piece(0), attention_piece(1), fc_one))
    attention_pieces = tuple(near(part) for part in parts)
    fc_two = next_plane(fc_one)
    proj_piece, *attention_pieces = lax.optimization_barrier((piece_of(proj_weight, None), *attention_pieces))
    proj_one = near(proj_piece)
    attention_far = far(*attention_pieces)
    later, fc_two = lax.optimization_barrier((proj_one, fc_two))
    proj_two = next_plane(later)
    fc_again, *attention_far = lax.optimization_barrier((fc_one, *attention_far))
    fc_far = far(fc_again, fc_two)
    proj_pieces = (proj_one, proj_two, *far(proj_one, proj_two))
    attention_pieces = (*attention_pieces, *attention_far)
    attention_weights = (qkv_weight, out_weight, *attention_pieces)

    def which_of(layer):
        kind = jnp.where(row == layer, jnp.where(home, 0, 1), jnp.where(home, 1, 2))
        return [jnp.stack([kind, first]).astype(jnp.int32) for first in (jnp.zeros_like(side), side)]

    which_attention, which_feed = zip(which_of(0), which_of(1))

    def own_sequence(values):
        mine = lax.dynamic_index_in_dim(values, half, 0, keepdims=False)
        theirs = swap_cores(mine)
        return jnp.where(core == row, mine, theirs)

    small = jnp.concatenate([qkv_bias, fc_bias, norm_gains.reshape(-1), shifts.reshape(-1)]).reshape(1, -1)
    others = [send(small, lambda s, z, c, bits=bits: (s ^ bits, z, c)) for bits in (1, 2, 3)]
    x0 = own_sequence(inputs)
    cot = own_sequence(cotangent)
    drawn = own_sequence(jnp.broadcast_to(included.astype(F32)[:, None, None], (2, 8, 128)))[0, 0]
    small_all = jnp.concatenate([small] + others, axis=0)
    small_all = jnp.where(half == 0, small_all, jnp.concatenate([small_all[i : i + 1] for i in (1, 0, 3, 2)]))
    small_all = jnp.where(on_top, small_all, jnp.concatenate([small_all[2:], small_all[:2]]))
    small_all = small_all.reshape(2, 2, -1)
    bias = jnp.where(core == 0, small_all[:, 0], small_all[:, 1])
    bqkv, bfc = bias[:, :QW], bias[:, QW : QW + FW]
    vecs = small_all[:, :, QW + FW :].reshape(2, 2, 6, HALF).transpose(0, 2, 1, 3).reshape(2, 6, D)
    vecs = jnp.pad(vecs, ((0, 0), (0, 2), (0, 0))).reshape(16, D)

    shapes = ((D, QW), (QW,), (HALF, D), (D, FW), (FW,), (FW, D), (2, HALF), (4, HALF))
    a0, qkv0, o0, lse0, part = attention_forward(0, which_attention[0], attention_weights, vecs, bqkv, x0)
    part, *fc_far = lax.optimization_barrier((part, *fc_far))
    feed_weights_all = (fc_weight, proj_weight, fc_one, fc_two, *fc_far, *proj_pieces)
    part_theirs = swap_cores(part)
    h0, c0, g0, part_two, slope0 = feed_forward(
        0, which_feed[0], feed_weights_all, vecs, bfc, x0, part, part_theirs
    )
    a1, qkv1, o1, lse1, part, x1 = attention_forward(
        1, which_attention[1], attention_weights, vecs, bqkv, h0, part_two, swap_cores(part_two)
    )
    h1, c1, g1, part_two, du1, dc = feed_forward(
        1, which_feed[1], feed_weights_all, vecs, bfc, x1, part, swap_cores(part), cot
    )
    dc_theirs = swap_cores(dc)
    y1 = (h1 + (part_two.astype(F32) + swap_cores(part_two).astype(F32)) + vecs[13:14]).astype(BF)

    def spread(block_for):
        received = []
        for step in range(2):
            block = block_for(2 * core + (step ^ half))
            received.append(send(block, lambda s, z, c, step=step: (2 * c + (step ^ (s % 2)), z, s // 2)))
        return received

    both_out = jnp.concatenate([x1, y1], axis=1)
    def over_x(values):
        return send(values, lambda s, z, c: None if is_home(s, c) else (s ^ 1, z, c))

    def over_y(layer, values):
        return send(values, lambda s, z, c: None if s // 2 == layer else (s ^ 2, z, c))

    *grads1, squares_feed1, bias_fc1 = feed_grad(g1, cot, c1, du1)
    dc, dc_theirs, *grads1 = lax.optimization_barrier((dc, dc_theirs, *grads1))
    proj_x1, fc_x1, proj_y1 = over_x(grads1[0]), over_x(grads1[1]), over_y(1, grads1[2])
    dh1, dz1, dqkv1, da, sums1, bias_qkv1 = attention_back(
        1, which_attention[1], attention_weights, vecs, cot, dc, dc_theirs, h1, qkv1, o1, lse1
    )
    da, proj_x1, fc_x1, proj_y1 = lax.optimization_barrier((da, proj_x1, fc_x1, proj_y1))
    da_theirs = swap_cores(da)
    fc_y1 = over_y(1, grads1[3])
    first1, second1, squares_attention1 = attention_grad(o1, dz1, a1, dqkv1)
    da, da_theirs, first1 = lax.optimization_barrier((da, da_theirs, first1))
    dm0, du0, dc, first_sums1 = feed_back(which_feed[0], feed_weights_all, vecs, dh1, da, da_theirs, x1, slope0)
    dc, fc_y1 = lax.optimization_barrier((dc, fc_y1))
    dc_theirs = swap_cores(dc)
    attention_x1 = over_x(first1)
    *grads0, squares_feed0, bias_fc0 = feed_grad(g0, dm0, c0, du0)
    dc, dc_theirs, attention_x1, *grads0 = lax.optimization_barrier((dc, dc_theirs, attention_x1, *grads0))
    proj_x0, fc_x0, proj_y0 = over_x(grads0[0]), over_x(grads0[1]), over_y(0, grads0[2])
    attention_y1 = over_y(1, second1)
    dh0, dz0, dqkv0, da, sums0, bias_qkv0 = attention_back(
        0, which_attention[0], attention_weights, vecs, dm0, dc, dc_theirs, h0, qkv0, o0, lse0
    )
    da, proj_x0, fc_x0, proj_y0, attention_y1 = lax.optimization_barrier((da, proj_x0, fc_x0, proj_y0, attention_y1))
    da_theirs = swap_cores(da)
    fc_y0 = over_y(0, grads0[3])
    first0, second0, squares_attention0 = attention_grad(o0, dz0, a0, dqkv0)
    dx0, first_sums0 = input_back(vecs, dh0, da, da_theirs, x0)
    small_pair, squares = pack_small(
        core.astype(jnp.int32).reshape(1),
        *(bias_qkv0, bias_fc0, first_sums0, sums0, squares_feed0, squares_attention0),
        *(bias_qkv1, bias_fc1, first_sums1, sums1, squares_feed1, squares_attention1),
    )
    small_there = send(small_pair, lambda s, z, c: None if is_home(s, c) else (s ^ 1, z, c))

    squares = squares + swap_cores(squares)
    factor = drawn * jnp.minimum(1.0, clip_norm / jnp.sqrt(squares))
    across = send(factor, lambda s, z, c: (s ^ 1, z, 1 - c) if is_home(s, c) else None)
    above = send(factor, lambda s, z, c: (s ^ 2, z, c))
    factor, across, above, fc_y0 = lax.optimization_barrier((factor, across, above, fc_y0))
    weights = (factor, across, above)
    roles = jnp.stack([row, home]).astype(jnp.int32)
    small_sum = jnp.where(home, factor[0, 0] * small_pair + across[0, 0] * small_there, 0.0)

    proj0, proj1 = (grads0[0], proj_x0, grads0[2], proj_y0), (grads1[0], proj_x1, grads1[2], proj_y1)
    fc0, fc1 = (grads0[1], fc_x0, grads0[3], fc_y0), (grads1[1], fc_x1, grads1[3], fc_y1)
    attention1 = (first1, attention_x1, second1, attention_y1)

    token_rows = LEN // lax.axis_size("section")

    def exchange_outputs(both_out, dx0):
        def block_for(number):
            columns = lax.dynamic_slice_in_dim(both_out, number * HALF, HALF, 1)
            rows = lax.dynamic_slice_in_dim(dx0, number * token_rows, token_rows, 0)
            return jnp.concatenate([columns, rows[:, :HALF], rows[:, HALF:]])

        return spread(block_for)

    places = ranks // 2
    middle = places // 2

    def to_middle(step):
        def route(s, z, c):
            if z == step:
                return (s, z + 1, c)
            if z == places - 1 - step:
                return (s, z - 1, c)
            return None

        return route

    def at_middle(s, z, c):
        return (s, places - 1 - z, c) if z in (middle - 1, middle) else None

    def from_middle(step):
        def route(s, z, c):
            if z == middle - 1 - step:
                return (s, z - 1, c)
            if z == middle + step:
                return (s, z + 1, c)
            return None

        return route

    def add(left, right):
        return (left.astype(F32) + right.astype(F32)).astype(BF)

    def weigh_stage(args):
        other, keep, aside = weigh(*args)
        arrived = send(other, lambda s, z, c: (s ^ 2, z, c) if is_home(s, c) else (s ^ 1, z, 1 - c))
        aside = send(aside, lambda s, z, c: (s, z, 1 - c) if is_home(s, c) else None)
        return keep, aside, arrived

    def weigh_end(held):
        keep, aside, arrived = held
        return (jnp.where(home, keep, aside.astype(F32)) + arrived.astype(F32)).astype(BF)

    def chain_stage(hop):
        def stage(held):
            total = add(*held) if len(held) == 2 else weigh_end(held)
            return total, send(total, hop)

        return stage

    def spread_stage(step):
        def stage(held):
            total, arrived = held
            if step == 0:
                total = add(total, arrived)
            else:
                takes = (place == middle - 1 - step) | (place == middle + step)
                total = jnp.where(takes, arrived, total)
            return total, send(total, from_middle(step))

        return stage

    def last_stage(held):
        total, arrived = held
        if middle > 1:
            takes = (place == 0) | (place == places - 1)
            total = jnp.where(takes, arrived, total)
        else:
            total = add(total, arrived)
        return total, swap_cores(total)

    hops = [to_middle(step) for step in range(middle - 1)] + [at_middle]
    stages = [weigh_stage] + [chain_stage(hop) for hop in hops]
    stages += [spread_stage(step) for step in range(middle - 1)] + [last_stage]

    chunk = D // 2

    noise_flat = noise.reshape(-1, 128)

    def small_noise(number, dims):
        first = NOISE_ROWS[number] * 128
        return noise[first : first + math.prod(dims)].reshape(dims).astype(F32)

    def finish_proj(one, two):
        return finish(
            functools.partial(finish_feed_kernel, False), denominator, flip, *zip(one, two), noise_flat, (5,), ((FW, D),), "finish_feed"
        )[0]

    def finish_fc(one, two):
        return finish(
            functools.partial(finish_feed_kernel, True), denominator, flip, *zip(one, two), noise_flat, (3,), ((D, FW),), "finish_feed"
        )[0]

    if middle == 2:
        edge = (place == 0) | (place == places - 1)

        def to_next(s, z, c):
            return (s, z ^ 1, c)

        count = 6
        begun, sums, lows, totals, ready = ({} for _ in range(5))
        outer, last = None, None

        def tie(*values):
            if last is None or last[1] not in last[0]:
                return values if len(values) > 1 else values[0]
            store, name = last
            *values, store[name] = lax.optimization_barrier((*values, store[name]))
            return values if len(values) > 1 else values[0]

        def begin(group, pair, *small):
            begun[group], begun[group, 1], begun[group, 2] = weigh_stage(
                (slice(0, D), roles, tie(*weights), pair, *small)
            )
            return begun, group

        last = begin(0, (proj0, proj1))
        last = begin(1, (fc0, fc1))
        first0, second0 = tie(first0, second0)
        attention_x0, attention_y0 = over_x(first0), over_y(0, second0)
        inners = {}
        for tick in range(count + 4):
            old_outer = outer
            if 0 <= tick - 3 < count:
                totals[tick - 3] = add(tie(lows.pop(tick - 3)), inners.pop(tick - 3))
                last = totals, tick - 3
            if tick < count and tick % 2 == 0:
                group = tick // 2
                total = weigh_end((tie(begun.pop(group)), begun.pop((group, 1)), begun.pop((group, 2))))
                sums[tick], sums[tick + 1] = total[:chunk], total[chunk:]
                last = sums, tick
            inward, outward = sums.get(tick), totals.get(tick - 3)
            if inward is not None and outward is not None:
                tall = [inward.shape[0], outward.shape[0]]
                padded = [jnp.pad(part, ((0, max(tall) - part.shape[0]), (0, 0))) for part in (inward, outward)]
                outer = send(jnp.where(edge, *padded), to_next)
                outer = (outer[: tall[0]], outer[: tall[1]])
            else:
                outer = (
                    None if inward is None else send(inward, to_middle(0)),
                    None if outward is None else send(outward, from_middle(0)),
                )
            if 0 <= tick - 1 < count:
                lows[tick - 1] = add(tie(sums.pop(tick - 1)), old_outer[0])
                last = lows, tick - 1
                inners[tick - 1] = send(lows[tick - 1], at_middle)
            if 0 <= tick - 4 < count:
                ready[tick - 4] = jnp.where(edge, old_outer[1], tie(totals.pop(tick - 4)))
                last = ready, tick - 4
            if tick == 2:
                attention_x0, attention_y0, small_sum = tie(attention_x0, attention_y0, small_sum)
                attention0 = (first0, attention_x0, second0, attention_y0)
                last = begin(2, (attention0, attention1), small_sum)
            if tick == 6:
                outputs = exchange_outputs(*tie(both_out, dx0))
                proj_grad = finish_proj(*((ready[i], swap_cores(ready[i])) for i in (0, 1)))
            if tick == 8:
                proj_grad = tie(proj_grad)
                fc_grad = finish_fc(*((ready[i], swap_cores(ready[i])) for i in (2, 3)))
            if tick == 9:
                fc_grad = tie(fc_grad)
        jobs = [None] * 4 + [(ready[i], swap_cores(ready[i])) for i in (4, 5)]
        small_own, small_swapped = jobs[5]
        stages = []
    else:
        attention0 = (first0, over_x(first0), second0, over_y(0, second0))
        jobs = []
        for pair in ((proj0, proj1), (fc0, fc1), (attention0, attention1)):
            jobs += [(slice(i * chunk, (i + 1) * chunk), roles, weights, pair) for i in range(2)]
        jobs[5] += (small_sum,)
        outputs = exchange_outputs(both_out, dx0)
    for tick in range(len(jobs) + len(stages) - 1 if stages else 0):
        for stage in reversed(range(len(stages))):
            index = tick - stage
            if 0 <= index < len(jobs):
                held = jobs[index]
                jobs[index] = stages[stage](held)
    if stages:
        proj_grad, fc_grad = finish_proj(*jobs[0:2]), finish_fc(*jobs[2:4])
        small_own, small_swapped = jobs[5]
    attention = jobs[4:]
    own, swapped = zip(*attention)
    qkv_grad, out_grad = finish(
        finish_attention_kernel, denominator, flip, own, swapped, noise_flat, (0, 2), ((D, QW), (HALF, D)), "finish_attention"
    )
    small_sum = jnp.where(home, small_own[chunk:], small_swapped[chunk:]).astype(F32)
    small_done = [
        (part + NOISE_MULT * clip_norm * small_noise(number, part.shape)) / denominator
        for part, number in zip(unpack_small(small_sum), (1, 4, 6, 7))
    ]
    first, second = outputs
    outputs = jnp.where(half == 0, jnp.stack([first, second]), jnp.stack([second, first]))
    layer_out = outputs[:, :LEN]
    input_grad = jnp.concatenate([outputs[:, LEN : LEN + token_rows], outputs[:, LEN + token_rows :]], axis=2)
    return (
        layer_out,
        input_grad,
        qkv_grad,
        small_done[0],
        out_grad,
        fc_grad,
        small_done[1],
        proj_grad,
        small_done[2],
        small_done[3],
    )


def solution(mesh):
    return jax.shard_map(
        local,
        mesh=mesh,
        in_specs=(
            P("dp", None, None),
            P("dp", None, None),
            P("dp"),
            P(None, "section"),
            P("section"),
            P("section", None),
            P(None, "section"),
            P("section"),
            P("section", None),
            P(None, "section"),
            P(None, "section"),
            P("section"),
        ),
        out_specs=(
            P("dp", None, "section"),
            P("dp", "section", None),
            P(None, "section"),
            P("section"),
            P("section", None),
            P(None, "section"),
            P("section"),
            P("section", None),
            P(None, "section"),
            P(None, "section"),
        ),
        check_vma=False,
    )
```

```python
import functools
import math

import jax
import jax.numpy as jnp
from jax import lax
from jax.experimental import pallas as pl
from jax.experimental.pallas import tpu as pltpu
from jax.sharding import PartitionSpec as P

D = 768
FF = 3072
HS = 64
LEN = 1024
HALF = D // 2
QW = 3 * HALF
FW = FF // 2
PAIRS = HALF // 128
BT = 256
NB = LEN // BT
BQ = 256
BR = 512
BK = 256

CLIP_FRACTION = 0.05
NOISE_MULT = 0.001
SAMPLE_RATE = 0.5
NORM_EPS = 1e-05
MASKED_SCORE = -1e30
VMEM_BYTES = 58 * 1024 * 1024
SMALL_VMEM_BYTES = 36 * 1024 * 1024

BF = jnp.bfloat16
F32 = jnp.float32


def mm(left, right):
    return lax.dot_general(left, right, (((1,), (0,)), ((), ())), preferred_element_type=F32)


def mm_nt(left, right):
    return lax.dot_general(left, right, (((1,), (1,)), ((), ())), preferred_element_type=F32)


def mm_tn(left, right):
    return lax.dot_general(left, right, (((0,), (0,)), ((), ())), preferred_element_type=F32)


def normalize(values):
    center = values - jnp.mean(values, axis=-1, keepdims=True)
    spread = jnp.mean(center * center, axis=-1, keepdims=True)
    scale = lax.rsqrt(spread + NORM_EPS)
    return center * scale, scale


def normalize_back(grad, unit, scale, gain):
    inner = grad * gain
    mean_inner = jnp.mean(inner, axis=-1, keepdims=True)
    mean_cross = jnp.mean(inner * unit, axis=-1, keepdims=True)
    return scale * (inner - mean_inner - unit * mean_cross)


def column_sum(values):
    return jnp.sum(values, axis=0, keepdims=True)


def block_rows(index):
    return pl.ds(pl.multiple_of(index * BT, BT), BT)


def lane_group(index, width=128):
    return pl.ds(pl.multiple_of(index * 128, 128), width)


def lower_lanes(rows=BT):
    return lax.broadcasted_iota(jnp.int32, (rows, 128), 1) < HS


def to_pairs(block, group):
    low = lower_lanes()
    start = 3 * 128 * group
    one, two, three = (block[:, start + 128 * i : start + 128 * (i + 1)] for i in range(3))
    query = jnp.where(low, one, two)
    key = pltpu.roll(jnp.where(low, three, one), HS, 1)
    value = jnp.where(low, two, three)
    return query, key, value


def from_pairs(query, key, value):
    low = lower_lanes()
    turned = pltpu.roll(key, HS, 1)
    return jnp.where(low, query, turned), jnp.where(low, value, query), jnp.where(low, turned, value)


class Copies:
    def __init__(self, sems):
        self.sems, self.used, self.left = sems, 0, []

    def begin(self, source, target):
        copy = pltpu.make_async_copy(source, target, self.sems.at[self.used])
        self.used += 1
        copy.start()
        return copy

    def leave(self, source, target):
        self.left.append(self.begin(source, target))

    def finish(self):
        for copy in self.left:
            copy.wait()


COPIES = 64


def row_slices(tall):
    return [slice(start, start + tall) for start in range(0, LEN, tall)]


def part_of(ref, rows):
    return ref.at[pl.ds(rows.start, rows.stop - rows.start)]


def start_fetch(which_ref, own, pieces, parts, sems, lower=1):
    @pl.when(which_ref[0] == 0)
    def _():
        for number, (target, _) in enumerate(parts):
            pltpu.make_async_copy(own[number], target, sems.at[number]).start()

    for kind in (1, 2):

        @pl.when(which_ref[0] == kind)
        def _(kind=kind):
            for order in range(2):
                piece = pieces[2 * kind - 2 + order]
                side = which_ref[lower] if order == 0 else 1 - which_ref[lower]
                for number, (target, blocks) in enumerate(parts):
                    base = pl.multiple_of(side * (target.shape[0] // 2), 64)
                    for (top, left), (tall, wide), (down, right) in blocks:
                        pltpu.make_async_copy(
                            piece.at[pl.ds(top, tall), pl.ds(left, wide)],
                            target.at[pl.ds(base + down, tall), pl.ds(right, wide)],
                            sems.at[number],
                        ).start()


def end_fetch(own, target, sem):
    pltpu.make_async_copy(own, target, sem).wait()


SIDE = HALF // 2
QKV_BLOCKS = (
    ((0, 0), (HALF, D), (0, 0)),
    ((HALF, 0), (SIDE, HALF), (0, D)),
    ((HALF, HALF), (SIDE, HALF), (SIDE, D)),
)
OUT_BLOCKS = (((HALF + SIDE, 0), (SIDE, D), (0, 0)),)
FC_BLOCKS = (((0, 0), (HALF, D), (0, 0)), ((HALF, 0), (HALF, D), (0, D)))
PROJ_BLOCKS = (((0, 0), (D, D), (0, 0)),)


def attention_forward_kernel(layer, *refs):
    which_ref, own, pieces, refs = refs[0], refs[1:3], refs[3:7], refs[7:]
    vec_ref, bqkv_ref, refs = refs[0], refs[1], refs[2:]
    first = layer == 0
    count = 1 if first else 3
    ins, refs = refs[:count], refs[count:]
    outs, refs = refs[: 5 if first else 6], refs[5 if first else 6 :]
    held, refs = refs[:count], refs[count:]
    (a_ref, qkv_ref, o_ref, lse_ref, part_ref), refs = refs[:5], refs[5:]
    if not first:
        x_ref, refs = refs[0], refs[1:]
    wqkv_ref, wout_ref, sems, copy_sems = refs
    copies = Copies(copy_sems)
    blocks = row_slices(BT)
    arriving = [[copies.begin(part_of(src, rows), part_of(dst, rows)) for src, dst in zip(ins, held)] for rows in blocks]
    start_fetch(which_ref, own, pieces, ((wqkv_ref, QKV_BLOCKS), (wout_ref, OUT_BLOCKS)), sems)

    for number, rows in enumerate(blocks):
        for copy in arriving[number]:
            copy.wait()
        if first:
            values = held[0][rows, :].astype(F32)
        else:
            total = held[0][rows, :] + (held[1][rows, :].astype(F32) + held[2][rows, :].astype(F32)) + vec_ref[5:6, :]
            x_ref[rows, :] = total.astype(BF)
            copies.leave(part_of(x_ref, rows), part_of(outs[5], rows))
            values = total.astype(BF).astype(F32)
        unit, _ = normalize(values)
        a = (unit * vec_ref[8 * layer : 8 * layer + 1, :] + vec_ref[8 * layer + 2 : 8 * layer + 3, :]).astype(BF)
        a_ref[rows, :] = a
        copies.leave(part_of(a_ref, rows), part_of(outs[0], rows))
        if number == 0:
            end_fetch(own[0], wqkv_ref, sems.at[0])
        projected = mm(a, wqkv_ref[...]) + bqkv_ref[layer : layer + 1, :]
        for group in range(PAIRS):
            query, key, value = to_pairs(projected, group)
            start = 3 * 128 * group
            qkv_ref[rows, start : start + 128] = query.astype(BF) * 0.125
            qkv_ref[rows, start + 128 : start + 256] = key.astype(BF)
            qkv_ref[rows, start + 256 : start + 384] = value.astype(BF)
        copies.leave(part_of(qkv_ref, rows), part_of(outs[1], rows))

    def attend(group, carry):
        low = lower_lanes(BQ)
        keep_diag = lax.broadcasted_iota(jnp.int32, (BQ, BQ), 1) <= lax.broadcasted_iota(jnp.int32, (BQ, BQ), 0)
        value = qkv_ref[:, lane_group(3 * group + 2)]
        low_all = lower_lanes(LEN)
        one = jnp.ones_like(value)
        values = (jnp.where(low_all, value, one), jnp.where(low_all, one, value))

        def scores(i, head):
            past, here = i * BQ, (i + 1) * BQ
            query = qkv_ref[past:here, lane_group(3 * group)]
            nothing = jnp.zeros_like(query)
            query = jnp.where(low, query, nothing) if head == 0 else jnp.where(low, nothing, query)
            diag = jnp.where(keep_diag, mm_nt(query, qkv_ref[past:here, lane_group(3 * group + 1)]), MASKED_SCORE)
            left = mm_nt(query, qkv_ref[0:past, lane_group(3 * group + 1)]) if i else None
            return diag, left

        units = [(i, head) for i in range(LEN // BQ) for head in range(2)]
        ahead = scores(*units[0])
        mixed, largest = [], []
        for number, (i, head) in enumerate(units):
            past, here = i * BQ, (i + 1) * BQ
            diag, left = ahead
            if number + 1 < len(units):
                ahead = scores(*units[number + 1])
            top = jnp.max(diag, axis=1, keepdims=True)
            if i:
                top = jnp.maximum(top, jnp.max(left, axis=1, keepdims=True))
            total = mm(jnp.exp(diag - top).astype(BF), values[head][past:here])
            if i:
                total = total + mm(jnp.exp(left - top).astype(BF), values[head][:past])
            mixed.append(total)
            largest.append(top)
            if head == 1:
                sums = pltpu.roll(jnp.where(low, mixed[1], mixed[0]), HS, 1)
                o_ref[past:here, lane_group(group)] = (jnp.where(low, mixed[0], mixed[1]) / sums).astype(BF)
                lse_ref[past:here, lane_group(group)] = jnp.where(low, largest[0], largest[1]) + jnp.log(sums)
                mixed, largest = [], []
        return carry

    lax.fori_loop(0, PAIRS, attend, 0)

    copies.leave(o_ref, outs[2])
    copies.leave(lse_ref, outs[3])
    end_fetch(own[1], wout_ref, sems.at[1])
    for rows in row_slices(512):
        part_ref[rows, :] = mm(o_ref[rows, :], wout_ref[...]).astype(BF)
        copies.leave(part_of(part_ref, rows), part_of(outs[4], rows))
    copies.finish()


def params(limit=VMEM_BYTES):
    return pltpu.CompilerParams(vmem_limit_bytes=limit)


def shape(dims, kind):
    return jax.ShapeDtypeStruct(dims, kind)


def cost(flops, moved, transcendentals=0):
    return pl.CostEstimate(flops=int(flops) // 1000, bytes_accessed=int(moved) // 1000, transcendentals=0)


def buffers(values):
    return [pltpu.VMEM(value.shape, value.dtype) for value in values]


def run_kernel(kernel, name, smem, weights, rows, acts, outs, scratch, flops):
    smem_spec, vmem, hbm = (pl.BlockSpec(memory_space=kind) for kind in (pltpu.SMEM, pltpu.VMEM, pl.ANY))
    return pl.pallas_call(
        kernel,
        out_shape=outs,
        in_specs=[smem_spec] * len(smem) + [hbm] * len(weights) + [vmem] * len(rows) + [hbm] * len(acts),
        out_specs=[hbm] * len(outs),
        scratch_shapes=buffers(acts) + buffers(outs) + list(scratch) + [pltpu.SemaphoreType.DMA((COPIES,))],
        compiler_params=params(),
        cost_estimate=cost(flops, 2e7),
        name=name,
    )(*smem, *weights, *rows, *acts)


def attention_forward(layer, which, weights, vecs, bqkv, *acts):
    outs = [
        shape((LEN, D), BF),
        shape((LEN, QW), BF),
        shape((LEN, HALF), BF),
        shape((LEN, HALF), F32),
        shape((LEN, D), BF),
    ]
    if layer:
        outs.append(shape((LEN, D), BF))
    scratch = [pltpu.VMEM((D, QW), BF), pltpu.VMEM((HALF, D), BF), pltpu.SemaphoreType.DMA((2,))]
    kernel = functools.partial(attention_forward_kernel, layer)
    return run_kernel(kernel, "attention_forward", (which,), weights, (vecs, bqkv), acts, outs, scratch, 1.2e10)


def gelu_parts(u):
    slope = math.sqrt(2.0 / math.pi)
    square = u * u
    half = 0.5 + 0.5 * jnp.tanh(u * (slope + (slope * 0.044715) * square))
    value = u * half
    return value, half + (value - value * half) * (2.0 * slope + (6.0 * slope * 0.044715) * square)


def feed_forward_kernel(layer, *refs):
    both = layer == 1
    which_ref, own, fc_pieces, proj_pieces, refs = refs[0], refs[1:3], refs[3:7], refs[7:11], refs[11:]
    vec_ref, bfc_ref, refs = refs[0], refs[1], refs[2:]
    count = 4 if both else 3
    ins, refs = refs[:count], refs[count:]
    outs, refs = refs[: 6 if both else 5], refs[6 if both else 5 :]
    held, refs = refs[:count], refs[count:]
    (h_ref, c_ref, g_ref, part_ref, slope_ref), refs = refs[:5], refs[5:]
    if both:
        dc_ref, refs = refs[0], refs[1:]
    wfc_ref, wproj_ref, sems, copy_sems = refs
    base = 8 * layer
    copies = Copies(copy_sems)
    blocks = row_slices(BR)
    arriving = [[copies.begin(part_of(src, rows), part_of(dst, rows)) for src, dst in zip(ins, held)] for rows in blocks]
    start_fetch(which_ref, own[0:1], fc_pieces, ((wfc_ref, FC_BLOCKS),), sems.at[pl.ds(0, 1)])
    start_fetch(which_ref, own[1:2], proj_pieces, ((wproj_ref, PROJ_BLOCKS),), sems.at[pl.ds(1, 1)], 2)

    for number, rows in enumerate(blocks):
        for copy in arriving[number]:
            copy.wait()
        h = held[0][rows, :].astype(F32) + (
            held[1][rows, :].astype(F32) + held[2][rows, :].astype(F32) + vec_ref[base + 3 : base + 4, :]
        )
        h_ref[rows, :] = h
        copies.leave(part_of(h_ref, rows), part_of(outs[0], rows))
        unit, _ = normalize(h)
        c = (unit * vec_ref[base + 1 : base + 2, :] + vec_ref[base + 4 : base + 5, :]).astype(BF)
        c_ref[rows, :] = c
        copies.leave(part_of(c_ref, rows), part_of(outs[1], rows))
        if number == 0:
            end_fetch(own[0], wfc_ref, sems.at[0])
            end_fetch(own[1], wproj_ref, sems.at[1])

        width = 512
        starts = list(range(0, FW, width))

        def up(start):
            cols = slice(start, start + width)
            u = mm(c, wfc_ref[:, cols]) + bfc_ref[layer : layer + 1, cols]
            return u, (mm_nt(held[3][rows, :], wproj_ref[cols, :]) if both else None)

        part, dc = None, None
        ahead = up(starts[0])
        for position, start in enumerate(starts):
            cols = slice(start, start + width)
            u, dg = ahead
            if position + 1 < len(starts):
                ahead = up(starts[position + 1])
            g, slope = gelu_parts(u)
            g = g.astype(BF)
            g_ref[rows, cols] = g
            more = mm(g, wproj_ref[cols, :])
            part = more if part is None else part + more
            if both:
                du = (dg * slope).astype(BF)
                slope_ref[rows, cols] = du
                more = mm_nt(du, wfc_ref[:, cols])
                dc = more if dc is None else dc + more
            else:
                slope_ref[rows, cols] = slope.astype(BF)
        copies.leave(part_of(g_ref, rows), part_of(outs[2], rows))
        copies.leave(part_of(slope_ref, rows), part_of(outs[4], rows))
        if both:
            dc_ref[rows, :] = dc.astype(BF)
            copies.leave(part_of(dc_ref, rows), part_of(outs[5], rows))
        part_ref[rows, :] = part.astype(BF)
        copies.leave(part_of(part_ref, rows), part_of(outs[3], rows))
    copies.finish()


def whole_spec(dims):
    return pl.BlockSpec(dims, lambda *i: (0,) * len(dims))


def feed_weights():
    return [pltpu.VMEM((D, FW), BF), pltpu.VMEM((FW, D), BF), pltpu.SemaphoreType.DMA((2,))]


def feed_forward(layer, which, weights, vecs, bfc, *acts):
    outs = [shape((LEN, D), F32), shape((LEN, D), BF), shape((LEN, FW), BF), shape((LEN, D), BF), shape((LEN, FW), BF)]
    if layer == 1:
        outs.append(shape((LEN, D), BF))
    kernel = functools.partial(feed_forward_kernel, layer)
    return run_kernel(kernel, "feed_forward", (which,), weights, (vecs, bfc), acts, outs, feed_weights(), 1e10)


def norm_back(vec, da, unit, scale, sums_ref):
    sums_ref[0:1, :] += column_sum(da * unit)
    sums_ref[1:2, :] += column_sum(da)
    return normalize_back(da, unit, scale, vec)


def feed_back_kernel(*refs):
    which_ref, own, fc_pieces, proj_pieces, refs = refs[0], refs[1:3], refs[3:7], refs[7:11], refs[11:]
    vec_ref, ins, outs, held, refs = refs[0], refs[1:6], refs[6:10], refs[10:15], refs[15:]
    (dm_ref, du_ref, dc_ref, sums_ref), (wfc_ref, wproj_ref, sems, copy_sems) = refs[:4], refs[4:]
    dh_ref, own_ref, recv_ref, x_ref, slope_ref = held
    copies = Copies(copy_sems)
    blocks = row_slices(BR)
    arriving = []
    for rows in blocks:
        arriving.append([copies.begin(part_of(src, rows), part_of(dst, rows)) for src, dst in zip(ins, held)])
        if len(arriving) == 1:
            start_fetch(which_ref, own[1:2], proj_pieces, ((wproj_ref, PROJ_BLOCKS),), sems.at[pl.ds(1, 1)], 2)
            start_fetch(which_ref, own[0:1], fc_pieces, ((wfc_ref, FC_BLOCKS),), sems.at[pl.ds(0, 1)])
    sums_ref[...] = jnp.zeros_like(sums_ref)

    for number, rows in enumerate(blocks):
        for copy in arriving[number]:
            copy.wait()
        unit, scale = normalize(x_ref[rows, :].astype(F32))
        da = own_ref[rows, :].astype(F32) + recv_ref[rows, :].astype(F32)
        dm = (dh_ref[rows, :] + norm_back(vec_ref[8:9, :], da, unit, scale, sums_ref)).astype(BF)
        dm_ref[rows, :] = dm
        copies.leave(part_of(dm_ref, rows), part_of(outs[0], rows))
        if number == 0:
            end_fetch(own[1], wproj_ref, sems.at[1])
            end_fetch(own[0], wfc_ref, sems.at[0])
        width = 512
        starts = list(range(0, FW, width))

        def up(start):
            return mm_nt(dm, wproj_ref[start : start + width, :])

        dc = None
        ahead = up(starts[0])
        for position, start in enumerate(starts):
            cols = slice(start, start + width)
            dg = ahead
            if position + 1 < len(starts):
                ahead = up(starts[position + 1])
            du = (dg * slope_ref[rows, cols].astype(F32)).astype(BF)
            du_ref[rows, cols] = du
            more = mm_nt(du, wfc_ref[:, cols])
            dc = more if dc is None else dc + more
        copies.leave(part_of(du_ref, rows), part_of(outs[1], rows))
        dc_ref[rows, :] = dc.astype(BF)
        copies.leave(part_of(dc_ref, rows), part_of(outs[2], rows))
    copies.leave(sums_ref, outs[3])
    copies.finish()


def feed_back(which, weights, vecs, *acts):
    outs = [shape((LEN, D), BF), shape((LEN, FW), BF), shape((LEN, D), BF), shape((8, D), F32)]
    return run_kernel(feed_back_kernel, "feed_back", (which,), weights, (vecs,), acts, outs, feed_weights(), 5e9)


def input_back_kernel(vec_ref, *refs):
    ins, outs, held, (dx_ref, sums_ref, copy_sems) = refs[:4], refs[4:6], refs[6:10], refs[10:]
    dh_ref, own_ref, recv_ref, x_ref = held
    copies = Copies(copy_sems)
    blocks = row_slices(BT)
    arriving = [[copies.begin(part_of(src, rows), part_of(dst, rows)) for src, dst in zip(ins, held)] for rows in blocks]
    sums_ref[...] = jnp.zeros_like(sums_ref)
    for number, rows in enumerate(blocks):
        for copy in arriving[number]:
            copy.wait()
        unit, scale = normalize(x_ref[rows, :].astype(F32))
        da = own_ref[rows, :].astype(F32) + recv_ref[rows, :].astype(F32)
        dx_ref[rows, :] = (dh_ref[rows, :] + norm_back(vec_ref[0:1, :], da, unit, scale, sums_ref)).astype(BF)
        copies.leave(part_of(dx_ref, rows), part_of(outs[0], rows))
    copies.leave(sums_ref, outs[1])
    copies.finish()


def input_back(vecs, *acts):
    outs = [shape((LEN, D), BF), shape((8, D), F32)]
    return run_kernel(input_back_kernel, "input_back", (), (), (vecs,), acts, outs, (), 1e7)


def in_three(values, spots):
    high = values.astype(BF)
    rest = values - high.astype(F32)
    middle = rest.astype(BF)
    low = (rest - middle.astype(F32)).astype(BF)
    return jnp.where(spots == 0, high, jnp.where(spots == 1, middle, jnp.where(spots == 2, low, jnp.zeros_like(low))))


def attention_back_kernel(layer, *refs):
    which_ref, own, pieces, refs = refs[0], refs[1:3], refs[3:7], refs[7:]
    vec_ref, ins, outs, held, refs = refs[0], refs[1:8], refs[8:14], refs[14:21], refs[21:]
    (dh_ref, dz_ref, dqkv_ref, da_ref, sums_ref, bias_ref), refs = refs[:6], refs[6:]
    do_ref, dk_ref, dv_ref, wqkv_ref, wout_ref, sems, copy_sems = refs
    dm_ref, own_ref, recv_ref, h_ref, qkv_ref, o_ref, lse_ref = held
    copies = Copies(copy_sems)
    blocks = row_slices(BT)
    arriving = []
    for rows in blocks:
        arriving.append([copies.begin(part_of(src, rows), part_of(dst, rows)) for src, dst in zip(ins[:4], held[:4])])
        if len(arriving) == 1:
            start_fetch(which_ref, own, pieces, ((wqkv_ref, QKV_BLOCKS), (wout_ref, OUT_BLOCKS)), sems)
    later = [copies.begin(src, dst) for src, dst in zip(ins[4:], held[4:])]
    gain = vec_ref[8 * layer + 1 : 8 * layer + 2, :]
    sums_ref[...] = jnp.zeros_like(sums_ref)
    bias_ref[...] = jnp.zeros_like(bias_ref)

    for number, rows in enumerate(blocks):
        for copy in arriving[number]:
            copy.wait()
        unit, scale = normalize(h_ref[rows, :])
        dc = own_ref[rows, :].astype(F32) + recv_ref[rows, :].astype(F32)
        dm = dm_ref[rows, :].astype(F32)
        dh = dm + norm_back(gain, dc, unit, scale, sums_ref)
        dh_ref[rows, :] = dh
        copies.leave(part_of(dh_ref, rows), part_of(outs[0], rows))
        dz = dh.astype(BF)
        dz_ref[rows, :] = dz
        copies.leave(part_of(dz_ref, rows), part_of(outs[1], rows))
        sums_ref[2:3, :] += column_sum(dz.astype(F32))
        sums_ref[3:4, :] += column_sum(dm)
        if number == 0:
            end_fetch(own[1], wout_ref, sems.at[1])
        do_ref[rows, :] = mm_nt(dz, wout_ref[...]).astype(BF)
    copies.leave(sums_ref, outs[4])
    for copy in later:
        copy.wait()

    def attend(group, carry):
        low = lower_lanes(BK)
        low_all = lower_lanes(LEN)
        spots = lax.broadcasted_iota(jnp.int32, (BK, 128), 1) % HS
        ones = jnp.where(lax.broadcasted_iota(jnp.int32, (LEN, 128), 1) % HS < 3, 1.0, 0.0).astype(BF)
        keep_diag = lax.broadcasted_iota(jnp.int32, (BK, BK), 0) <= lax.broadcasted_iota(jnp.int32, (BK, BK), 1)
        nothing = jnp.zeros((BK, 128), BF)
        key = qkv_ref[:, lane_group(3 * group + 1)]
        value = qkv_ref[:, lane_group(3 * group + 2)]
        blank = jnp.zeros_like(key)
        keys_with = (jnp.where(low_all, key, ones), jnp.where(low_all, ones, key))
        values_with = (jnp.where(low_all, value, ones), jnp.where(low_all, ones, value))
        keys_one = (jnp.where(low_all, key, blank), jnp.where(low_all, blank, key))

        def prepare(i):
            mine = slice(i * BK, (i + 1) * BK)
            query = qkv_ref[mine, lane_group(3 * group)]
            do = do_ref[mine, lane_group(group)]
            lse = in_three(-pltpu.roll(lse_ref[mine, lane_group(group)], HS, 1), spots)
            inner = do.astype(F32) * o_ref[mine, lane_group(group)].astype(F32)
            t_low = jnp.sum(jnp.where(low, inner, 0.0), axis=1, keepdims=True)
            t_high = jnp.sum(jnp.where(low, 0.0, inner), axis=1, keepdims=True)
            t = in_three(-jnp.where(low, t_high, t_low), spots)
            return (
                (jnp.where(low, query, lse), jnp.where(low, lse, query)),
                (jnp.where(low, do, t), jnp.where(low, t, do)),
                (jnp.where(low, query, nothing), jnp.where(low, nothing, query)),
                (jnp.where(low, do, nothing), jnp.where(low, nothing, do)),
            )

        def products(i, head, prepared):
            past, here = i * BK, (i + 1) * BK
            query_with, do_with = prepared[0][head], prepared[1][head]
            diag = jnp.where(keep_diag, mm_nt(keys_with[head][past:here], query_with), MASKED_SCORE)
            out = [(diag, mm_nt(values_with[head][past:here], do_with))]
            if i:
                out.append((mm_nt(keys_with[head][:past], query_with), mm_nt(values_with[head][:past], do_with)))
            return out

        units = [(i, head) for i in range(LEN // BK) for head in range(2)]
        prepared = prepare(0)
        ahead = products(0, 0, prepared)
        dq = None
        for number, (i, head) in enumerate(units):
            past, here = i * BK, (i + 1) * BK
            now, now_prepared = ahead, prepared
            if number + 1 < len(units):
                if head == 1:
                    prepared = prepare(i + 1)
                ahead = products(*units[number + 1], prepared)
            query_one, do_one = now_prepared[2][head], now_prepared[3][head]
            for rows, (score, inner) in zip((slice(past, here), slice(0, past)), now):
                p = jnp.exp(score)
                ds = (p * inner).astype(BF)
                dv = mm(p.astype(BF), do_one)
                dk = mm(ds, query_one)
                part = mm_tn(ds, keys_one[head][rows])
                dq = part if dq is None else dq + part
                if head == 0 and rows.start == past:
                    dv_ref[rows, :] = dv
                    dk_ref[rows, :] = dk
                else:
                    dv_ref[rows, :] += dv
                    dk_ref[rows, :] += dk
            if head == 1:
                dqkv_ref[past:here, lane_group(3 * group)] = (dq * 0.125).astype(BF)
                dq = None
        for i in range(NB):
            mine = slice(i * BT, (i + 1) * BT)
            one, two, three = from_pairs(
                dqkv_ref[mine, lane_group(3 * group)].astype(F32), dk_ref[mine, :], dv_ref[mine, :]
            )
            dqkv_ref[mine, lane_group(3 * group)] = one.astype(BF)
            dqkv_ref[mine, lane_group(3 * group + 1)] = two.astype(BF)
            dqkv_ref[mine, lane_group(3 * group + 2)] = three.astype(BF)
        return carry

    lax.fori_loop(0, PAIRS, attend, 0)

    copies.leave(dqkv_ref, outs[2])
    end_fetch(own[0], wqkv_ref, sems.at[0])
    for rows in row_slices(512):
        da_ref[rows, :] = mm_nt(dqkv_ref[rows, :], wqkv_ref[...]).astype(BF)
        copies.leave(part_of(da_ref, rows), part_of(outs[3], rows))
        bias_ref[0:1, :] += column_sum(dqkv_ref[rows, :].astype(F32))
    copies.leave(bias_ref, outs[5])
    copies.finish()


def attention_back(layer, which, weights, vecs, *acts):
    outs = [
        shape((LEN, D), F32),
        shape((LEN, D), BF),
        shape((LEN, QW), BF),
        shape((LEN, D), BF),
        shape((8, D), F32),
        shape((8, QW), F32),
    ]
    scratch = [
        pltpu.VMEM((LEN, HALF), BF),
        pltpu.VMEM((LEN, 128), F32),
        pltpu.VMEM((LEN, 128), F32),
        pltpu.VMEM((D, QW), BF),
        pltpu.VMEM((HALF, D), BF),
        pltpu.SemaphoreType.DMA((2,)),
    ]
    kernel = functools.partial(attention_back_kernel, layer)
    return run_kernel(kernel, "attention_back", (which,), weights, (vecs,), acts, outs, scratch, 2.2e10)


def feed_grad_kernel(*refs):
    ins, outs, held, refs = refs[:4], refs[4:10], refs[10:14], refs[14:]
    grads, (square_ref, bias_ref, copy_sems) = refs[:4], refs[4:]
    copies = Copies(copy_sems)
    g_ref, dm_ref, c_ref, du_ref = held
    bias_ref[...] = jnp.zeros_like(bias_ref)
    halves = [pl.ds(0, D), pl.ds(D, D)]
    arriving = []
    for half in range(2):
        arriving.append(copies.begin(ins[0].at[:, halves[half]], g_ref.at[:, halves[half]]))
        if half == 0:
            arriving.append(copies.begin(ins[1], dm_ref))
        arriving.append(copies.begin(ins[3].at[:, halves[half]], du_ref.at[:, halves[half]]))
        if half == 0:
            arriving.append(copies.begin(ins[2], c_ref))
    total = None
    for number in range(4):
        for copy in (arriving[0:2], arriving[2:4], arriving[4:5], arriving[5:6])[number]:
            copy.wait()
        cols = slice(number // 2 * D, (number // 2 + 1) * D)
        if number % 2 == 0:
            grad = mm_tn(g_ref[:, cols], dm_ref[...])
        else:
            grad = mm_tn(c_ref[...], du_ref[:, cols])
            bias_ref[0:1, cols] = column_sum(du_ref[:, cols].astype(F32))
        grads[number][...] = grad.astype(BF)
        copies.leave(grads[number], outs[number])
        square = column_sum(grad * grad)
        total = square if total is None else total + square
    square_ref[...] = jnp.zeros_like(square_ref)
    square_ref[0:1, :] = total
    copies.leave(square_ref, outs[4])
    copies.leave(bias_ref, outs[5])
    copies.finish()


def feed_grad(*acts):
    outs = [shape((D, D), BF)] * 4 + [shape((8, D), F32), shape((8, FW), F32)]
    return run_kernel(feed_grad_kernel, "feed_grad", (), (), (), acts, outs, (), 1e10)


def attention_grad_kernel(*refs):
    ins, outs, held, refs = refs[:4], refs[4:7], refs[7:11], refs[11:]
    targets, square_ref, copy_sems = refs[:2], refs[2], refs[3]
    copies = Copies(copy_sems)
    o_ref, dz_ref, a_ref, dqkv_ref = held
    arriving = [copies.begin(ins[number], held[number]) for number in (2, 3, 0, 1)]
    square_ref[...] = jnp.zeros_like(square_ref)
    for part, target in enumerate(targets):
        half = slice(part * HALF, (part + 1) * HALF)

        def place(grad, rows, cols):
            square_ref[0:1, 0:HALF] += column_sum(grad * grad)
            target[rows, cols] = grad.astype(BF)

        if part == 0:
            arriving[0].wait()
            arriving[1].wait()
        top = mm_tn(a_ref[:, half], dqkv_ref[...])
        if part == 0:
            arriving[2].wait()
            arriving[3].wait()
        out = mm_tn(o_ref[...], dz_ref[:, half])
        place(top[:, 0:HALF], slice(0, HALF), slice(0, HALF))
        place(top[:, HALF:D], slice(0, HALF), slice(HALF, D))
        for start, grad in ((HALF, top[:, D:]), (HALF + SIDE, out)):
            place(grad[:SIDE], slice(start, start + SIDE), slice(0, HALF))
            place(grad[SIDE:], slice(start, start + SIDE), slice(HALF, D))
        copies.leave(target, outs[part])
    copies.leave(square_ref, outs[2])
    copies.finish()


def attention_grad(*acts):
    outs = [shape((D, D), BF), shape((D, D), BF), shape((8, D), F32)]
    return run_kernel(attention_grad_kernel, "attention_grad", (), (), (), acts, outs, (), 5e9)


def pack_small_kernel(core_ref, *refs):
    ins, (small_ref, square_ref) = refs[:12], refs[12:]
    small_ref[...] = jnp.zeros_like(small_ref)
    lower = core_ref[0] == 0
    total = jnp.zeros((8, D), F32)
    for layer in range(2):
        bias_qkv, bias_fc, first, second, squares_feed, squares_attention = (ref[...] for ref in ins[6 * layer : 6 * layer + 6])

        def side(values):
            return jnp.where(lower, values[:, :HALF], values[:, HALF:])

        small_ref[layer, 0:1, :] = bias_fc[0:1, 0:D]
        small_ref[layer, 1:2, :] = bias_fc[0:1, D:]
        small_ref[layer, 2:3, :] = bias_qkv[0:1, 0:D]
        small_ref[layer, 3:4, 0:HALF] = bias_qkv[0:1, D:]
        rows = (first[0:1], second[0:1], first[1:2], second[2:3], second[1:2], second[3:4])
        for number, row in enumerate(rows):
            line, right = divmod(number + 1, 2)
            small_ref[layer, 3 + line : 4 + line, right * HALF : (right + 1) * HALF] = side(row)
        total = total + squares_feed + squares_attention
        total = total + small_ref[layer, 0:8, :] * small_ref[layer, 0:8, :]
    square_ref[...] = jnp.broadcast_to(jnp.sum(total, keepdims=True), (8, 128))


def pack_small(core, *parts):
    vmem = pl.BlockSpec(memory_space=pltpu.VMEM)
    return pl.pallas_call(
        pack_small_kernel,
        in_specs=[pl.BlockSpec(memory_space=pltpu.SMEM)] + [vmem] * 12,
        out_specs=[vmem] * 2,
        out_shape=[shape((2, 16, D), F32), shape((8, 128), F32)],
        compiler_params=params(),
        cost_estimate=cost(1e5, 1e5),
        name="pack_small",
    )(core, *parts)


def unpack_small(rows):
    tail = rows[3:7].reshape(8, HALF)
    bias = jnp.concatenate([rows[2], tail[0]])
    return bias, rows[0:2].reshape(FW), tail[1:3], tail[3:7]


def weigh_kernel(rows, roles_ref, mine_ref, across_ref, above_ref, *refs):
    sources, refs = refs[:8], refs[8:]
    if len(refs) == 6:
        (small_ref, other_ref, keep_ref, aside_ref, held_ref, sems) = refs
    else:
        (other_ref, keep_ref, aside_ref, held_ref, sems) = refs
        small_ref = None
    mine, home = roles_ref[0], roles_ref[1]

    def bring(slot, one, two):
        for number, source in enumerate((one, two)):
            pltpu.make_async_copy(source.at[rows], held_ref.at[2 * slot + number], sems.at[slot]).start()

    for layer in range(2):
        first, first_there, second, second_there = sources[4 * layer : 4 * layer + 4]

        @pl.when(mine == layer)
        def _(second=second, second_there=second_there):
            bring(2, second, second_there)

        for role in range(2):

            @pl.when((home == 1) & ((mine == layer) == (role == 1)))
            def _(role=role, first=first, first_there=first_there):
                bring(role, first, first_there)

    count = held_ref.shape[1]

    def total(slot, weight_ref):
        both = held_ref.at[pl.ds(2 * slot, 2)]
        pltpu.make_async_copy(both, both, sems.at[slot]).wait()
        return mine_ref[0:1, 0:1] * held_ref[2 * slot].astype(F32) + weight_ref[0:1, 0:1] * held_ref[
            2 * slot + 1
        ].astype(F32)

    @pl.when(home == 1)
    def _():
        for slot, target in ((0, other_ref), (1, keep_ref)):
            target[0:count, :] = total(slot, across_ref).astype(target.dtype)
            if small_ref is not None:
                target[count:, :] = jnp.where(mine == slot, small_ref[1], small_ref[0]).astype(target.dtype)
        aside_ref[0:count, :] = total(2, above_ref).astype(BF)
        if small_ref is not None:
            aside_ref[count:, :] = jnp.zeros((16, D), BF)

    @pl.when(home == 0)
    def _():
        other_ref[0:count, :] = total(2, above_ref).astype(BF)
        if small_ref is not None:
            other_ref[count:, :] = jnp.zeros((16, D), BF)


def weigh(rows, roles, weights, layers, small=None):
    count = rows.stop - rows.start
    tall = count + (0 if small is None else 16)
    vmem, smem, hbm = (pl.BlockSpec(memory_space=kind) for kind in (pltpu.VMEM, pltpu.SMEM, pl.ANY))
    return pl.pallas_call(
        functools.partial(weigh_kernel, pl.ds(rows.start, count)),
        out_shape=[shape((tall, D), BF), shape((tall, D), F32), shape((tall, D), BF)],
        in_specs=[smem] + [vmem] * 3 + [hbm] * 8 + ([] if small is None else [vmem]),
        out_specs=[vmem] * 3,
        scratch_shapes=[pltpu.VMEM((6, count, D), BF), pltpu.SemaphoreType.DMA((3,))],
        compiler_params=params(SMALL_VMEM_BYTES),
        cost_estimate=cost(1e7, 1e7),
        name="weigh",
    )(roles, *weights, *layers[0], *layers[1], *(() if small is None else (small,)))


def noise_rows():
    sizes = (D * QW, QW, HALF * D, D * FW, FW, FW * D, 2 * HALF, 4 * HALF)
    starts = [0]
    for size in sizes:
        starts.append(starts[-1] + size // 128)
    return starts


NOISE_ROWS = noise_rows()


def bring_noise(noise_ref, begin, raw_ref, sem):
    copy = pltpu.make_async_copy(noise_ref.at[pl.ds(begin, raw_ref.shape[0])], raw_ref, sem)
    copy.start()
    return copy


def put_noised(target, block, rows, col, wide_ref, first, denominator):
    scale = NOISE_MULT * CLIP_FRACTION * math.sqrt(LEN * FF * D)
    per = target.shape[1] // 128
    tall = rows.stop - rows.start
    for tile in range(block.shape[1] // 128):
        place = col // 128 + tile
        noise = wide_ref[pl.ds(first + per * rows.start + place, tall, stride=per), :]
        value = block[:, tile * 128 : (tile + 1) * 128].astype(F32)
        target[rows, place * 128 : (place + 1) * 128] = (value + scale * noise) / denominator


def finish_feed_kernel(columns, denominator, home_ref, *refs):
    own, swapped = refs[:2], refs[2:4]
    noise_ref, grad_ref, raw_ref, wide_ref, sem = refs[4:]
    first = NOISE_ROWS[3 if columns else 5]
    begin = first // 16 * 16
    bring_noise(noise_ref, begin, raw_ref, sem).wait()
    wide_ref[...] = raw_ref[...].astype(F32)
    step = D // 2

    def run(parts):
        for number, part in enumerate(parts):
            for index in range(2):
                row, col = (index * step, number * D) if columns else (number * D + index * step, 0)
                block = part[index][0:step, :]
                put_noised(grad_ref, block, slice(row, row + step), col, wide_ref, first - begin, denominator)

    @pl.when(home_ref[0] == 1)
    def _():
        run((own, swapped))

    @pl.when(home_ref[0] == 0)
    def _():
        run((swapped, own))


def finish_attention_kernel(denominator, home_ref, *refs):
    own, swapped = refs[0:2], refs[2:4]
    noise_ref, qkv_ref, out_ref, raw_ref, wide_ref, sem = refs[4:]
    bring_noise(noise_ref, 0, raw_ref, sem).wait()
    wide_ref[...] = raw_ref[...].astype(F32)

    def run(parts):
        for number, (one, two) in enumerate(parts):
            start = number * HALF
            put_noised(qkv_ref, one[...], slice(start, start + HALF), 0, wide_ref, NOISE_ROWS[0], denominator)
            for index in range(2):
                cols = slice(index * HALF, (index + 1) * HALF)
                rows = slice(start + index * SIDE, start + (index + 1) * SIDE)
                put_noised(qkv_ref, two[0:SIDE, cols], rows, D, wide_ref, NOISE_ROWS[0], denominator)
                rows = slice(index * SIDE, (index + 1) * SIDE)
                put_noised(out_ref, two[SIDE : 2 * SIDE, cols], rows, start, wide_ref, NOISE_ROWS[2], denominator)

    @pl.when(home_ref[0] == 1)
    def _():
        run((own, swapped))

    @pl.when(home_ref[0] == 0)
    def _():
        run((swapped, own))


def finish(kernel, denominator, home, own, swapped, noise, numbers, shapes, name):
    smem, vmem, hbm = (pl.BlockSpec(memory_space=kind) for kind in (pltpu.SMEM, pltpu.VMEM, pl.ANY))
    begin, end = NOISE_ROWS[numbers[0]] // 16 * 16, -(-NOISE_ROWS[numbers[-1] + 1] // 16) * 16
    return pl.pallas_call(
        functools.partial(kernel, denominator),
        out_shape=[shape(dims, F32) for dims in shapes],
        in_specs=[smem] + [vmem] * (2 * len(own)) + [hbm],
        out_specs=[vmem] * len(shapes),
        scratch_shapes=[
            pltpu.VMEM((end - begin, 128), BF),
            pltpu.VMEM((end - begin, 128), F32),
            pltpu.SemaphoreType.DMA,
        ],
        compiler_params=params(),
        cost_estimate=cost(1e7, 1.6e7),
        name=name,
    )(home, *own, *swapped, noise)


def send(values, route):
    sections, ranks = lax.axis_size("section"), lax.axis_size("dp")
    pairs = []
    for section in range(sections):
        for rank in range(ranks):
            target = route(section, rank // 2, rank % 2)
            if target is not None:
                to_section, to_pair, to_core = target
                pairs.append((section * ranks + rank, to_section * ranks + to_pair * 2 + to_core))
    return lax.ppermute(values, ("section", "dp"), pairs)


def swap_cores(values):
    return send(values, lambda s, z, c: (s, z, 1 - c))


def is_home(s, c):
    return s % 2 == c


def after(values, *others):
    return lax.optimization_barrier((values, *others))[0]


def local(
    inputs,
    cotangent,
    included,
    qkv_weight,
    qkv_bias,
    out_weight,
    fc_weight,
    fc_bias,
    proj_weight,
    norm_gains,
    shifts,
    noise,
):
    clip_norm = CLIP_FRACTION * math.sqrt(LEN * FF * D)
    section = lax.axis_index("section")
    rank = lax.axis_index("dp")
    ranks = lax.axis_size("dp")
    row, half = section // 2, section % 2
    place, core = rank // 2, rank % 2
    home = half == core
    on_top = row == 0
    flip = home.astype(jnp.int32).reshape(1)
    denominator = SAMPLE_RATE * inputs.shape[0] * ranks

    side = place % 2

    def piece_of(weight, number):
        tall = weight.shape[0] // 2
        if number is None:
            return lax.dynamic_slice_in_dim(weight, side * tall, tall, 0)
        return weight[number * tall : (number + 1) * tall]

    def attention_piece(number):
        qkv = piece_of(qkv_weight, number)
        tail = jnp.concatenate([qkv[:SIDE, D:], qkv[SIDE:, D:]], axis=1)
        return jnp.concatenate([qkv[:, :D], tail, piece_of(out_weight, number)])

    fc_piece = piece_of(fc_weight, None)
    fc_piece = jnp.concatenate([fc_piece[:, :D], fc_piece[:, D:]])

    def near(piece):
        return send(piece, lambda s, z, c: (s ^ 2, z, c) if is_home(s, c) else (s ^ 1, z, 1 - c))

    def far(one, two):
        far_one = send(one, lambda s, z, c: (s ^ 1, z, c) if is_home(s, c) else None)
        return far_one, send(two, lambda s, z, c: None if is_home(s, c) else (s ^ 2, z, c))

    def next_plane(one):
        return send(one, lambda s, z, c: (s, z ^ 1, c))

    fc_one = near(fc_piece)
    *parts, fc_one = lax.optimization_barrier((attention_piece(0), attention_piece(1), fc_one))
    attention_pieces = tuple(near(part) for part in parts)
    fc_two = next_plane(fc_one)
    *parts, one, two = lax.optimization_barrier((*(piece_of(proj_weight, i) for i in range(2)), *attention_pieces))
    attention_pieces = (one, two)
    attention_far = far(*attention_pieces)
    proj_pieces = tuple(near(part) for part in parts)
    fc_again, *attention_far = lax.optimization_barrier((fc_one, *attention_far))
    fc_far = far(fc_again, fc_two)
    proj_pieces = (*proj_pieces, *far(*proj_pieces))
    attention_pieces = (*attention_pieces, *attention_far)
    attention_weights = (qkv_weight, out_weight, *attention_pieces)

    def which_of(layer):
        kind = jnp.where(row == layer, jnp.where(home, 0, 1), jnp.where(home, 1, 2))
        nothing = jnp.zeros_like(side)
        return [jnp.stack([kind, first, nothing]).astype(jnp.int32) for first in (nothing, side)]

    which_attention, which_feed = zip(which_of(0), which_of(1))

    def own_sequence(values):
        mine = lax.dynamic_index_in_dim(values, half, 0, keepdims=False)
        theirs = swap_cores(mine)
        return jnp.where(core == row, mine, theirs)

    small = jnp.concatenate([qkv_bias, fc_bias, norm_gains.reshape(-1), shifts.reshape(-1)]).reshape(1, -1)
    others = [send(small, lambda s, z, c, bits=bits: (s ^ bits, z, c)) for bits in (1, 2, 3)]
    x0 = own_sequence(inputs)
    cot = own_sequence(cotangent)
    drawn = own_sequence(jnp.broadcast_to(included.astype(F32)[:, None, None], (2, 8, 128)))[0, 0]
    x0, cot = lax.optimization_barrier((x0, cot))
    small_all = jnp.concatenate([small] + others, axis=0)
    small_all = jnp.where(half == 0, small_all, jnp.concatenate([small_all[i : i + 1] for i in (1, 0, 3, 2)]))
    small_all = jnp.where(on_top, small_all, jnp.concatenate([small_all[2:], small_all[:2]]))
    small_all = small_all.reshape(2, 2, -1)
    bias = jnp.where(core == 0, small_all[:, 0], small_all[:, 1])
    bqkv, bfc = bias[:, :QW], bias[:, QW : QW + FW]
    vecs = small_all[:, :, QW + FW :].reshape(2, 2, 6, HALF).transpose(0, 2, 1, 3).reshape(2, 6, D)
    vecs = jnp.pad(vecs, ((0, 0), (0, 2), (0, 0))).reshape(16, D)

    shapes = ((D, QW), (QW,), (HALF, D), (D, FW), (FW,), (FW, D), (2, HALF), (4, HALF))
    a0, qkv0, o0, lse0, part = attention_forward(0, which_attention[0], attention_weights, vecs, bqkv, x0)
    part, *fc_far = lax.optimization_barrier((part, *fc_far))
    feed_weights_all = (fc_weight, proj_weight, fc_one, fc_two, *fc_far, *proj_pieces)
    part_theirs = swap_cores(part)
    h0, c0, g0, part_two, slope0 = feed_forward(
        0, which_feed[0], feed_weights_all, vecs, bfc, x0, part, part_theirs
    )
    a1, qkv1, o1, lse1, part, x1 = attention_forward(
        1, which_attention[1], attention_weights, vecs, bqkv, h0, part_two, swap_cores(part_two)
    )
    h1, c1, g1, part_two, du1, dc = feed_forward(
        1, which_feed[1], feed_weights_all, vecs, bfc, x1, part, swap_cores(part), cot
    )
    dc_theirs = swap_cores(dc)

    def spread(block_for):
        received = []
        for step in range(2):
            block = block_for(2 * core + (step ^ half))
            received.append(send(block, lambda s, z, c, step=step: (2 * c + (step ^ (s % 2)), z, s // 2)))
        return received

    def over_x(values):
        return send(values, lambda s, z, c: None if is_home(s, c) else (s ^ 1, z, c))

    def over_y(layer, values):
        return send(values, lambda s, z, c: None if s // 2 == layer else (s ^ 2, z, c))

    *grads1, squares_feed1, bias_fc1 = feed_grad(g1, cot, c1, du1)
    dc, dc_theirs, *grads1 = lax.optimization_barrier((dc, dc_theirs, *grads1))
    proj_x1, fc_x1, proj_y1 = over_x(grads1[0]), over_x(grads1[1]), over_y(1, grads1[2])
    dh1, dz1, dqkv1, da, sums1, bias_qkv1 = attention_back(
        1, which_attention[1], attention_weights, vecs, cot, dc, dc_theirs, h1, qkv1, o1, lse1
    )
    da, proj_x1, fc_x1, proj_y1 = lax.optimization_barrier((da, proj_x1, fc_x1, proj_y1))
    da_theirs = swap_cores(da)
    fc_y1 = over_y(1, grads1[3])
    first1, second1, squares_attention1 = attention_grad(o1, dz1, a1, dqkv1)
    da, da_theirs, first1 = lax.optimization_barrier((da, da_theirs, first1))
    dm0, du0, dc, first_sums1 = feed_back(which_feed[0], feed_weights_all, vecs, dh1, da, da_theirs, x1, slope0)
    dc, fc_y1 = lax.optimization_barrier((dc, fc_y1))
    dc_theirs = swap_cores(dc)
    attention_x1 = over_x(first1)
    *grads0, squares_feed0, bias_fc0 = feed_grad(g0, dm0, c0, du0)
    dc, dc_theirs, attention_x1, *grads0 = lax.optimization_barrier((dc, dc_theirs, attention_x1, *grads0))
    proj_x0, fc_x0, proj_y0 = over_x(grads0[0]), over_x(grads0[1]), over_y(0, grads0[2])
    attention_y1 = over_y(1, second1)
    dh0, dz0, dqkv0, da, sums0, bias_qkv0 = attention_back(
        0, which_attention[0], attention_weights, vecs, dm0, dc, dc_theirs, h0, qkv0, o0, lse0
    )
    da, proj_x0, fc_x0, proj_y0, attention_y1 = lax.optimization_barrier((da, proj_x0, fc_x0, proj_y0, attention_y1))
    da_theirs = swap_cores(da)
    fc_y0 = over_y(0, grads0[3])
    first0, second0, squares_attention0 = attention_grad(o0, dz0, a0, dqkv0)
    dx0, first_sums0 = input_back(vecs, dh0, da, da_theirs, x0)
    small_pair, squares = pack_small(
        core.astype(jnp.int32).reshape(1),
        *(bias_qkv0, bias_fc0, first_sums0, sums0, squares_feed0, squares_attention0),
        *(bias_qkv1, bias_fc1, first_sums1, sums1, squares_feed1, squares_attention1),
    )
    small_there = send(small_pair, lambda s, z, c: None if is_home(s, c) else (s ^ 1, z, c))

    squares = squares + swap_cores(squares)
    factor = drawn * jnp.minimum(1.0, clip_norm / jnp.sqrt(squares))
    across = send(factor, lambda s, z, c: (s ^ 1, z, 1 - c) if is_home(s, c) else None)
    above = send(factor, lambda s, z, c: (s ^ 2, z, c))
    factor, across, above, fc_y0 = lax.optimization_barrier((factor, across, above, fc_y0))
    weights = (factor, across, above)
    roles = jnp.stack([row, home]).astype(jnp.int32)

    def send_first(first, small_pair):
        there = over_x(jnp.concatenate([first, small_pair[:, :8].reshape(16, D).astype(BF)]))
        small = there[D:].astype(F32).reshape(2, 8, D)
        small = jnp.where(home, weights[0][0, 0] * small_pair[:, :8] + weights[1][0, 0] * small, 0.0)
        return there, jnp.pad(small, ((0, 0), (0, 8), (0, 0)))


    proj0, proj1 = (grads0[0], proj_x0, grads0[2], proj_y0), (grads1[0], proj_x1, grads1[2], proj_y1)
    fc0, fc1 = (grads0[1], fc_x0, grads0[3], fc_y0), (grads1[1], fc_x1, grads1[3], fc_y1)
    attention1 = (first1, attention_x1, second1, attention_y1)

    token_rows = LEN // lax.axis_size("section")

    def last_output(part_two):
        return (h1 + (part_two.astype(F32) + swap_cores(part_two).astype(F32)) + vecs[13:14]).astype(BF)

    def exchange_outputs(y1, dx0):
        both_out = jnp.concatenate([x1, y1], axis=1)

        def block_for(number):
            columns = lax.dynamic_slice_in_dim(both_out, number * HALF, HALF, 1)
            rows = lax.dynamic_slice_in_dim(dx0, number * token_rows, token_rows, 0)
            return jnp.concatenate([columns, rows[:, :HALF], rows[:, HALF:]])

        return spread(block_for)

    def ordered_outputs(outputs):
        outputs = in_order(*outputs)
        rows = (outputs[:, LEN : LEN + token_rows], outputs[:, LEN + token_rows :])
        return outputs[:, :LEN], jnp.concatenate(rows, axis=2)

    def in_order(first, second):
        return jnp.where(half == 0, jnp.stack([first, second]), jnp.stack([second, first]))

    places = ranks // 2
    middle = places // 2

    def to_middle(step):
        def route(s, z, c):
            if z == step:
                return (s, z + 1, c)
            if z == places - 1 - step:
                return (s, z - 1, c)
            return None

        return route

    def at_middle(s, z, c):
        return (s, places - 1 - z, c) if z in (middle - 1, middle) else None

    def from_middle(step):
        def route(s, z, c):
            if z == middle - 1 - step:
                return (s, z - 1, c)
            if z == middle + step:
                return (s, z + 1, c)
            return None

        return route

    def add(left, right):
        return (left.astype(F32) + right.astype(F32)).astype(BF)

    def weigh_stage(args):
        other, keep, aside = weigh(*args)
        arrived = send(other, lambda s, z, c: (s ^ 2, z, c) if is_home(s, c) else (s ^ 1, z, 1 - c))
        aside = send(aside, lambda s, z, c: (s, z, 1 - c) if is_home(s, c) else None)
        return keep, aside, arrived

    def weigh_end(held):
        keep, aside, arrived = held
        return (jnp.where(home, keep, aside.astype(F32)) + arrived.astype(F32)).astype(BF)

    def chain_stage(hop):
        def stage(held):
            total = add(*held) if len(held) == 2 else weigh_end(held)
            return total, send(total, hop)

        return stage

    def spread_stage(step):
        def stage(held):
            total, arrived = held
            if step == 0:
                total = add(total, arrived)
            else:
                takes = (place == middle - 1 - step) | (place == middle + step)
                total = jnp.where(takes, arrived, total)
            return total, send(total, from_middle(step))

        return stage

    def last_stage(held):
        total, arrived = held
        if middle > 1:
            takes = (place == 0) | (place == places - 1)
            total = jnp.where(takes, arrived, total)
        else:
            total = add(total, arrived)
        return total, swap_cores(total)

    hops = [to_middle(step) for step in range(middle - 1)] + [at_middle]
    stages = [weigh_stage] + [chain_stage(hop) for hop in hops]
    stages += [spread_stage(step) for step in range(middle - 1)] + [last_stage]

    chunk = D // 2

    noise_flat = noise.reshape(-1, 128)

    def small_noise(number, dims):
        first = NOISE_ROWS[number] * 128
        return noise[first : first + math.prod(dims)].reshape(dims).astype(F32)

    def finish_proj(one, two):
        return finish(
            functools.partial(finish_feed_kernel, False), denominator, flip, *zip(one, two), noise_flat, (5,), ((FW, D),), "finish_feed"
        )[0]

    def finish_fc(one, two):
        return finish(
            functools.partial(finish_feed_kernel, True), denominator, flip, *zip(one, two), noise_flat, (3,), ((D, FW),), "finish_feed"
        )[0]

    if middle == 2:
        edge = (place == 0) | (place == places - 1)

        def to_next(s, z, c):
            return (s, z ^ 1, c)

        count = 6
        begun, sums, lows, totals, ready = ({} for _ in range(5))
        outer, last = None, None

        def tie(*values):
            if last is None or last[1] not in last[0]:
                return values if len(values) > 1 else values[0]
            store, name = last
            *values, store[name] = lax.optimization_barrier((*values, store[name]))
            return values if len(values) > 1 else values[0]

        def begin(group, pair, *small):
            begun[group], begun[group, 1], begun[group, 2] = weigh_stage(
                (slice(0, D), roles, tie(*weights), pair, *small)
            )
            return begun, group

        attention_x0, small_sum = send_first(first0, small_pair)
        last = begin(0, (proj0, proj1))
        last = begin(1, (fc0, fc1))
        second0 = tie(second0)
        attention_y0 = over_y(0, second0)
        inners = {}
        for tick in range(count + 4):
            old_outer = outer
            if 0 <= tick - 3 < count:
                totals[tick - 3] = add(tie(lows.pop(tick - 3)), inners.pop(tick - 3))
                last = totals, tick - 3
            if tick < count and tick % 2 == 0:
                group = tick // 2
                total = weigh_end((tie(begun.pop(group)), begun.pop((group, 1)), begun.pop((group, 2))))
                sums[tick], sums[tick + 1] = total[:chunk], total[chunk:]
                last = sums, tick
            inward, outward = sums.get(tick), totals.get(tick - 3)
            if inward is not None and outward is not None:
                tall = [inward.shape[0], outward.shape[0]]
                padded = [jnp.pad(part, ((0, max(tall) - part.shape[0]), (0, 0))) for part in (inward, outward)]
                outer = send(jnp.where(edge, *padded), to_next)
                outer = (outer[: tall[0]], outer[: tall[1]])
            else:
                outer = (
                    None if inward is None else send(inward, to_middle(0)),
                    None if outward is None else send(outward, from_middle(0)),
                )
            if 0 <= tick - 1 < count:
                lows[tick - 1] = add(tie(sums.pop(tick - 1)), old_outer[0])
                last = lows, tick - 1
                inners[tick - 1] = send(lows[tick - 1], at_middle)
            if 0 <= tick - 4 < count:
                total = tie(totals.pop(tick - 4))
                if tick == count + 3:
                    total, layer_out, input_grad = lax.optimization_barrier(
                        (total, *ordered_outputs(outputs))
                    )
                ready[tick - 4] = jnp.where(edge, old_outer[1], total)
                last = ready, tick - 4
            if tick == 2:
                attention_x0, attention_y0, small_sum = tie(attention_x0, attention_y0, small_sum)
                attention0 = (first0, attention_x0, second0, attention_y0)
                last = begin(2, (attention0, attention1), small_sum)
            if tick == 2:
                y1 = last_output(tie(part_two))
            if tick == 4:
                outputs = exchange_outputs(*tie(y1, dx0))
            if tick == 6:
                proj_grad = finish_proj(*((ready[i], swap_cores(ready[i])) for i in (0, 1)))
            if tick == 8:
                proj_grad = tie(proj_grad)
                fc_grad = finish_fc(*((ready[i], swap_cores(ready[i])) for i in (2, 3)))
            if tick == 9:
                fc_grad = tie(fc_grad)
        jobs = [None] * 4 + [(ready[i], swap_cores(ready[i])) for i in (4, 5)]
        small_own, small_swapped = jobs[5]
        stages = []
    else:
        attention_x0, small_sum = send_first(first0, small_pair)
        attention0 = (first0, attention_x0, second0, over_y(0, second0))
        jobs = []
        for pair in ((proj0, proj1), (fc0, fc1), (attention0, attention1)):
            jobs += [(slice(i * chunk, (i + 1) * chunk), roles, weights, pair) for i in range(2)]
        jobs[5] += (small_sum,)
        layer_out, input_grad = ordered_outputs(exchange_outputs(last_output(part_two), dx0))
    for tick in range(len(jobs) + len(stages) - 1 if stages else 0):
        for stage in reversed(range(len(stages))):
            index = tick - stage
            if 0 <= index < len(jobs):
                held = jobs[index]
                jobs[index] = stages[stage](held)
    if stages:
        proj_grad, fc_grad = finish_proj(*jobs[0:2]), finish_fc(*jobs[2:4])
        small_own, small_swapped = jobs[5]
    attention = jobs[4:]
    own, swapped = zip(*attention)
    qkv_grad, out_grad = finish(
        finish_attention_kernel, denominator, flip, own, swapped, noise_flat, (0, 2), ((D, QW), (HALF, D)), "finish_attention"
    )
    small_sum = jnp.where(home, small_own[chunk:], small_swapped[chunk:]).astype(F32)
    small_done = [
        (part + NOISE_MULT * clip_norm * small_noise(number, part.shape)) / denominator
        for part, number in zip(unpack_small(small_sum), (1, 4, 6, 7))
    ]
    return (
        layer_out,
        input_grad,
        qkv_grad,
        small_done[0],
        out_grad,
        fc_grad,
        small_done[1],
        proj_grad,
        small_done[2],
        small_done[3],
    )


def solution(mesh):
    return jax.shard_map(
        local,
        mesh=mesh,
        in_specs=(
            P("dp", None, None),
            P("dp", None, None),
            P("dp"),
            P(None, "section"),
            P("section"),
            P("section", None),
            P(None, "section"),
            P("section"),
            P("section", None),
            P(None, "section"),
            P(None, "section"),
            P("section"),
        ),
        out_specs=(
            P("dp", None, "section"),
            P("dp", "section", None),
            P(None, "section"),
            P("section"),
            P("section", None),
            P(None, "section"),
            P("section"),
            P("section", None),
            P(None, "section"),
            P(None, "section"),
        ),
        check_vma=False,
    )
```

```python
import functools
import math

import jax
import jax.numpy as jnp
from jax import lax
from jax.experimental import pallas as pl
from jax.experimental.pallas import tpu as pltpu
from jax.sharding import PartitionSpec as P

D = 768
FF = 3072
HS = 64
LEN = 1024
HALF = D // 2
QW = 3 * HALF
FW = FF // 2
PAIRS = HALF // 128
BT = 256
NB = LEN // BT
BQ = 256
BR = 512
BK = 256

CLIP_FRACTION = 0.05
NOISE_MULT = 0.001
SAMPLE_RATE = 0.5
NORM_EPS = 1e-05
MASKED_SCORE = -1e30
VMEM_BYTES = 52 * 1024 * 1024
SMALL_VMEM_BYTES = 36 * 1024 * 1024

BF = jnp.bfloat16
F32 = jnp.float32


def mm(left, right):
    return lax.dot_general(left, right, (((1,), (0,)), ((), ())), preferred_element_type=F32)


def mm_nt(left, right):
    return lax.dot_general(left, right, (((1,), (1,)), ((), ())), preferred_element_type=F32)


def mm_tn(left, right):
    return lax.dot_general(left, right, (((0,), (0,)), ((), ())), preferred_element_type=F32)


def normalize(values):
    center = values - jnp.mean(values, axis=-1, keepdims=True)
    spread = jnp.mean(center * center, axis=-1, keepdims=True)
    scale = lax.rsqrt(spread + NORM_EPS)
    return center * scale, scale


def normalize_back(grad, unit, scale, gain):
    inner = grad * gain
    mean_inner = jnp.mean(inner, axis=-1, keepdims=True)
    mean_cross = jnp.mean(inner * unit, axis=-1, keepdims=True)
    return scale * (inner - mean_inner - unit * mean_cross)


def column_sum(values):
    return jnp.sum(values, axis=0, keepdims=True)


def block_rows(index):
    return pl.ds(pl.multiple_of(index * BT, BT), BT)


def lane_group(index, width=128):
    return pl.ds(pl.multiple_of(index * 128, 128), width)


def lower_lanes(rows=BT):
    return lax.broadcasted_iota(jnp.int32, (rows, 128), 1) < HS


def to_pairs(block, group):
    low = lower_lanes()
    start = 3 * 128 * group
    one, two, three = (block[:, start + 128 * i : start + 128 * (i + 1)] for i in range(3))
    query = jnp.where(low, one, two)
    key = pltpu.roll(jnp.where(low, three, one), HS, 1)
    value = jnp.where(low, two, three)
    return query, key, value


def from_pairs(query, key, value):
    low = lower_lanes()
    turned = pltpu.roll(key, HS, 1)
    return jnp.where(low, query, turned), jnp.where(low, value, query), jnp.where(low, turned, value)


class Copies:
    def __init__(self, sems):
        self.sems, self.used, self.left = sems, 0, []

    def begin(self, source, target):
        copy = pltpu.make_async_copy(source, target, self.sems.at[self.used])
        self.used += 1
        copy.start()
        return copy

    def leave(self, source, target):
        self.left.append(self.begin(source, target))

    def finish(self):
        for copy in self.left:
            copy.wait()


COPIES = 64


def row_slices(tall):
    return [slice(start, start + tall) for start in range(0, LEN, tall)]


def part_of(ref, rows):
    return ref.at[pl.ds(rows.start, rows.stop - rows.start)]


def start_fetch(which_ref, own, pieces, parts, sems, lower=1):
    @pl.when(which_ref[0] == 0)
    def _():
        for number, (target, _) in enumerate(parts):
            pltpu.make_async_copy(own[number], target, sems.at[number]).start()

    for kind in (1, 2):

        @pl.when(which_ref[0] == kind)
        def _(kind=kind):
            for order in range(2):
                piece = pieces[2 * kind - 2 + order]
                side = which_ref[lower] if order == 0 else 1 - which_ref[lower]
                for number, (target, blocks) in enumerate(parts):
                    base = pl.multiple_of(side * (target.shape[0] // 2), 64)
                    for (top, left), (tall, wide), (down, right) in blocks:
                        pltpu.make_async_copy(
                            piece.at[pl.ds(top, tall), pl.ds(left, wide)],
                            target.at[pl.ds(base + down, tall), pl.ds(right, wide)],
                            sems.at[number],
                        ).start()


def end_fetch(own, target, sem):
    pltpu.make_async_copy(own, target, sem).wait()


SIDE = HALF // 2
QKV_BLOCKS = (
    ((0, 0), (HALF, D), (0, 0)),
    ((HALF, 0), (SIDE, HALF), (0, D)),
    ((HALF, HALF), (SIDE, HALF), (SIDE, D)),
)
OUT_BLOCKS = (((HALF + SIDE, 0), (SIDE, D), (0, 0)),)
FC_BLOCKS = (((0, 0), (HALF, D), (0, 0)), ((HALF, 0), (HALF, D), (0, D)))
PROJ_BLOCKS = (((0, 0), (D, D), (0, 0)),)


def attention_forward_kernel(layer, *refs):
    which_ref, own, pieces, refs = refs[0], refs[1:3], refs[3:7], refs[7:]
    vec_ref, bqkv_ref, refs = refs[0], refs[1], refs[2:]
    first = layer == 0
    count = 1 if first else 3
    ins, refs = refs[:count], refs[count:]
    outs, refs = refs[: 5 if first else 6], refs[5 if first else 6 :]
    held, refs = refs[:count], refs[count:]
    (a_ref, qkv_ref, o_ref, lse_ref, part_ref), refs = refs[:5], refs[5:]
    if not first:
        x_ref, refs = refs[0], refs[1:]
    wqkv_ref, wout_ref, sems, copy_sems = refs
    copies = Copies(copy_sems)
    blocks = row_slices(BT)
    arriving = [[copies.begin(part_of(src, rows), part_of(dst, rows)) for src, dst in zip(ins, held)] for rows in blocks]
    start_fetch(which_ref, own, pieces, ((wqkv_ref, QKV_BLOCKS), (wout_ref, OUT_BLOCKS)), sems)

    for number, rows in enumerate(blocks):
        for copy in arriving[number]:
            copy.wait()
        if first:
            values = held[0][rows, :].astype(F32)
        else:
            total = held[0][rows, :] + (held[1][rows, :].astype(F32) + held[2][rows, :].astype(F32)) + vec_ref[5:6, :]
            x_ref[rows, :] = total.astype(BF)
            copies.leave(part_of(x_ref, rows), part_of(outs[5], rows))
            values = total.astype(BF).astype(F32)
        unit, _ = normalize(values)
        a = (unit * vec_ref[8 * layer : 8 * layer + 1, :] + vec_ref[8 * layer + 2 : 8 * layer + 3, :]).astype(BF)
        a_ref[rows, :] = a
        copies.leave(part_of(a_ref, rows), part_of(outs[0], rows))
        if number == 0:
            end_fetch(own[0], wqkv_ref, sems.at[0])
        projected = mm(a, wqkv_ref[...]) + bqkv_ref[layer : layer + 1, :]
        for group in range(PAIRS):
            query, key, value = to_pairs(projected, group)
            start = 3 * 128 * group
            qkv_ref[rows, start : start + 128] = query.astype(BF) * 0.125
            qkv_ref[rows, start + 128 : start + 256] = key.astype(BF)
            qkv_ref[rows, start + 256 : start + 384] = value.astype(BF)
        copies.leave(part_of(qkv_ref, rows), part_of(outs[1], rows))

    def attend(group, carry):
        low = lower_lanes(BQ)
        keep_diag = lax.broadcasted_iota(jnp.int32, (BQ, BQ), 1) <= lax.broadcasted_iota(jnp.int32, (BQ, BQ), 0)
        value = qkv_ref[:, lane_group(3 * group + 2)]
        low_all = lower_lanes(LEN)
        one = jnp.ones_like(value)
        values = (jnp.where(low_all, value, one), jnp.where(low_all, one, value))

        def scores(i, head):
            past, here = i * BQ, (i + 1) * BQ
            query = qkv_ref[past:here, lane_group(3 * group)]
            nothing = jnp.zeros_like(query)
            query = jnp.where(low, query, nothing) if head == 0 else jnp.where(low, nothing, query)
            diag = jnp.where(keep_diag, mm_nt(query, qkv_ref[past:here, lane_group(3 * group + 1)]), MASKED_SCORE)
            left = mm_nt(query, qkv_ref[0:past, lane_group(3 * group + 1)]) if i else None
            return diag, left

        units = [(i, head) for i in range(LEN // BQ) for head in range(2)]
        ahead = scores(*units[0])
        mixed, largest = [], []
        for number, (i, head) in enumerate(units):
            past, here = i * BQ, (i + 1) * BQ
            diag, left = ahead
            if number + 1 < len(units):
                ahead = scores(*units[number + 1])
            top = jnp.max(diag, axis=1, keepdims=True)
            if i:
                top = jnp.maximum(top, jnp.max(left, axis=1, keepdims=True))
            total = mm(jnp.exp(diag - top).astype(BF), values[head][past:here])
            if i:
                total = total + mm(jnp.exp(left - top).astype(BF), values[head][:past])
            mixed.append(total)
            largest.append(top)
            if head == 1:
                sums = pltpu.roll(jnp.where(low, mixed[1], mixed[0]), HS, 1)
                o_ref[past:here, lane_group(group)] = (jnp.where(low, mixed[0], mixed[1]) / sums).astype(BF)
                lse_ref[past:here, lane_group(group)] = jnp.where(low, largest[0], largest[1]) + jnp.log(sums)
                mixed, largest = [], []
        return carry

    lax.fori_loop(0, PAIRS, attend, 0)

    copies.leave(o_ref, outs[2])
    copies.leave(lse_ref, outs[3])
    end_fetch(own[1], wout_ref, sems.at[1])
    for rows in row_slices(512):
        part_ref[rows, :] = mm(o_ref[rows, :], wout_ref[...]).astype(BF)
        copies.leave(part_of(part_ref, rows), part_of(outs[4], rows))
    copies.finish()


def params(limit=VMEM_BYTES):
    return pltpu.CompilerParams(vmem_limit_bytes=limit)


def shape(dims, kind):
    return jax.ShapeDtypeStruct(dims, kind)


def cost(flops, moved, transcendentals=0):
    return pl.CostEstimate(flops=int(flops) // 1000, bytes_accessed=int(moved) // 1000, transcendentals=0)


def buffers(values):
    return [pltpu.VMEM(value.shape, value.dtype) for value in values]


def run_kernel(kernel, name, smem, weights, rows, acts, outs, scratch, flops):
    smem_spec, vmem, hbm = (pl.BlockSpec(memory_space=kind) for kind in (pltpu.SMEM, pltpu.VMEM, pl.ANY))
    return pl.pallas_call(
        kernel,
        out_shape=outs,
        in_specs=[smem_spec] * len(smem) + [hbm] * len(weights) + [vmem] * len(rows) + [hbm] * len(acts),
        out_specs=[hbm] * len(outs),
        scratch_shapes=buffers(acts) + buffers(outs) + list(scratch) + [pltpu.SemaphoreType.DMA((COPIES,))],
        compiler_params=params(),
        cost_estimate=cost(flops, 2e7),
        name=name,
    )(*smem, *weights, *rows, *acts)


def attention_forward(layer, which, weights, vecs, bqkv, *acts):
    outs = [
        shape((LEN, D), BF),
        shape((LEN, QW), BF),
        shape((LEN, HALF), BF),
        shape((LEN, HALF), F32),
        shape((LEN, D), BF),
    ]
    if layer:
        outs.append(shape((LEN, D), BF))
    scratch = [pltpu.VMEM((D, QW), BF), pltpu.VMEM((HALF, D), BF), pltpu.SemaphoreType.DMA((2,))]
    kernel = functools.partial(attention_forward_kernel, layer)
    return run_kernel(kernel, "attention_forward", (which,), weights, (vecs, bqkv), acts, outs, scratch, 1.2e10)


def gelu_parts(u):
    slope = math.sqrt(2.0 / math.pi)
    square = u * u
    half = 0.5 + 0.5 * jnp.tanh(u * (slope + (slope * 0.044715) * square))
    value = u * half
    return value, half + (value - value * half) * (2.0 * slope + (6.0 * slope * 0.044715) * square)


def feed_forward_kernel(layer, *refs):
    both = layer == 1
    which_ref, own, fc_pieces, proj_pieces, refs = refs[0], refs[1:3], refs[3:7], refs[7:11], refs[11:]
    vec_ref, bfc_ref, refs = refs[0], refs[1], refs[2:]
    count = 4 if both else 3
    ins, refs = refs[:count], refs[count:]
    outs, refs = refs[: 6 if both else 5], refs[6 if both else 5 :]
    held, refs = refs[:count], refs[count:]
    (h_ref, c_ref, g_ref, part_ref, slope_ref), refs = refs[:5], refs[5:]
    if both:
        dc_ref, refs = refs[0], refs[1:]
    wfc_ref, wproj_ref, sems, copy_sems = refs
    base = 8 * layer
    copies = Copies(copy_sems)
    blocks = row_slices(BR)
    arriving = [[copies.begin(part_of(src, rows), part_of(dst, rows)) for src, dst in zip(ins, held)] for rows in blocks]
    start_fetch(which_ref, own[0:1], fc_pieces, ((wfc_ref, FC_BLOCKS),), sems.at[pl.ds(0, 1)])
    start_fetch(which_ref, own[1:2], proj_pieces, ((wproj_ref, PROJ_BLOCKS),), sems.at[pl.ds(1, 1)], 2)

    for number, rows in enumerate(blocks):
        for copy in arriving[number]:
            copy.wait()
        h = held[0][rows, :].astype(F32) + (
            held[1][rows, :].astype(F32) + held[2][rows, :].astype(F32) + vec_ref[base + 3 : base + 4, :]
        )
        h_ref[rows, :] = h
        copies.leave(part_of(h_ref, rows), part_of(outs[0], rows))
        unit, _ = normalize(h)
        c = (unit * vec_ref[base + 1 : base + 2, :] + vec_ref[base + 4 : base + 5, :]).astype(BF)
        c_ref[rows, :] = c
        copies.leave(part_of(c_ref, rows), part_of(outs[1], rows))
        if number == 0:
            end_fetch(own[0], wfc_ref, sems.at[0])
            end_fetch(own[1], wproj_ref, sems.at[1])

        width = 512
        starts = list(range(0, FW, width))

        def up(start):
            cols = slice(start, start + width)
            u = mm(c, wfc_ref[:, cols]) + bfc_ref[layer : layer + 1, cols]
            return u, (mm_nt(held[3][rows, :], wproj_ref[cols, :]) if both else None)

        part, dc = None, None
        ahead = up(starts[0])
        for position, start in enumerate(starts):
            cols = slice(start, start + width)
            u, dg = ahead
            if position + 1 < len(starts):
                ahead = up(starts[position + 1])
            g, slope = gelu_parts(u)
            g = g.astype(BF)
            g_ref[rows, cols] = g
            more = mm(g, wproj_ref[cols, :])
            part = more if part is None else part + more
            if both:
                du = (dg * slope).astype(BF)
                slope_ref[rows, cols] = du
                more = mm_nt(du, wfc_ref[:, cols])
                dc = more if dc is None else dc + more
            else:
                slope_ref[rows, cols] = slope.astype(BF)
        copies.leave(part_of(g_ref, rows), part_of(outs[2], rows))
        copies.leave(part_of(slope_ref, rows), part_of(outs[4], rows))
        if both:
            dc_ref[rows, :] = dc.astype(BF)
            copies.leave(part_of(dc_ref, rows), part_of(outs[5], rows))
        part_ref[rows, :] = part.astype(BF)
        copies.leave(part_of(part_ref, rows), part_of(outs[3], rows))
    copies.finish()


def whole_spec(dims):
    return pl.BlockSpec(dims, lambda *i: (0,) * len(dims))


def feed_weights():
    return [pltpu.VMEM((D, FW), BF), pltpu.VMEM((FW, D), BF), pltpu.SemaphoreType.DMA((2,))]


def feed_forward(layer, which, weights, vecs, bfc, *acts):
    outs = [shape((LEN, D), F32), shape((LEN, D), BF), shape((LEN, FW), BF), shape((LEN, D), BF), shape((LEN, FW), BF)]
    if layer == 1:
        outs.append(shape((LEN, D), BF))
    kernel = functools.partial(feed_forward_kernel, layer)
    return run_kernel(kernel, "feed_forward", (which,), weights, (vecs, bfc), acts, outs, feed_weights(), 1e10)


def norm_back(vec, da, unit, scale, sums_ref):
    sums_ref[0:1, :] += column_sum(da * unit)
    sums_ref[1:2, :] += column_sum(da)
    return normalize_back(da, unit, scale, vec)


def feed_back_kernel(*refs):
    which_ref, own, fc_pieces, proj_pieces, refs = refs[0], refs[1:3], refs[3:7], refs[7:11], refs[11:]
    vec_ref, ins, outs, held, refs = refs[0], refs[1:6], refs[6:10], refs[10:15], refs[15:]
    (dm_ref, du_ref, dc_ref, sums_ref), (wfc_ref, wproj_ref, sems, copy_sems) = refs[:4], refs[4:]
    dh_ref, own_ref, recv_ref, x_ref, slope_ref = held
    copies = Copies(copy_sems)
    blocks = row_slices(BR)
    arriving = []
    for rows in blocks:
        arriving.append([copies.begin(part_of(src, rows), part_of(dst, rows)) for src, dst in zip(ins, held)])
        if len(arriving) == 1:
            start_fetch(which_ref, own[1:2], proj_pieces, ((wproj_ref, PROJ_BLOCKS),), sems.at[pl.ds(1, 1)], 2)
            start_fetch(which_ref, own[0:1], fc_pieces, ((wfc_ref, FC_BLOCKS),), sems.at[pl.ds(0, 1)])
    sums_ref[...] = jnp.zeros_like(sums_ref)

    for number, rows in enumerate(blocks):
        for copy in arriving[number]:
            copy.wait()
        unit, scale = normalize(x_ref[rows, :].astype(F32))
        da = own_ref[rows, :].astype(F32) + recv_ref[rows, :].astype(F32)
        dm = (dh_ref[rows, :] + norm_back(vec_ref[8:9, :], da, unit, scale, sums_ref)).astype(BF)
        dm_ref[rows, :] = dm
        copies.leave(part_of(dm_ref, rows), part_of(outs[0], rows))
        if number == 0:
            end_fetch(own[1], wproj_ref, sems.at[1])
            end_fetch(own[0], wfc_ref, sems.at[0])
        width = 512
        starts = list(range(0, FW, width))

        def up(start):
            return mm_nt(dm, wproj_ref[start : start + width, :])

        dc = None
        ahead = up(starts[0])
        for position, start in enumerate(starts):
            cols = slice(start, start + width)
            dg = ahead
            if position + 1 < len(starts):
                ahead = up(starts[position + 1])
            du = (dg * slope_ref[rows, cols].astype(F32)).astype(BF)
            du_ref[rows, cols] = du
            more = mm_nt(du, wfc_ref[:, cols])
            dc = more if dc is None else dc + more
        copies.leave(part_of(du_ref, rows), part_of(outs[1], rows))
        dc_ref[rows, :] = dc.astype(BF)
        copies.leave(part_of(dc_ref, rows), part_of(outs[2], rows))
    copies.leave(sums_ref, outs[3])
    copies.finish()


def feed_back(which, weights, vecs, *acts):
    outs = [shape((LEN, D), BF), shape((LEN, FW), BF), shape((LEN, D), BF), shape((8, D), F32)]
    return run_kernel(feed_back_kernel, "feed_back", (which,), weights, (vecs,), acts, outs, feed_weights(), 5e9)


def input_back_kernel(vec_ref, *refs):
    ins, outs, held, (dx_ref, sums_ref, copy_sems) = refs[:4], refs[4:6], refs[6:10], refs[10:]
    dh_ref, own_ref, recv_ref, x_ref = held
    copies = Copies(copy_sems)
    blocks = row_slices(BT)
    arriving = [[copies.begin(part_of(src, rows), part_of(dst, rows)) for src, dst in zip(ins, held)] for rows in blocks]
    sums_ref[...] = jnp.zeros_like(sums_ref)
    for number, rows in enumerate(blocks):
        for copy in arriving[number]:
            copy.wait()
        unit, scale = normalize(x_ref[rows, :].astype(F32))
        da = own_ref[rows, :].astype(F32) + recv_ref[rows, :].astype(F32)
        dx_ref[rows, :] = (dh_ref[rows, :] + norm_back(vec_ref[0:1, :], da, unit, scale, sums_ref)).astype(BF)
        copies.leave(part_of(dx_ref, rows), part_of(outs[0], rows))
    copies.leave(sums_ref, outs[1])
    copies.finish()


def input_back(vecs, *acts):
    outs = [shape((LEN, D), BF), shape((8, D), F32)]
    return run_kernel(input_back_kernel, "input_back", (), (), (vecs,), acts, outs, (), 1e7)


def in_three(values, spots):
    high = values.astype(BF)
    rest = values - high.astype(F32)
    middle = rest.astype(BF)
    low = (rest - middle.astype(F32)).astype(BF)
    return jnp.where(spots == 0, high, jnp.where(spots == 1, middle, jnp.where(spots == 2, low, jnp.zeros_like(low))))


def attention_back_kernel(layer, *refs):
    which_ref, own, pieces, refs = refs[0], refs[1:3], refs[3:7], refs[7:]
    vec_ref, ins, outs, held, refs = refs[0], refs[1:8], refs[8:14], refs[14:21], refs[21:]
    (dh_ref, dz_ref, dqkv_ref, da_ref, sums_ref, bias_ref), refs = refs[:6], refs[6:]
    do_ref, dk_ref, dv_ref, wqkv_ref, wout_ref, sems, copy_sems = refs
    dm_ref, own_ref, recv_ref, h_ref, qkv_ref, o_ref, lse_ref = held
    copies = Copies(copy_sems)
    blocks = row_slices(BT)
    arriving = []
    for rows in blocks:
        arriving.append([copies.begin(part_of(src, rows), part_of(dst, rows)) for src, dst in zip(ins[:4], held[:4])])
        if len(arriving) == 1:
            start_fetch(which_ref, own, pieces, ((wqkv_ref, QKV_BLOCKS), (wout_ref, OUT_BLOCKS)), sems)
    later = [copies.begin(src, dst) for src, dst in zip(ins[4:], held[4:])]
    gain = vec_ref[8 * layer + 1 : 8 * layer + 2, :]
    sums_ref[...] = jnp.zeros_like(sums_ref)
    bias_ref[...] = jnp.zeros_like(bias_ref)

    for number, rows in enumerate(blocks):
        for copy in arriving[number]:
            copy.wait()
        unit, scale = normalize(h_ref[rows, :])
        dc = own_ref[rows, :].astype(F32) + recv_ref[rows, :].astype(F32)
        dm = dm_ref[rows, :].astype(F32)
        dh = dm + norm_back(gain, dc, unit, scale, sums_ref)
        dh_ref[rows, :] = dh
        copies.leave(part_of(dh_ref, rows), part_of(outs[0], rows))
        dz = dh.astype(BF)
        dz_ref[rows, :] = dz
        copies.leave(part_of(dz_ref, rows), part_of(outs[1], rows))
        sums_ref[2:3, :] += column_sum(dz.astype(F32))
        sums_ref[3:4, :] += column_sum(dm)
        if number == 0:
            end_fetch(own[1], wout_ref, sems.at[1])
        do_ref[rows, :] = mm_nt(dz, wout_ref[...]).astype(BF)
    copies.leave(sums_ref, outs[4])
    for copy in later:
        copy.wait()

    def attend(group, carry):
        low = lower_lanes(BK)
        low_all = lower_lanes(LEN)
        spots = lax.broadcasted_iota(jnp.int32, (BK, 128), 1) % HS
        ones = jnp.where(lax.broadcasted_iota(jnp.int32, (LEN, 128), 1) % HS < 3, 1.0, 0.0).astype(BF)
        keep_diag = lax.broadcasted_iota(jnp.int32, (BK, BK), 0) <= lax.broadcasted_iota(jnp.int32, (BK, BK), 1)
        nothing = jnp.zeros((BK, 128), BF)
        key = qkv_ref[:, lane_group(3 * group + 1)]
        value = qkv_ref[:, lane_group(3 * group + 2)]
        blank = jnp.zeros_like(key)
        keys_with = (jnp.where(low_all, key, ones), jnp.where(low_all, ones, key))
        values_with = (jnp.where(low_all, value, ones), jnp.where(low_all, ones, value))
        keys_one = (jnp.where(low_all, key, blank), jnp.where(low_all, blank, key))

        def prepare(i):
            mine = slice(i * BK, (i + 1) * BK)
            query = qkv_ref[mine, lane_group(3 * group)]
            do = do_ref[mine, lane_group(group)]
            lse = in_three(-pltpu.roll(lse_ref[mine, lane_group(group)], HS, 1), spots)
            inner = do.astype(F32) * o_ref[mine, lane_group(group)].astype(F32)
            t_low = jnp.sum(jnp.where(low, inner, 0.0), axis=1, keepdims=True)
            t_high = jnp.sum(jnp.where(low, 0.0, inner), axis=1, keepdims=True)
            t = in_three(-jnp.where(low, t_high, t_low), spots)
            return (
                (jnp.where(low, query, lse), jnp.where(low, lse, query)),
                (jnp.where(low, do, t), jnp.where(low, t, do)),
                (jnp.where(low, query, nothing), jnp.where(low, nothing, query)),
                (jnp.where(low, do, nothing), jnp.where(low, nothing, do)),
            )

        def products(i, head, prepared):
            past, here = i * BK, (i + 1) * BK
            query_with, do_with = prepared[0][head], prepared[1][head]
            diag = jnp.where(keep_diag, mm_nt(keys_with[head][past:here], query_with), MASKED_SCORE)
            out = [(diag, mm_nt(values_with[head][past:here], do_with))]
            if i:
                out.append((mm_nt(keys_with[head][:past], query_with), mm_nt(values_with[head][:past], do_with)))
            return out

        units = [(i, head) for i in range(LEN // BK) for head in range(2)]
        prepared = prepare(0)
        ahead = products(0, 0, prepared)
        dq = None
        for number, (i, head) in enumerate(units):
            past, here = i * BK, (i + 1) * BK
            now, now_prepared = ahead, prepared
            if number + 1 < len(units):
                if head == 1:
                    prepared = prepare(i + 1)
                ahead = products(*units[number + 1], prepared)
            query_one, do_one = now_prepared[2][head], now_prepared[3][head]
            for rows, (score, inner) in zip((slice(past, here), slice(0, past)), now):
                p = jnp.exp(score)
                ds = (p * inner).astype(BF)
                dv = mm(p.astype(BF), do_one)
                dk = mm(ds, query_one)
                part = mm_tn(ds, keys_one[head][rows])
                dq = part if dq is None else dq + part
                if head == 0 and rows.start == past:
                    dv_ref[rows, :] = dv
                    dk_ref[rows, :] = dk
                else:
                    dv_ref[rows, :] += dv
                    dk_ref[rows, :] += dk
            if head == 1:
                dqkv_ref[past:here, lane_group(3 * group)] = (dq * 0.125).astype(BF)
                dq = None
        for i in range(NB):
            mine = slice(i * BT, (i + 1) * BT)
            one, two, three = from_pairs(
                dqkv_ref[mine, lane_group(3 * group)].astype(F32), dk_ref[mine, :], dv_ref[mine, :]
            )
            dqkv_ref[mine, lane_group(3 * group)] = one.astype(BF)
            dqkv_ref[mine, lane_group(3 * group + 1)] = two.astype(BF)
            dqkv_ref[mine, lane_group(3 * group + 2)] = three.astype(BF)
        return carry

    lax.fori_loop(0, PAIRS, attend, 0)

    copies.leave(dqkv_ref, outs[2])
    end_fetch(own[0], wqkv_ref, sems.at[0])
    for rows in row_slices(512):
        da_ref[rows, :] = mm_nt(dqkv_ref[rows, :], wqkv_ref[...]).astype(BF)
        copies.leave(part_of(da_ref, rows), part_of(outs[3], rows))
        bias_ref[0:1, :] += column_sum(dqkv_ref[rows, :].astype(F32))
    copies.leave(bias_ref, outs[5])
    copies.finish()


def attention_back(layer, which, weights, vecs, *acts):
    outs = [
        shape((LEN, D), F32),
        shape((LEN, D), BF),
        shape((LEN, QW), BF),
        shape((LEN, D), BF),
        shape((8, D), F32),
        shape((8, QW), F32),
    ]
    scratch = [
        pltpu.VMEM((LEN, HALF), BF),
        pltpu.VMEM((LEN, 128), F32),
        pltpu.VMEM((LEN, 128), F32),
        pltpu.VMEM((D, QW), BF),
        pltpu.VMEM((HALF, D), BF),
        pltpu.SemaphoreType.DMA((2,)),
    ]
    kernel = functools.partial(attention_back_kernel, layer)
    return run_kernel(kernel, "attention_back", (which,), weights, (vecs,), acts, outs, scratch, 2.2e10)


def feed_grad_kernel(*refs):
    ins, outs, held, refs = refs[:4], refs[4:10], refs[10:14], refs[14:]
    grads, (square_ref, bias_ref, copy_sems) = refs[:4], refs[4:]
    copies = Copies(copy_sems)
    g_ref, dm_ref, c_ref, du_ref = held
    bias_ref[...] = jnp.zeros_like(bias_ref)
    halves = [pl.ds(0, D), pl.ds(D, D)]
    arriving = []
    for half in range(2):
        arriving.append(copies.begin(ins[0].at[:, halves[half]], g_ref.at[:, halves[half]]))
        if half == 0:
            arriving.append(copies.begin(ins[1], dm_ref))
        arriving.append(copies.begin(ins[3].at[:, halves[half]], du_ref.at[:, halves[half]]))
        if half == 0:
            arriving.append(copies.begin(ins[2], c_ref))
    total = None
    for number in range(4):
        for copy in (arriving[0:2], arriving[2:4], arriving[4:5], arriving[5:6])[number]:
            copy.wait()
        cols = slice(number // 2 * D, (number // 2 + 1) * D)
        if number % 2 == 0:
            grad = mm_tn(g_ref[:, cols], dm_ref[...])
        else:
            grad = mm_tn(c_ref[...], du_ref[:, cols])
            bias_ref[0:1, cols] = column_sum(du_ref[:, cols].astype(F32))
        grads[number][...] = grad.astype(BF)
        copies.leave(grads[number], outs[number])
        square = column_sum(grad * grad)
        total = square if total is None else total + square
    square_ref[...] = jnp.zeros_like(square_ref)
    square_ref[0:1, :] = total
    copies.leave(square_ref, outs[4])
    copies.leave(bias_ref, outs[5])
    copies.finish()


def feed_grad(*acts):
    outs = [shape((D, D), BF)] * 4 + [shape((8, D), F32), shape((8, FW), F32)]
    return run_kernel(feed_grad_kernel, "feed_grad", (), (), (), acts, outs, (), 1e10)


def attention_grad_kernel(*refs):
    ins, outs, held, refs = refs[:4], refs[4:7], refs[7:11], refs[11:]
    targets, square_ref, copy_sems = refs[:2], refs[2], refs[3]
    copies = Copies(copy_sems)
    o_ref, dz_ref, a_ref, dqkv_ref = held
    arriving = [copies.begin(ins[number], held[number]) for number in (2, 3, 0, 1)]
    square_ref[...] = jnp.zeros_like(square_ref)
    for part, target in enumerate(targets):
        half = slice(part * HALF, (part + 1) * HALF)

        def place(grad, rows, cols):
            square_ref[0:1, 0:HALF] += column_sum(grad * grad)
            target[rows, cols] = grad.astype(BF)

        if part == 0:
            arriving[0].wait()
            arriving[1].wait()
        top = mm_tn(a_ref[:, half], dqkv_ref[...])
        if part == 0:
            arriving[2].wait()
            arriving[3].wait()
        out = mm_tn(o_ref[...], dz_ref[:, half])
        place(top[:, 0:HALF], slice(0, HALF), slice(0, HALF))
        place(top[:, HALF:D], slice(0, HALF), slice(HALF, D))
        for start, grad in ((HALF, top[:, D:]), (HALF + SIDE, out)):
            place(grad[:SIDE], slice(start, start + SIDE), slice(0, HALF))
            place(grad[SIDE:], slice(start, start + SIDE), slice(HALF, D))
        copies.leave(target, outs[part])
    copies.leave(square_ref, outs[2])
    copies.finish()


def attention_grad(*acts):
    outs = [shape((D, D), BF), shape((D, D), BF), shape((8, D), F32)]
    return run_kernel(attention_grad_kernel, "attention_grad", (), (), (), acts, outs, (), 5e9)


def pack_small_kernel(core_ref, *refs):
    ins, (small_ref, square_ref) = refs[:12], refs[12:]
    small_ref[...] = jnp.zeros_like(small_ref)
    lower = core_ref[0] == 0
    total = jnp.zeros((8, D), F32)
    for layer in range(2):
        bias_qkv, bias_fc, first, second, squares_feed, squares_attention = (ref[...] for ref in ins[6 * layer : 6 * layer + 6])

        def side(values):
            return jnp.where(lower, values[:, :HALF], values[:, HALF:])

        small_ref[layer, 0:1, :] = bias_fc[0:1, 0:D]
        small_ref[layer, 1:2, :] = bias_fc[0:1, D:]
        small_ref[layer, 2:3, :] = bias_qkv[0:1, 0:D]
        small_ref[layer, 3:4, 0:HALF] = bias_qkv[0:1, D:]
        rows = (first[0:1], second[0:1], first[1:2], second[2:3], second[1:2], second[3:4])
        for number, row in enumerate(rows):
            line, right = divmod(number + 1, 2)
            small_ref[layer, 3 + line : 4 + line, right * HALF : (right + 1) * HALF] = side(row)
        total = total + squares_feed + squares_attention
        total = total + small_ref[layer, 0:8, :] * small_ref[layer, 0:8, :]
    square_ref[...] = jnp.broadcast_to(jnp.sum(total, keepdims=True), (8, 128))


def pack_small(core, *parts):
    vmem = pl.BlockSpec(memory_space=pltpu.VMEM)
    return pl.pallas_call(
        pack_small_kernel,
        in_specs=[pl.BlockSpec(memory_space=pltpu.SMEM)] + [vmem] * 12,
        out_specs=[vmem] * 2,
        out_shape=[shape((2, 16, D), F32), shape((8, 128), F32)],
        compiler_params=params(),
        cost_estimate=cost(1e5, 1e5),
        name="pack_small",
    )(core, *parts)


def unpack_small(rows):
    tail = rows[3:7].reshape(8, HALF)
    bias = jnp.concatenate([rows[2], tail[0]])
    return bias, rows[0:2].reshape(FW), tail[1:3], tail[3:7]


def weigh_kernel(rows, roles_ref, mine_ref, across_ref, above_ref, *refs):
    sources, refs = refs[:8], refs[8:]
    if len(refs) == 6:
        (small_ref, other_ref, keep_ref, aside_ref, held_ref, sems) = refs
    else:
        (other_ref, keep_ref, aside_ref, held_ref, sems) = refs
        small_ref = None
    mine, home = roles_ref[0], roles_ref[1]

    def bring(slot, one, two):
        for number, source in enumerate((one, two)):
            pltpu.make_async_copy(source.at[rows], held_ref.at[2 * slot + number], sems.at[slot]).start()

    for layer in range(2):
        first, first_there, second, second_there = sources[4 * layer : 4 * layer + 4]

        @pl.when(mine == layer)
        def _(second=second, second_there=second_there):
            bring(2, second, second_there)

        for role in range(2):

            @pl.when((home == 1) & ((mine == layer) == (role == 1)))
            def _(role=role, first=first, first_there=first_there):
                bring(role, first, first_there)

    count = held_ref.shape[1]

    def total(slot, weight_ref):
        both = held_ref.at[pl.ds(2 * slot, 2)]
        pltpu.make_async_copy(both, both, sems.at[slot]).wait()
        return mine_ref[0:1, 0:1] * held_ref[2 * slot].astype(F32) + weight_ref[0:1, 0:1] * held_ref[
            2 * slot + 1
        ].astype(F32)

    @pl.when(home == 1)
    def _():
        for slot, target in ((0, other_ref), (1, keep_ref)):
            target[0:count, :] = total(slot, across_ref).astype(target.dtype)
            if small_ref is not None:
                target[count:, :] = jnp.where(mine == slot, small_ref[1], small_ref[0]).astype(target.dtype)
        aside_ref[0:count, :] = total(2, above_ref).astype(BF)
        if small_ref is not None:
            aside_ref[count:, :] = jnp.zeros((16, D), BF)

    @pl.when(home == 0)
    def _():
        other_ref[0:count, :] = total(2, above_ref).astype(BF)
        if small_ref is not None:
            other_ref[count:, :] = jnp.zeros((16, D), BF)


def weigh(rows, roles, weights, layers, small=None):
    count = rows.stop - rows.start
    tall = count + (0 if small is None else 16)
    vmem, smem, hbm = (pl.BlockSpec(memory_space=kind) for kind in (pltpu.VMEM, pltpu.SMEM, pl.ANY))
    return pl.pallas_call(
        functools.partial(weigh_kernel, pl.ds(rows.start, count)),
        out_shape=[shape((tall, D), BF), shape((tall, D), F32), shape((tall, D), BF)],
        in_specs=[smem] + [vmem] * 3 + [hbm] * 8 + ([] if small is None else [vmem]),
        out_specs=[vmem] * 3,
        scratch_shapes=[pltpu.VMEM((6, count, D), BF), pltpu.SemaphoreType.DMA((3,))],
        compiler_params=params(SMALL_VMEM_BYTES),
        cost_estimate=cost(1e7, 1e7),
        name="weigh",
    )(roles, *weights, *layers[0], *layers[1], *(() if small is None else (small,)))


def noise_rows():
    sizes = (D * QW, QW, HALF * D, D * FW, FW, FW * D, 2 * HALF, 4 * HALF)
    starts = [0]
    for size in sizes:
        starts.append(starts[-1] + size // 128)
    return starts


NOISE_ROWS = noise_rows()


def bring_noise(noise_ref, begin, raw_ref, sem):
    copy = pltpu.make_async_copy(noise_ref.at[pl.ds(begin, raw_ref.shape[0])], raw_ref, sem)
    copy.start()
    return copy


def put_noised(target, block, rows, col, wide_ref, first, denominator):
    scale = NOISE_MULT * CLIP_FRACTION * math.sqrt(LEN * FF * D)
    per = target.shape[1] // 128
    tall = rows.stop - rows.start
    for tile in range(block.shape[1] // 128):
        place = col // 128 + tile
        noise = wide_ref[pl.ds(first + per * rows.start + place, tall, stride=per), :]
        value = block[:, tile * 128 : (tile + 1) * 128].astype(F32)
        target[rows, place * 128 : (place + 1) * 128] = (value + scale * noise) / denominator


def finish_feed_kernel(columns, denominator, home_ref, *refs):
    own, swapped = refs[:2], refs[2:4]
    noise_ref, grad_ref, raw_ref, wide_ref, sem = refs[4:]
    first = NOISE_ROWS[3 if columns else 5]
    begin = first // 16 * 16
    bring_noise(noise_ref, begin, raw_ref, sem).wait()
    wide_ref[...] = raw_ref[...].astype(F32)
    step = D // 2

    def run(parts):
        for number, part in enumerate(parts):
            for index in range(2):
                row, col = (index * step, number * D) if columns else (number * D + index * step, 0)
                block = part[index][0:step, :]
                put_noised(grad_ref, block, slice(row, row + step), col, wide_ref, first - begin, denominator)

    @pl.when(home_ref[0] == 1)
    def _():
        run((own, swapped))

    @pl.when(home_ref[0] == 0)
    def _():
        run((swapped, own))


def finish_attention_kernel(denominator, home_ref, *refs):
    own, swapped = refs[0:2], refs[2:4]
    noise_ref, qkv_ref, out_ref, raw_ref, wide_ref, sem = refs[4:]
    bring_noise(noise_ref, 0, raw_ref, sem).wait()
    wide_ref[...] = raw_ref[...].astype(F32)

    def run(parts):
        for number, (one, two) in enumerate(parts):
            start = number * HALF
            put_noised(qkv_ref, one[...], slice(start, start + HALF), 0, wide_ref, NOISE_ROWS[0], denominator)
            for index in range(2):
                cols = slice(index * HALF, (index + 1) * HALF)
                rows = slice(start + index * SIDE, start + (index + 1) * SIDE)
                put_noised(qkv_ref, two[0:SIDE, cols], rows, D, wide_ref, NOISE_ROWS[0], denominator)
                rows = slice(index * SIDE, (index + 1) * SIDE)
                put_noised(out_ref, two[SIDE : 2 * SIDE, cols], rows, start, wide_ref, NOISE_ROWS[2], denominator)

    @pl.when(home_ref[0] == 1)
    def _():
        run((own, swapped))

    @pl.when(home_ref[0] == 0)
    def _():
        run((swapped, own))


def finish(kernel, denominator, home, own, swapped, noise, numbers, shapes, name):
    smem, vmem, hbm = (pl.BlockSpec(memory_space=kind) for kind in (pltpu.SMEM, pltpu.VMEM, pl.ANY))
    begin, end = NOISE_ROWS[numbers[0]] // 16 * 16, -(-NOISE_ROWS[numbers[-1] + 1] // 16) * 16
    return pl.pallas_call(
        functools.partial(kernel, denominator),
        out_shape=[shape(dims, F32) for dims in shapes],
        in_specs=[smem] + [vmem] * (2 * len(own)) + [hbm],
        out_specs=[vmem] * len(shapes),
        scratch_shapes=[
            pltpu.VMEM((end - begin, 128), BF),
            pltpu.VMEM((end - begin, 128), F32),
            pltpu.SemaphoreType.DMA,
        ],
        compiler_params=params(),
        cost_estimate=cost(1e7, 1.6e7),
        name=name,
    )(home, *own, *swapped, noise)


def send(values, route):
    sections, ranks = lax.axis_size("section"), lax.axis_size("dp")
    pairs = []
    for section in range(sections):
        for rank in range(ranks):
            target = route(section, rank // 2, rank % 2)
            if target is not None:
                to_section, to_pair, to_core = target
                pairs.append((section * ranks + rank, to_section * ranks + to_pair * 2 + to_core))
    return lax.ppermute(values, ("section", "dp"), pairs)


def swap_cores(values):
    return send(values, lambda s, z, c: (s, z, 1 - c))


def is_home(s, c):
    return s % 2 == c


def after(values, *others):
    return lax.optimization_barrier((values, *others))[0]


def local(
    inputs,
    cotangent,
    included,
    qkv_weight,
    qkv_bias,
    out_weight,
    fc_weight,
    fc_bias,
    proj_weight,
    norm_gains,
    shifts,
    noise,
):
    clip_norm = CLIP_FRACTION * math.sqrt(LEN * FF * D)
    section = lax.axis_index("section")
    rank = lax.axis_index("dp")
    ranks = lax.axis_size("dp")
    row, half = section // 2, section % 2
    place, core = rank // 2, rank % 2
    home = half == core
    on_top = row == 0
    flip = home.astype(jnp.int32).reshape(1)
    denominator = SAMPLE_RATE * inputs.shape[0] * ranks

    side = place % 2

    def piece_of(weight, number):
        tall = weight.shape[0] // 2
        if number is None:
            return lax.dynamic_slice_in_dim(weight, side * tall, tall, 0)
        return weight[number * tall : (number + 1) * tall]

    def attention_piece(number):
        qkv = piece_of(qkv_weight, number)
        tail = jnp.concatenate([qkv[:SIDE, D:], qkv[SIDE:, D:]], axis=1)
        return jnp.concatenate([qkv[:, :D], tail, piece_of(out_weight, number)])

    fc_piece = piece_of(fc_weight, None)
    fc_piece = jnp.concatenate([fc_piece[:, :D], fc_piece[:, D:]])

    def near(piece):
        return send(piece, lambda s, z, c: (s ^ 2, z, c) if is_home(s, c) else (s ^ 1, z, 1 - c))

    def far(one, two):
        far_one = send(one, lambda s, z, c: (s ^ 1, z, c) if is_home(s, c) else None)
        return far_one, send(two, lambda s, z, c: None if is_home(s, c) else (s ^ 2, z, c))

    def next_plane(one):
        return send(one, lambda s, z, c: (s, z ^ 1, c))

    fc_one = near(fc_piece)
    *parts, fc_one = lax.optimization_barrier((attention_piece(0), attention_piece(1), fc_one))
    attention_pieces = tuple(near(part) for part in parts)
    fc_two = next_plane(fc_one)
    *parts, one, two = lax.optimization_barrier((*(piece_of(proj_weight, i) for i in range(2)), *attention_pieces))
    attention_pieces = (one, two)
    attention_far = far(*attention_pieces)
    proj_pieces = tuple(near(part) for part in parts)
    fc_again, *attention_far = lax.optimization_barrier((fc_one, *attention_far))
    fc_far = far(fc_again, fc_two)
    proj_pieces = (*proj_pieces, *far(*proj_pieces))
    attention_pieces = (*attention_pieces, *attention_far)
    attention_weights = (qkv_weight, out_weight, *attention_pieces)

    def which_of(layer):
        kind = jnp.where(row == layer, jnp.where(home, 0, 1), jnp.where(home, 1, 2))
        nothing = jnp.zeros_like(side)
        return [jnp.stack([kind, first, nothing]).astype(jnp.int32) for first in (nothing, side)]

    which_attention, which_feed = zip(which_of(0), which_of(1))

    def own_sequence(values):
        mine = lax.dynamic_index_in_dim(values, half, 0, keepdims=False)
        theirs = swap_cores(mine)
        return jnp.where(core == row, mine, theirs)

    small = jnp.concatenate([qkv_bias, fc_bias, norm_gains.reshape(-1), shifts.reshape(-1)]).reshape(1, -1)
    others = [send(small, lambda s, z, c, bits=bits: (s ^ bits, z, c)) for bits in (1, 2, 3)]
    x0 = own_sequence(inputs)
    cot = own_sequence(cotangent)
    drawn = own_sequence(jnp.broadcast_to(included.astype(F32)[:, None, None], (2, 8, 128)))[0, 0]
    x0, cot = lax.optimization_barrier((x0, cot))
    small_all = jnp.concatenate([small] + others, axis=0)
    small_all = jnp.where(half == 0, small_all, jnp.concatenate([small_all[i : i + 1] for i in (1, 0, 3, 2)]))
    small_all = jnp.where(on_top, small_all, jnp.concatenate([small_all[2:], small_all[:2]]))
    small_all = small_all.reshape(2, 2, -1)
    bias = jnp.where(core == 0, small_all[:, 0], small_all[:, 1])
    bqkv, bfc = bias[:, :QW], bias[:, QW : QW + FW]
    vecs = small_all[:, :, QW + FW :].reshape(2, 2, 6, HALF).transpose(0, 2, 1, 3).reshape(2, 6, D)
    vecs = jnp.pad(vecs, ((0, 0), (0, 2), (0, 0))).reshape(16, D)

    shapes = ((D, QW), (QW,), (HALF, D), (D, FW), (FW,), (FW, D), (2, HALF), (4, HALF))
    a0, qkv0, o0, lse0, part = attention_forward(0, which_attention[0], attention_weights, vecs, bqkv, x0)
    part, *fc_far = lax.optimization_barrier((part, *fc_far))
    feed_weights_all = (fc_weight, proj_weight, fc_one, fc_two, *fc_far, *proj_pieces)
    part_theirs = swap_cores(part)
    h0, c0, g0, part_two, slope0 = feed_forward(
        0, which_feed[0], feed_weights_all, vecs, bfc, x0, part, part_theirs
    )
    a1, qkv1, o1, lse1, part, x1 = attention_forward(
        1, which_attention[1], attention_weights, vecs, bqkv, h0, part_two, swap_cores(part_two)
    )
    h1, c1, g1, part_two, du1, dc = feed_forward(
        1, which_feed[1], feed_weights_all, vecs, bfc, x1, part, swap_cores(part), cot
    )
    dc_theirs = swap_cores(dc)

    def spread(block_for):
        received = []
        for step in range(2):
            block = block_for(2 * core + (step ^ half))
            received.append(send(block, lambda s, z, c, step=step: (2 * c + (step ^ (s % 2)), z, s // 2)))
        return received

    def over_x(values):
        return send(values, lambda s, z, c: None if is_home(s, c) else (s ^ 1, z, c))

    def over_y(layer, values):
        return send(values, lambda s, z, c: None if s // 2 == layer else (s ^ 2, z, c))

    *grads1, squares_feed1, bias_fc1 = feed_grad(g1, cot, c1, du1)
    dc, dc_theirs, *grads1 = lax.optimization_barrier((dc, dc_theirs, *grads1))
    proj_x1, fc_x1, proj_y1 = over_x(grads1[0]), over_x(grads1[1]), over_y(1, grads1[2])
    dh1, dz1, dqkv1, da, sums1, bias_qkv1 = attention_back(
        1, which_attention[1], attention_weights, vecs, cot, dc, dc_theirs, h1, qkv1, o1, lse1
    )
    da, proj_x1, fc_x1, proj_y1 = lax.optimization_barrier((da, proj_x1, fc_x1, proj_y1))
    da_theirs = swap_cores(da)
    fc_y1 = over_y(1, grads1[3])
    first1, second1, squares_attention1 = attention_grad(o1, dz1, a1, dqkv1)
    da, da_theirs, first1 = lax.optimization_barrier((da, da_theirs, first1))
    dm0, du0, dc, first_sums1 = feed_back(which_feed[0], feed_weights_all, vecs, dh1, da, da_theirs, x1, slope0)
    dc, fc_y1 = lax.optimization_barrier((dc, fc_y1))
    dc_theirs = swap_cores(dc)
    attention_x1 = over_x(first1)
    *grads0, squares_feed0, bias_fc0 = feed_grad(g0, dm0, c0, du0)
    dc, dc_theirs, attention_x1, *grads0 = lax.optimization_barrier((dc, dc_theirs, attention_x1, *grads0))
    proj_x0, fc_x0, proj_y0 = over_x(grads0[0]), over_x(grads0[1]), over_y(0, grads0[2])
    attention_y1 = over_y(1, second1)
    dh0, dz0, dqkv0, da, sums0, bias_qkv0 = attention_back(
        0, which_attention[0], attention_weights, vecs, dm0, dc, dc_theirs, h0, qkv0, o0, lse0
    )
    da, proj_x0, fc_x0, proj_y0, attention_y1 = lax.optimization_barrier((da, proj_x0, fc_x0, proj_y0, attention_y1))
    da_theirs = swap_cores(da)
    fc_y0 = over_y(0, grads0[3])
    first0, second0, squares_attention0 = attention_grad(o0, dz0, a0, dqkv0)
    dx0, first_sums0 = input_back(vecs, dh0, da, da_theirs, x0)
    small_pair, squares = pack_small(
        core.astype(jnp.int32).reshape(1),
        *(bias_qkv0, bias_fc0, first_sums0, sums0, squares_feed0, squares_attention0),
        *(bias_qkv1, bias_fc1, first_sums1, sums1, squares_feed1, squares_attention1),
    )
    small_there = send(small_pair, lambda s, z, c: None if is_home(s, c) else (s ^ 1, z, c))

    squares = squares + swap_cores(squares)
    factor = drawn * jnp.minimum(1.0, clip_norm / jnp.sqrt(squares))
    across = send(factor, lambda s, z, c: (s ^ 1, z, 1 - c) if is_home(s, c) else None)
    above = send(factor, lambda s, z, c: (s ^ 2, z, c))
    factor, across, above, fc_y0 = lax.optimization_barrier((factor, across, above, fc_y0))
    weights = (factor, across, above)
    roles = jnp.stack([row, home]).astype(jnp.int32)

    def send_first(first, small_pair):
        there = over_x(jnp.concatenate([first, small_pair[:, :8].reshape(16, D).astype(BF)]))
        small = there[D:].astype(F32).reshape(2, 8, D)
        small = jnp.where(home, weights[0][0, 0] * small_pair[:, :8] + weights[1][0, 0] * small, 0.0)
        return there, jnp.pad(small, ((0, 0), (0, 8), (0, 0)))


    proj0, proj1 = (grads0[0], proj_x0, grads0[2], proj_y0), (grads1[0], proj_x1, grads1[2], proj_y1)
    fc0, fc1 = (grads0[1], fc_x0, grads0[3], fc_y0), (grads1[1], fc_x1, grads1[3], fc_y1)
    attention1 = (first1, attention_x1, second1, attention_y1)

    token_rows = LEN // lax.axis_size("section")

    def last_output(part_two):
        return (h1 + (part_two.astype(F32) + swap_cores(part_two).astype(F32)) + vecs[13:14]).astype(BF)

    def exchange_outputs(y1, dx0):
        both_out = jnp.concatenate([x1, y1], axis=1)

        def block_for(number):
            columns = lax.dynamic_slice_in_dim(both_out, number * HALF, HALF, 1)
            rows = lax.dynamic_slice_in_dim(dx0, number * token_rows, token_rows, 0)
            return jnp.concatenate([columns, rows[:, :HALF], rows[:, HALF:]])

        return spread(block_for)

    def ordered_outputs(outputs):
        outputs = in_order(*outputs)
        rows = (outputs[:, LEN : LEN + token_rows], outputs[:, LEN + token_rows :])
        return outputs[:, :LEN], jnp.concatenate(rows, axis=2)

    def in_order(first, second):
        return jnp.where(half == 0, jnp.stack([first, second]), jnp.stack([second, first]))

    places = ranks // 2
    middle = places // 2

    def to_middle(step):
        def route(s, z, c):
            if z == step:
                return (s, z + 1, c)
            if z == places - 1 - step:
                return (s, z - 1, c)
            return None

        return route

    def at_middle(s, z, c):
        return (s, places - 1 - z, c) if z in (middle - 1, middle) else None

    def from_middle(step):
        def route(s, z, c):
            if z == middle - 1 - step:
                return (s, z - 1, c)
            if z == middle + step:
                return (s, z + 1, c)
            return None

        return route

    def add(left, right):
        return (left.astype(F32) + right.astype(F32)).astype(BF)

    def weigh_stage(args):
        other, keep, aside = weigh(*args)
        arrived = send(other, lambda s, z, c: (s ^ 2, z, c) if is_home(s, c) else (s ^ 1, z, 1 - c))
        aside = send(aside, lambda s, z, c: (s, z, 1 - c) if is_home(s, c) else None)
        return keep, aside, arrived

    def weigh_end(held):
        keep, aside, arrived = held
        return (jnp.where(home, keep, aside.astype(F32)) + arrived.astype(F32)).astype(BF)

    def chain_stage(hop):
        def stage(held):
            total = add(*held) if len(held) == 2 else weigh_end(held)
            return total, send(total, hop)

        return stage

    def spread_stage(step):
        def stage(held):
            total, arrived = held
            if step == 0:
                total = add(total, arrived)
            else:
                takes = (place == middle - 1 - step) | (place == middle + step)
                total = jnp.where(takes, arrived, total)
            return total, send(total, from_middle(step))

        return stage

    def last_stage(held):
        total, arrived = held
        if middle > 1:
            takes = (place == 0) | (place == places - 1)
            total = jnp.where(takes, arrived, total)
        else:
            total = add(total, arrived)
        return total, swap_cores(total)

    hops = [to_middle(step) for step in range(middle - 1)] + [at_middle]
    stages = [weigh_stage] + [chain_stage(hop) for hop in hops]
    stages += [spread_stage(step) for step in range(middle - 1)] + [last_stage]

    chunk = D // 2

    noise_flat = noise.reshape(-1, 128)

    def small_noise(number, dims):
        first = NOISE_ROWS[number] * 128
        return noise[first : first + math.prod(dims)].reshape(dims).astype(F32)

    def finish_proj(one, two):
        return finish(
            functools.partial(finish_feed_kernel, False), denominator, flip, *zip(one, two), noise_flat, (5,), ((FW, D),), "finish_feed"
        )[0]

    def finish_fc(one, two):
        return finish(
            functools.partial(finish_feed_kernel, True), denominator, flip, *zip(one, two), noise_flat, (3,), ((D, FW),), "finish_feed"
        )[0]

    if middle == 2:
        edge = (place == 0) | (place == places - 1)

        def to_next(s, z, c):
            return (s, z ^ 1, c)

        count = 6
        begun, sums, lows, totals, ready = ({} for _ in range(5))
        outer, last = None, None

        def tie(*values):
            if last is None or last[1] not in last[0]:
                return values if len(values) > 1 else values[0]
            store, name = last
            *values, store[name] = lax.optimization_barrier((*values, store[name]))
            return values if len(values) > 1 else values[0]

        def begin(group, pair, *small):
            begun[group], begun[group, 1], begun[group, 2] = weigh_stage(
                (slice(0, D), roles, tie(*weights), pair, *small)
            )
            return begun, group

        attention_x0, small_sum = send_first(first0, small_pair)
        last = begin(0, (proj0, proj1))
        last = begin(1, (fc0, fc1))
        second0 = tie(second0)
        attention_y0 = over_y(0, second0)
        inners = {}
        for tick in range(count + 4):
            old_outer = outer
            if 0 <= tick - 3 < count:
                totals[tick - 3] = add(tie(lows.pop(tick - 3)), inners.pop(tick - 3))
                last = totals, tick - 3
            if tick < count and tick % 2 == 0:
                group = tick // 2
                total = weigh_end((tie(begun.pop(group)), begun.pop((group, 1)), begun.pop((group, 2))))
                sums[tick], sums[tick + 1] = total[:chunk], total[chunk:]
                last = sums, tick
            inward, outward = sums.get(tick), totals.get(tick - 3)
            if inward is not None and outward is not None:
                tall = [inward.shape[0], outward.shape[0]]
                padded = [jnp.pad(part, ((0, max(tall) - part.shape[0]), (0, 0))) for part in (inward, outward)]
                outer = send(jnp.where(edge, *padded), to_next)
                outer = (outer[: tall[0]], outer[: tall[1]])
            else:
                outer = (
                    None if inward is None else send(inward, to_middle(0)),
                    None if outward is None else send(outward, from_middle(0)),
                )
            if 0 <= tick - 1 < count:
                lows[tick - 1] = add(tie(sums.pop(tick - 1)), old_outer[0])
                last = lows, tick - 1
                inners[tick - 1] = send(lows[tick - 1], at_middle)
            if 0 <= tick - 4 < count:
                total = tie(totals.pop(tick - 4))
                if tick == count + 3:
                    total, layer_out, input_grad = lax.optimization_barrier(
                        (total, *ordered_outputs(outputs))
                    )
                ready[tick - 4] = jnp.where(edge, old_outer[1], total)
                last = ready, tick - 4
            if tick == 2:
                attention_x0, attention_y0, small_sum = tie(attention_x0, attention_y0, small_sum)
                attention0 = (first0, attention_x0, second0, attention_y0)
                last = begin(2, (attention0, attention1), small_sum)
            if tick == 2:
                y1 = last_output(tie(part_two))
            if tick == 4:
                outputs = exchange_outputs(*tie(y1, dx0))
            if tick == 6:
                proj_grad = finish_proj(*((ready[i], swap_cores(ready[i])) for i in (0, 1)))
            if tick == 8:
                proj_grad = tie(proj_grad)
                fc_grad = finish_fc(*((ready[i], swap_cores(ready[i])) for i in (2, 3)))
            if tick == 9:
                fc_grad = tie(fc_grad)
        jobs = [None] * 4 + [(ready[i], swap_cores(ready[i])) for i in (4, 5)]
        small_own, small_swapped = jobs[5]
        stages = []
    else:
        attention_x0, small_sum = send_first(first0, small_pair)
        attention0 = (first0, attention_x0, second0, over_y(0, second0))
        jobs = []
        for pair in ((proj0, proj1), (fc0, fc1), (attention0, attention1)):
            jobs += [(slice(i * chunk, (i + 1) * chunk), roles, weights, pair) for i in range(2)]
        jobs[5] += (small_sum,)
        layer_out, input_grad = ordered_outputs(exchange_outputs(last_output(part_two), dx0))
    for tick in range(len(jobs) + len(stages) - 1 if stages else 0):
        for stage in reversed(range(len(stages))):
            index = tick - stage
            if 0 <= index < len(jobs):
                held = jobs[index]
                jobs[index] = stages[stage](held)
    if stages:
        proj_grad, fc_grad = finish_proj(*jobs[0:2]), finish_fc(*jobs[2:4])
        small_own, small_swapped = jobs[5]
    attention = jobs[4:]
    own, swapped = zip(*attention)
    qkv_grad, out_grad = finish(
        finish_attention_kernel, denominator, flip, own, swapped, noise_flat, (0, 2), ((D, QW), (HALF, D)), "finish_attention"
    )
    small_sum = jnp.where(home, small_own[chunk:], small_swapped[chunk:]).astype(F32)
    small_done = [
        (part + NOISE_MULT * clip_norm * small_noise(number, part.shape)) / denominator
        for part, number in zip(unpack_small(small_sum), (1, 4, 6, 7))
    ]
    return (
        layer_out,
        input_grad,
        qkv_grad,
        small_done[0],
        out_grad,
        fc_grad,
        small_done[1],
        proj_grad,
        small_done[2],
        small_done[3],
    )


def solution(mesh):
    return jax.shard_map(
        local,
        mesh=mesh,
        in_specs=(
            P("dp", None, None),
            P("dp", None, None),
            P("dp"),
            P(None, "section"),
            P("section"),
            P("section", None),
            P(None, "section"),
            P("section"),
            P("section", None),
            P(None, "section"),
            P(None, "section"),
            P("section"),
        ),
        out_specs=(
            P("dp", None, "section"),
            P("dp", "section", None),
            P(None, "section"),
            P("section"),
            P("section", None),
            P(None, "section"),
            P("section"),
            P("section", None),
            P(None, "section"),
            P(None, "section"),
        ),
        check_vma=False,
    )
```

```python
import functools
import math

import jax
import jax.numpy as jnp
from jax import lax
from jax.experimental import pallas as pl
from jax.experimental.pallas import tpu as pltpu
from jax.sharding import PartitionSpec as P

D = 768
FF = 3072
HS = 64
LEN = 1024
HALF = D // 2
QW = 3 * HALF
FW = FF // 2
PAIRS = HALF // 128
BT = 256
NB = LEN // BT
BQ = 256
BR = 512
BK = 256

CLIP_FRACTION = 0.05
NOISE_MULT = 0.001
SAMPLE_RATE = 0.5
NORM_EPS = 1e-05
MASKED_SCORE = -1e30
VMEM_BYTES = 50 * 1024 * 1024
SMALL_VMEM_BYTES = 36 * 1024 * 1024

BF = jnp.bfloat16
F32 = jnp.float32


def mm(left, right):
    return lax.dot_general(left, right, (((1,), (0,)), ((), ())), preferred_element_type=F32)


def mm_nt(left, right):
    return lax.dot_general(left, right, (((1,), (1,)), ((), ())), preferred_element_type=F32)


def mm_tn(left, right):
    return lax.dot_general(left, right, (((0,), (0,)), ((), ())), preferred_element_type=F32)


def normalize(values):
    center = values - jnp.mean(values, axis=-1, keepdims=True)
    spread = jnp.mean(center * center, axis=-1, keepdims=True)
    scale = lax.rsqrt(spread + NORM_EPS)
    return center * scale, scale


def normalize_back(grad, unit, scale, gain):
    inner = grad * gain
    mean_inner = jnp.mean(inner, axis=-1, keepdims=True)
    mean_cross = jnp.mean(inner * unit, axis=-1, keepdims=True)
    return scale * (inner - mean_inner - unit * mean_cross)


def column_sum(values):
    return jnp.sum(values, axis=0, keepdims=True)


def block_rows(index):
    return pl.ds(pl.multiple_of(index * BT, BT), BT)


def lane_group(index, width=128):
    return pl.ds(pl.multiple_of(index * 128, 128), width)


def lower_lanes(rows=BT):
    return lax.broadcasted_iota(jnp.int32, (rows, 128), 1) < HS


def to_pairs(block, group):
    low = lower_lanes()
    start = 3 * 128 * group
    one, two, three = (block[:, start + 128 * i : start + 128 * (i + 1)] for i in range(3))
    query = jnp.where(low, one, two)
    key = pltpu.roll(jnp.where(low, three, one), HS, 1)
    value = jnp.where(low, two, three)
    return query, key, value


def from_pairs(query, key, value):
    low = lower_lanes()
    turned = pltpu.roll(key, HS, 1)
    return jnp.where(low, query, turned), jnp.where(low, value, query), jnp.where(low, turned, value)


class Copies:
    def __init__(self, sems):
        self.sems, self.used, self.left = sems, 0, []

    def begin(self, source, target):
        copy = pltpu.make_async_copy(source, target, self.sems.at[self.used])
        self.used += 1
        copy.start()
        return copy

    def leave(self, source, target):
        self.left.append(self.begin(source, target))

    def finish(self):
        for copy in self.left:
            copy.wait()


COPIES = 64


def row_slices(tall):
    return [slice(start, start + tall) for start in range(0, LEN, tall)]


def part_of(ref, rows):
    return ref.at[pl.ds(rows.start, rows.stop - rows.start)]


def start_fetch(which_ref, own, pieces, parts, sems, lower=1):
    @pl.when(which_ref[0] == 0)
    def _():
        for number, (target, _) in enumerate(parts):
            pltpu.make_async_copy(own[number], target, sems.at[number]).start()

    for kind in (1, 2):

        @pl.when(which_ref[0] == kind)
        def _(kind=kind):
            for order in range(2):
                piece = pieces[2 * kind - 2 + order]
                side = which_ref[lower] if order == 0 else 1 - which_ref[lower]
                for number, (target, blocks) in enumerate(parts):
                    base = pl.multiple_of(side * (target.shape[0] // 2), 64)
                    for (top, left), (tall, wide), (down, right) in blocks:
                        pltpu.make_async_copy(
                            piece.at[pl.ds(top, tall), pl.ds(left, wide)],
                            target.at[pl.ds(base + down, tall), pl.ds(right, wide)],
                            sems.at[number],
                        ).start()


def end_fetch(own, target, sem):
    pltpu.make_async_copy(own, target, sem).wait()


SIDE = HALF // 2
QKV_BLOCKS = (
    ((0, 0), (HALF, D), (0, 0)),
    ((HALF, 0), (SIDE, HALF), (0, D)),
    ((HALF, HALF), (SIDE, HALF), (SIDE, D)),
)
OUT_BLOCKS = (((HALF + SIDE, 0), (SIDE, D), (0, 0)),)
FC_BLOCKS = (((0, 0), (HALF, D), (0, 0)), ((HALF, 0), (HALF, D), (0, D)))
PROJ_BLOCKS = (((0, 0), (D, D), (0, 0)),)


def attention_forward_kernel(layer, *refs):
    which_ref, own, pieces, refs = refs[0], refs[1:3], refs[3:7], refs[7:]
    vec_ref, bqkv_ref, refs = refs[0], refs[1], refs[2:]
    first = layer == 0
    count = 1 if first else 3
    ins, refs = refs[:count], refs[count:]
    outs, refs = refs[: 5 if first else 6], refs[5 if first else 6 :]
    held, refs = refs[:count], refs[count:]
    (a_ref, qkv_ref, o_ref, lse_ref, part_ref), refs = refs[:5], refs[5:]
    if not first:
        x_ref, refs = refs[0], refs[1:]
    wqkv_ref, wout_ref, sems, copy_sems = refs
    copies = Copies(copy_sems)
    blocks = row_slices(BT)
    arriving = [[copies.begin(part_of(src, rows), part_of(dst, rows)) for src, dst in zip(ins, held)] for rows in blocks]
    start_fetch(which_ref, own, pieces, ((wqkv_ref, QKV_BLOCKS), (wout_ref, OUT_BLOCKS)), sems)

    for number, rows in enumerate(blocks):
        for copy in arriving[number]:
            copy.wait()
        if first:
            values = held[0][rows, :].astype(F32)
        else:
            total = held[0][rows, :] + (held[1][rows, :].astype(F32) + held[2][rows, :].astype(F32)) + vec_ref[5:6, :]
            x_ref[rows, :] = total.astype(BF)
            copies.leave(part_of(x_ref, rows), part_of(outs[5], rows))
            values = total.astype(BF).astype(F32)
        unit, _ = normalize(values)
        a = (unit * vec_ref[8 * layer : 8 * layer + 1, :] + vec_ref[8 * layer + 2 : 8 * layer + 3, :]).astype(BF)
        a_ref[rows, :] = a
        copies.leave(part_of(a_ref, rows), part_of(outs[0], rows))
        if number == 0:
            end_fetch(own[0], wqkv_ref, sems.at[0])
        projected = mm(a, wqkv_ref[...]) + bqkv_ref[layer : layer + 1, :]
        for group in range(PAIRS):
            query, key, value = to_pairs(projected, group)
            start = 3 * 128 * group
            qkv_ref[rows, start : start + 128] = query.astype(BF) * 0.125
            qkv_ref[rows, start + 128 : start + 256] = key.astype(BF)
            qkv_ref[rows, start + 256 : start + 384] = value.astype(BF)
        copies.leave(part_of(qkv_ref, rows), part_of(outs[1], rows))

    def attend(group, carry):
        low = lower_lanes(BQ)
        keep_diag = lax.broadcasted_iota(jnp.int32, (BQ, BQ), 1) <= lax.broadcasted_iota(jnp.int32, (BQ, BQ), 0)
        value = qkv_ref[:, lane_group(3 * group + 2)]
        low_all = lower_lanes(LEN)
        one = jnp.ones_like(value)
        values = (jnp.where(low_all, value, one), jnp.where(low_all, one, value))

        def scores(i, head):
            past, here = i * BQ, (i + 1) * BQ
            query = qkv_ref[past:here, lane_group(3 * group)]
            nothing = jnp.zeros_like(query)
            query = jnp.where(low, query, nothing) if head == 0 else jnp.where(low, nothing, query)
            diag = jnp.where(keep_diag, mm_nt(query, qkv_ref[past:here, lane_group(3 * group + 1)]), MASKED_SCORE)
            left = mm_nt(query, qkv_ref[0:past, lane_group(3 * group + 1)]) if i else None
            return diag, left

        units = [(i, head) for i in range(LEN // BQ) for head in range(2)]
        ahead = scores(*units[0])
        mixed, largest = [], []
        for number, (i, head) in enumerate(units):
            past, here = i * BQ, (i + 1) * BQ
            diag, left = ahead
            if number + 1 < len(units):
                ahead = scores(*units[number + 1])
            top = jnp.max(diag, axis=1, keepdims=True)
            if i:
                top = jnp.maximum(top, jnp.max(left, axis=1, keepdims=True))
            total = mm(jnp.exp(diag - top).astype(BF), values[head][past:here])
            if i:
                total = total + mm(jnp.exp(left - top).astype(BF), values[head][:past])
            mixed.append(total)
            largest.append(top)
            if head == 1:
                sums = pltpu.roll(jnp.where(low, mixed[1], mixed[0]), HS, 1)
                o_ref[past:here, lane_group(group)] = (jnp.where(low, mixed[0], mixed[1]) / sums).astype(BF)
                lse_ref[past:here, lane_group(group)] = jnp.where(low, largest[0], largest[1]) + jnp.log(sums)
                mixed, largest = [], []
        return carry

    lax.fori_loop(0, PAIRS, attend, 0)

    copies.leave(o_ref, outs[2])
    copies.leave(lse_ref, outs[3])
    end_fetch(own[1], wout_ref, sems.at[1])
    for rows in row_slices(512):
        part_ref[rows, :] = mm(o_ref[rows, :], wout_ref[...]).astype(BF)
        copies.leave(part_of(part_ref, rows), part_of(outs[4], rows))
    copies.finish()


def params(limit=VMEM_BYTES):
    return pltpu.CompilerParams(vmem_limit_bytes=limit)


def shape(dims, kind):
    return jax.ShapeDtypeStruct(dims, kind)


def cost(flops, moved, transcendentals=0):
    return pl.CostEstimate(flops=int(flops) // 1000, bytes_accessed=int(moved) // 1000, transcendentals=0)


def buffers(values):
    return [pltpu.VMEM(value.shape, value.dtype) for value in values]


def run_kernel(kernel, name, smem, weights, rows, acts, outs, scratch, flops):
    smem_spec, vmem, hbm = (pl.BlockSpec(memory_space=kind) for kind in (pltpu.SMEM, pltpu.VMEM, pl.ANY))
    return pl.pallas_call(
        kernel,
        out_shape=outs,
        in_specs=[smem_spec] * len(smem) + [hbm] * len(weights) + [vmem] * len(rows) + [hbm] * len(acts),
        out_specs=[hbm] * len(outs),
        scratch_shapes=buffers(acts) + buffers(outs) + list(scratch) + [pltpu.SemaphoreType.DMA((COPIES,))],
        compiler_params=params(),
        cost_estimate=cost(flops, 2e7),
        name=name,
    )(*smem, *weights, *rows, *acts)


def attention_forward(layer, which, weights, vecs, bqkv, *acts):
    outs = [
        shape((LEN, D), BF),
        shape((LEN, QW), BF),
        shape((LEN, HALF), BF),
        shape((LEN, HALF), F32),
        shape((LEN, D), BF),
    ]
    if layer:
        outs.append(shape((LEN, D), BF))
    scratch = [pltpu.VMEM((D, QW), BF), pltpu.VMEM((HALF, D), BF), pltpu.SemaphoreType.DMA((2,))]
    kernel = functools.partial(attention_forward_kernel, layer)
    return run_kernel(kernel, "attention_forward", (which,), weights, (vecs, bqkv), acts, outs, scratch, 1.2e10)


def gelu_parts(u):
    slope = math.sqrt(2.0 / math.pi)
    square = u * u
    half = 0.5 + 0.5 * jnp.tanh(u * (slope + (slope * 0.044715) * square))
    value = u * half
    return value, half + (value - value * half) * (2.0 * slope + (6.0 * slope * 0.044715) * square)


def feed_forward_kernel(layer, *refs):
    both = layer == 1
    which_ref, own, fc_pieces, proj_pieces, refs = refs[0], refs[1:3], refs[3:7], refs[7:11], refs[11:]
    vec_ref, bfc_ref, refs = refs[0], refs[1], refs[2:]
    count = 4 if both else 3
    ins, refs = refs[:count], refs[count:]
    outs, refs = refs[: 6 if both else 5], refs[6 if both else 5 :]
    held, refs = refs[:count], refs[count:]
    (h_ref, c_ref, g_ref, part_ref, slope_ref), refs = refs[:5], refs[5:]
    if both:
        dc_ref, refs = refs[0], refs[1:]
    wfc_ref, wproj_ref, sems, copy_sems = refs
    base = 8 * layer
    copies = Copies(copy_sems)
    blocks = row_slices(BR)
    arriving = [[copies.begin(part_of(src, rows), part_of(dst, rows)) for src, dst in zip(ins, held)] for rows in blocks]
    start_fetch(which_ref, own[0:1], fc_pieces, ((wfc_ref, FC_BLOCKS),), sems.at[pl.ds(0, 1)])
    start_fetch(which_ref, own[1:2], proj_pieces, ((wproj_ref, PROJ_BLOCKS),), sems.at[pl.ds(1, 1)], 2)

    for number, rows in enumerate(blocks):
        for copy in arriving[number]:
            copy.wait()
        h = held[0][rows, :].astype(F32) + (
            held[1][rows, :].astype(F32) + held[2][rows, :].astype(F32) + vec_ref[base + 3 : base + 4, :]
        )
        h_ref[rows, :] = h
        copies.leave(part_of(h_ref, rows), part_of(outs[0], rows))
        unit, _ = normalize(h)
        c = (unit * vec_ref[base + 1 : base + 2, :] + vec_ref[base + 4 : base + 5, :]).astype(BF)
        c_ref[rows, :] = c
        copies.leave(part_of(c_ref, rows), part_of(outs[1], rows))
        if number == 0:
            end_fetch(own[0], wfc_ref, sems.at[0])
            end_fetch(own[1], wproj_ref, sems.at[1])

        width = 512
        starts = list(range(0, FW, width))

        def up(start):
            cols = slice(start, start + width)
            u = mm(c, wfc_ref[:, cols]) + bfc_ref[layer : layer + 1, cols]
            return u, (mm_nt(held[3][rows, :], wproj_ref[cols, :]) if both else None)

        part, dc = None, None
        ahead = up(starts[0])
        for position, start in enumerate(starts):
            cols = slice(start, start + width)
            u, dg = ahead
            if position + 1 < len(starts):
                ahead = up(starts[position + 1])
            g, slope = gelu_parts(u)
            g = g.astype(BF)
            g_ref[rows, cols] = g
            more = mm(g, wproj_ref[cols, :])
            part = more if part is None else part + more
            if both:
                du = (dg * slope).astype(BF)
                slope_ref[rows, cols] = du
                more = mm_nt(du, wfc_ref[:, cols])
                dc = more if dc is None else dc + more
            else:
                slope_ref[rows, cols] = slope.astype(BF)
        copies.leave(part_of(g_ref, rows), part_of(outs[2], rows))
        copies.leave(part_of(slope_ref, rows), part_of(outs[4], rows))
        if both:
            dc_ref[rows, :] = dc.astype(BF)
            copies.leave(part_of(dc_ref, rows), part_of(outs[5], rows))
        part_ref[rows, :] = part.astype(BF)
        copies.leave(part_of(part_ref, rows), part_of(outs[3], rows))
    copies.finish()


def whole_spec(dims):
    return pl.BlockSpec(dims, lambda *i: (0,) * len(dims))


def feed_weights():
    return [pltpu.VMEM((D, FW), BF), pltpu.VMEM((FW, D), BF), pltpu.SemaphoreType.DMA((2,))]


def feed_forward(layer, which, weights, vecs, bfc, *acts):
    outs = [shape((LEN, D), F32), shape((LEN, D), BF), shape((LEN, FW), BF), shape((LEN, D), BF), shape((LEN, FW), BF)]
    if layer == 1:
        outs.append(shape((LEN, D), BF))
    kernel = functools.partial(feed_forward_kernel, layer)
    return run_kernel(kernel, "feed_forward", (which,), weights, (vecs, bfc), acts, outs, feed_weights(), 1e10)


def norm_back(vec, da, unit, scale, sums_ref):
    sums_ref[0:1, :] += column_sum(da * unit)
    sums_ref[1:2, :] += column_sum(da)
    return normalize_back(da, unit, scale, vec)


def feed_back_kernel(*refs):
    which_ref, own, fc_pieces, proj_pieces, refs = refs[0], refs[1:3], refs[3:7], refs[7:11], refs[11:]
    vec_ref, ins, outs, held, refs = refs[0], refs[1:6], refs[6:10], refs[10:15], refs[15:]
    (dm_ref, du_ref, dc_ref, sums_ref), (wfc_ref, wproj_ref, sems, copy_sems) = refs[:4], refs[4:]
    dh_ref, own_ref, recv_ref, x_ref, slope_ref = held
    copies = Copies(copy_sems)
    blocks = row_slices(BR)
    arriving = []
    for rows in blocks:
        arriving.append([copies.begin(part_of(src, rows), part_of(dst, rows)) for src, dst in zip(ins, held)])
        if len(arriving) == 1:
            start_fetch(which_ref, own[1:2], proj_pieces, ((wproj_ref, PROJ_BLOCKS),), sems.at[pl.ds(1, 1)], 2)
            start_fetch(which_ref, own[0:1], fc_pieces, ((wfc_ref, FC_BLOCKS),), sems.at[pl.ds(0, 1)])
    sums_ref[...] = jnp.zeros_like(sums_ref)

    for number, rows in enumerate(blocks):
        for copy in arriving[number]:
            copy.wait()
        unit, scale = normalize(x_ref[rows, :].astype(F32))
        da = own_ref[rows, :].astype(F32) + recv_ref[rows, :].astype(F32)
        dm = (dh_ref[rows, :] + norm_back(vec_ref[8:9, :], da, unit, scale, sums_ref)).astype(BF)
        dm_ref[rows, :] = dm
        copies.leave(part_of(dm_ref, rows), part_of(outs[0], rows))
        if number == 0:
            end_fetch(own[1], wproj_ref, sems.at[1])
            end_fetch(own[0], wfc_ref, sems.at[0])
        width = 512
        starts = list(range(0, FW, width))

        def up(start):
            return mm_nt(dm, wproj_ref[start : start + width, :])

        dc = None
        ahead = up(starts[0])
        for position, start in enumerate(starts):
            cols = slice(start, start + width)
            dg = ahead
            if position + 1 < len(starts):
                ahead = up(starts[position + 1])
            du = (dg * slope_ref[rows, cols].astype(F32)).astype(BF)
            du_ref[rows, cols] = du
            more = mm_nt(du, wfc_ref[:, cols])
            dc = more if dc is None else dc + more
        copies.leave(part_of(du_ref, rows), part_of(outs[1], rows))
        dc_ref[rows, :] = dc.astype(BF)
        copies.leave(part_of(dc_ref, rows), part_of(outs[2], rows))
    copies.leave(sums_ref, outs[3])
    copies.finish()


def feed_back(which, weights, vecs, *acts):
    outs = [shape((LEN, D), BF), shape((LEN, FW), BF), shape((LEN, D), BF), shape((8, D), F32)]
    return run_kernel(feed_back_kernel, "feed_back", (which,), weights, (vecs,), acts, outs, feed_weights(), 5e9)


def input_back_kernel(vec_ref, *refs):
    ins, outs, held, (dx_ref, sums_ref, copy_sems) = refs[:4], refs[4:6], refs[6:10], refs[10:]
    dh_ref, own_ref, recv_ref, x_ref = held
    copies = Copies(copy_sems)
    blocks = row_slices(BT)
    arriving = [[copies.begin(part_of(src, rows), part_of(dst, rows)) for src, dst in zip(ins, held)] for rows in blocks]
    sums_ref[...] = jnp.zeros_like(sums_ref)
    for number, rows in enumerate(blocks):
        for copy in arriving[number]:
            copy.wait()
        unit, scale = normalize(x_ref[rows, :].astype(F32))
        da = own_ref[rows, :].astype(F32) + recv_ref[rows, :].astype(F32)
        dx_ref[rows, :] = (dh_ref[rows, :] + norm_back(vec_ref[0:1, :], da, unit, scale, sums_ref)).astype(BF)
        copies.leave(part_of(dx_ref, rows), part_of(outs[0], rows))
    copies.leave(sums_ref, outs[1])
    copies.finish()


def input_back(vecs, *acts):
    outs = [shape((LEN, D), BF), shape((8, D), F32)]
    return run_kernel(input_back_kernel, "input_back", (), (), (vecs,), acts, outs, (), 1e7)


def in_three(values, spots):
    high = values.astype(BF)
    rest = values - high.astype(F32)
    middle = rest.astype(BF)
    low = (rest - middle.astype(F32)).astype(BF)
    return jnp.where(spots == 0, high, jnp.where(spots == 1, middle, jnp.where(spots == 2, low, jnp.zeros_like(low))))


def attention_back_kernel(layer, *refs):
    which_ref, own, pieces, refs = refs[0], refs[1:3], refs[3:7], refs[7:]
    vec_ref, ins, outs, held, refs = refs[0], refs[1:8], refs[8:14], refs[14:21], refs[21:]
    (dh_ref, dz_ref, dqkv_ref, da_ref, sums_ref, bias_ref), refs = refs[:6], refs[6:]
    do_ref, dk_ref, dv_ref, wqkv_ref, wout_ref, sems, copy_sems = refs
    dm_ref, own_ref, recv_ref, h_ref, qkv_ref, o_ref, lse_ref = held
    copies = Copies(copy_sems)
    blocks = row_slices(BT)
    arriving = []
    for rows in blocks:
        arriving.append([copies.begin(part_of(src, rows), part_of(dst, rows)) for src, dst in zip(ins[:4], held[:4])])
        if len(arriving) == 1:
            start_fetch(which_ref, own, pieces, ((wqkv_ref, QKV_BLOCKS), (wout_ref, OUT_BLOCKS)), sems)
    later = [copies.begin(src, dst) for src, dst in zip(ins[4:], held[4:])]
    gain = vec_ref[8 * layer + 1 : 8 * layer + 2, :]
    sums_ref[...] = jnp.zeros_like(sums_ref)
    bias_ref[...] = jnp.zeros_like(bias_ref)

    for number, rows in enumerate(blocks):
        for copy in arriving[number]:
            copy.wait()
        unit, scale = normalize(h_ref[rows, :])
        dc = own_ref[rows, :].astype(F32) + recv_ref[rows, :].astype(F32)
        dm = dm_ref[rows, :].astype(F32)
        dh = dm + norm_back(gain, dc, unit, scale, sums_ref)
        dh_ref[rows, :] = dh
        copies.leave(part_of(dh_ref, rows), part_of(outs[0], rows))
        dz = dh.astype(BF)
        dz_ref[rows, :] = dz
        copies.leave(part_of(dz_ref, rows), part_of(outs[1], rows))
        sums_ref[2:3, :] += column_sum(dz.astype(F32))
        sums_ref[3:4, :] += column_sum(dm)
        if number == 0:
            end_fetch(own[1], wout_ref, sems.at[1])
        do_ref[rows, :] = mm_nt(dz, wout_ref[...]).astype(BF)
    copies.leave(sums_ref, outs[4])
    for copy in later:
        copy.wait()

    def attend(group, carry):
        low = lower_lanes(BK)
        low_all = lower_lanes(LEN)
        spots = lax.broadcasted_iota(jnp.int32, (BK, 128), 1) % HS
        ones = jnp.where(lax.broadcasted_iota(jnp.int32, (LEN, 128), 1) % HS < 3, 1.0, 0.0).astype(BF)
        keep_diag = lax.broadcasted_iota(jnp.int32, (BK, BK), 0) <= lax.broadcasted_iota(jnp.int32, (BK, BK), 1)
        nothing = jnp.zeros((BK, 128), BF)
        key = qkv_ref[:, lane_group(3 * group + 1)]
        value = qkv_ref[:, lane_group(3 * group + 2)]
        blank = jnp.zeros_like(key)
        keys_with = (jnp.where(low_all, key, ones), jnp.where(low_all, ones, key))
        values_with = (jnp.where(low_all, value, ones), jnp.where(low_all, ones, value))
        keys_one = (jnp.where(low_all, key, blank), jnp.where(low_all, blank, key))

        def prepare(i):
            mine = slice(i * BK, (i + 1) * BK)
            query = qkv_ref[mine, lane_group(3 * group)]
            do = do_ref[mine, lane_group(group)]
            lse = in_three(-pltpu.roll(lse_ref[mine, lane_group(group)], HS, 1), spots)
            inner = do.astype(F32) * o_ref[mine, lane_group(group)].astype(F32)
            t_low = jnp.sum(jnp.where(low, inner, 0.0), axis=1, keepdims=True)
            t_high = jnp.sum(jnp.where(low, 0.0, inner), axis=1, keepdims=True)
            t = in_three(-jnp.where(low, t_high, t_low), spots)
            return (
                (jnp.where(low, query, lse), jnp.where(low, lse, query)),
                (jnp.where(low, do, t), jnp.where(low, t, do)),
                (jnp.where(low, query, nothing), jnp.where(low, nothing, query)),
                (jnp.where(low, do, nothing), jnp.where(low, nothing, do)),
            )

        def products(i, head, prepared):
            past, here = i * BK, (i + 1) * BK
            query_with, do_with = prepared[0][head], prepared[1][head]
            diag = jnp.where(keep_diag, mm_nt(keys_with[head][past:here], query_with), MASKED_SCORE)
            out = [(diag, mm_nt(values_with[head][past:here], do_with))]
            if i:
                out.append((mm_nt(keys_with[head][:past], query_with), mm_nt(values_with[head][:past], do_with)))
            return out

        units = [(i, head) for i in range(LEN // BK) for head in range(2)]
        prepared = prepare(0)
        ahead = products(0, 0, prepared)
        dq = None
        for number, (i, head) in enumerate(units):
            past, here = i * BK, (i + 1) * BK
            now, now_prepared = ahead, prepared
            if number + 1 < len(units):
                if head == 1:
                    prepared = prepare(i + 1)
                ahead = products(*units[number + 1], prepared)
            query_one, do_one = now_prepared[2][head], now_prepared[3][head]
            for rows, (score, inner) in zip((slice(past, here), slice(0, past)), now):
                p = jnp.exp(score)
                ds = (p * inner).astype(BF)
                dv = mm(p.astype(BF), do_one)
                dk = mm(ds, query_one)
                part = mm_tn(ds, keys_one[head][rows])
                dq = part if dq is None else dq + part
                if head == 0 and rows.start == past:
                    dv_ref[rows, :] = dv
                    dk_ref[rows, :] = dk
                else:
                    dv_ref[rows, :] += dv
                    dk_ref[rows, :] += dk
            if head == 1:
                dqkv_ref[past:here, lane_group(3 * group)] = (dq * 0.125).astype(BF)
                dq = None
        for i in range(NB):
            mine = slice(i * BT, (i + 1) * BT)
            one, two, three = from_pairs(
                dqkv_ref[mine, lane_group(3 * group)].astype(F32), dk_ref[mine, :], dv_ref[mine, :]
            )
            dqkv_ref[mine, lane_group(3 * group)] = one.astype(BF)
            dqkv_ref[mine, lane_group(3 * group + 1)] = two.astype(BF)
            dqkv_ref[mine, lane_group(3 * group + 2)] = three.astype(BF)
        return carry

    lax.fori_loop(0, PAIRS, attend, 0)

    copies.leave(dqkv_ref, outs[2])
    end_fetch(own[0], wqkv_ref, sems.at[0])
    for rows in row_slices(512):
        da_ref[rows, :] = mm_nt(dqkv_ref[rows, :], wqkv_ref[...]).astype(BF)
        copies.leave(part_of(da_ref, rows), part_of(outs[3], rows))
        bias_ref[0:1, :] += column_sum(dqkv_ref[rows, :].astype(F32))
    copies.leave(bias_ref, outs[5])
    copies.finish()


def attention_back(layer, which, weights, vecs, *acts):
    outs = [
        shape((LEN, D), F32),
        shape((LEN, D), BF),
        shape((LEN, QW), BF),
        shape((LEN, D), BF),
        shape((8, D), F32),
        shape((8, QW), F32),
    ]
    scratch = [
        pltpu.VMEM((LEN, HALF), BF),
        pltpu.VMEM((LEN, 128), F32),
        pltpu.VMEM((LEN, 128), F32),
        pltpu.VMEM((D, QW), BF),
        pltpu.VMEM((HALF, D), BF),
        pltpu.SemaphoreType.DMA((2,)),
    ]
    kernel = functools.partial(attention_back_kernel, layer)
    return run_kernel(kernel, "attention_back", (which,), weights, (vecs,), acts, outs, scratch, 2.2e10)


def feed_grad_kernel(*refs):
    ins, outs, held, refs = refs[:4], refs[4:10], refs[10:14], refs[14:]
    grads, (square_ref, bias_ref, copy_sems) = refs[:4], refs[4:]
    copies = Copies(copy_sems)
    g_ref, dm_ref, c_ref, du_ref = held
    bias_ref[...] = jnp.zeros_like(bias_ref)
    halves = [pl.ds(0, D), pl.ds(D, D)]
    arriving = []
    for half in range(2):
        arriving.append(copies.begin(ins[0].at[:, halves[half]], g_ref.at[:, halves[half]]))
        if half == 0:
            arriving.append(copies.begin(ins[1], dm_ref))
        arriving.append(copies.begin(ins[3].at[:, halves[half]], du_ref.at[:, halves[half]]))
        if half == 0:
            arriving.append(copies.begin(ins[2], c_ref))
    total = None
    for number in range(4):
        for copy in (arriving[0:2], arriving[2:4], arriving[4:5], arriving[5:6])[number]:
            copy.wait()
        cols = slice(number // 2 * D, (number // 2 + 1) * D)
        if number % 2 == 0:
            grad = mm_tn(g_ref[:, cols], dm_ref[...])
        else:
            grad = mm_tn(c_ref[...], du_ref[:, cols])
            bias_ref[0:1, cols] = column_sum(du_ref[:, cols].astype(F32))
        grads[number][...] = grad.astype(BF)
        copies.leave(grads[number], outs[number])
        square = column_sum(grad * grad)
        total = square if total is None else total + square
    square_ref[...] = jnp.zeros_like(square_ref)
    square_ref[0:1, :] = total
    copies.leave(square_ref, outs[4])
    copies.leave(bias_ref, outs[5])
    copies.finish()


def feed_grad(*acts):
    outs = [shape((D, D), BF)] * 4 + [shape((8, D), F32), shape((8, FW), F32)]
    return run_kernel(feed_grad_kernel, "feed_grad", (), (), (), acts, outs, (), 1e10)


def attention_grad_kernel(*refs):
    ins, outs, held, refs = refs[:4], refs[4:7], refs[7:11], refs[11:]
    targets, square_ref, copy_sems = refs[:2], refs[2], refs[3]
    copies = Copies(copy_sems)
    o_ref, dz_ref, a_ref, dqkv_ref = held
    arriving = [copies.begin(ins[number], held[number]) for number in (2, 3, 0, 1)]
    square_ref[...] = jnp.zeros_like(square_ref)
    for part, target in enumerate(targets):
        half = slice(part * HALF, (part + 1) * HALF)

        def place(grad, rows, cols):
            square_ref[0:1, 0:HALF] += column_sum(grad * grad)
            target[rows, cols] = grad.astype(BF)

        if part == 0:
            arriving[0].wait()
            arriving[1].wait()
        top = mm_tn(a_ref[:, half], dqkv_ref[...])
        if part == 0:
            arriving[2].wait()
            arriving[3].wait()
        out = mm_tn(o_ref[...], dz_ref[:, half])
        place(top[:, 0:HALF], slice(0, HALF), slice(0, HALF))
        place(top[:, HALF:D], slice(0, HALF), slice(HALF, D))
        for start, grad in ((HALF, top[:, D:]), (HALF + SIDE, out)):
            place(grad[:SIDE], slice(start, start + SIDE), slice(0, HALF))
            place(grad[SIDE:], slice(start, start + SIDE), slice(HALF, D))
        copies.leave(target, outs[part])
    copies.leave(square_ref, outs[2])
    copies.finish()


def attention_grad(*acts):
    outs = [shape((D, D), BF), shape((D, D), BF), shape((8, D), F32)]
    return run_kernel(attention_grad_kernel, "attention_grad", (), (), (), acts, outs, (), 5e9)


def pack_small_kernel(core_ref, *refs):
    ins, (small_ref, square_ref) = refs[:12], refs[12:]
    small_ref[...] = jnp.zeros_like(small_ref)
    lower = core_ref[0] == 0
    total = jnp.zeros((8, D), F32)
    for layer in range(2):
        bias_qkv, bias_fc, first, second, squares_feed, squares_attention = (ref[...] for ref in ins[6 * layer : 6 * layer + 6])

        def side(values):
            return jnp.where(lower, values[:, :HALF], values[:, HALF:])

        small_ref[layer, 0:1, :] = bias_fc[0:1, 0:D]
        small_ref[layer, 1:2, :] = bias_fc[0:1, D:]
        small_ref[layer, 2:3, :] = bias_qkv[0:1, 0:D]
        small_ref[layer, 3:4, 0:HALF] = bias_qkv[0:1, D:]
        rows = (first[0:1], second[0:1], first[1:2], second[2:3], second[1:2], second[3:4])
        for number, row in enumerate(rows):
            line, right = divmod(number + 1, 2)
            small_ref[layer, 3 + line : 4 + line, right * HALF : (right + 1) * HALF] = side(row)
        total = total + squares_feed + squares_attention
        total = total + small_ref[layer, 0:8, :] * small_ref[layer, 0:8, :]
    square_ref[...] = jnp.broadcast_to(jnp.sum(total, keepdims=True), (8, 128))


def pack_small(core, *parts):
    vmem = pl.BlockSpec(memory_space=pltpu.VMEM)
    return pl.pallas_call(
        pack_small_kernel,
        in_specs=[pl.BlockSpec(memory_space=pltpu.SMEM)] + [vmem] * 12,
        out_specs=[vmem] * 2,
        out_shape=[shape((2, 16, D), F32), shape((8, 128), F32)],
        compiler_params=params(),
        cost_estimate=cost(1e5, 1e5),
        name="pack_small",
    )(core, *parts)


def unpack_small(rows):
    tail = rows[3:7].reshape(8, HALF)
    bias = jnp.concatenate([rows[2], tail[0]])
    return bias, rows[0:2].reshape(FW), tail[1:3], tail[3:7]


def weigh_kernel(rows, roles_ref, mine_ref, across_ref, above_ref, *refs):
    sources, refs = refs[:8], refs[8:]
    if len(refs) == 6:
        (small_ref, other_ref, keep_ref, aside_ref, held_ref, sems) = refs
    else:
        (other_ref, keep_ref, aside_ref, held_ref, sems) = refs
        small_ref = None
    mine, home = roles_ref[0], roles_ref[1]

    def bring(slot, one, two):
        for number, source in enumerate((one, two)):
            pltpu.make_async_copy(source.at[rows], held_ref.at[2 * slot + number], sems.at[slot]).start()

    for layer in range(2):
        first, first_there, second, second_there = sources[4 * layer : 4 * layer + 4]

        @pl.when(mine == layer)
        def _(second=second, second_there=second_there):
            bring(2, second, second_there)

        for role in range(2):

            @pl.when((home == 1) & ((mine == layer) == (role == 1)))
            def _(role=role, first=first, first_there=first_there):
                bring(role, first, first_there)

    count = held_ref.shape[1]

    def total(slot, weight_ref):
        both = held_ref.at[pl.ds(2 * slot, 2)]
        pltpu.make_async_copy(both, both, sems.at[slot]).wait()
        return mine_ref[0:1, 0:1] * held_ref[2 * slot].astype(F32) + weight_ref[0:1, 0:1] * held_ref[
            2 * slot + 1
        ].astype(F32)

    @pl.when(home == 1)
    def _():
        for slot, target in ((0, other_ref), (1, keep_ref)):
            target[0:count, :] = total(slot, across_ref).astype(target.dtype)
            if small_ref is not None:
                target[count:, :] = jnp.where(mine == slot, small_ref[1], small_ref[0]).astype(target.dtype)
        aside_ref[0:count, :] = total(2, above_ref).astype(BF)
        if small_ref is not None:
            aside_ref[count:, :] = jnp.zeros((16, D), BF)

    @pl.when(home == 0)
    def _():
        other_ref[0:count, :] = total(2, above_ref).astype(BF)
        if small_ref is not None:
            other_ref[count:, :] = jnp.zeros((16, D), BF)


def weigh(rows, roles, weights, layers, small=None):
    count = rows.stop - rows.start
    tall = count + (0 if small is None else 16)
    vmem, smem, hbm = (pl.BlockSpec(memory_space=kind) for kind in (pltpu.VMEM, pltpu.SMEM, pl.ANY))
    return pl.pallas_call(
        functools.partial(weigh_kernel, pl.ds(rows.start, count)),
        out_shape=[shape((tall, D), BF), shape((tall, D), F32), shape((tall, D), BF)],
        in_specs=[smem] + [vmem] * 3 + [hbm] * 8 + ([] if small is None else [vmem]),
        out_specs=[vmem] * 3,
        scratch_shapes=[pltpu.VMEM((6, count, D), BF), pltpu.SemaphoreType.DMA((3,))],
        compiler_params=params(SMALL_VMEM_BYTES),
        cost_estimate=cost(1e7, 1e7),
        name="weigh",
    )(roles, *weights, *layers[0], *layers[1], *(() if small is None else (small,)))


def noise_rows():
    sizes = (D * QW, QW, HALF * D, D * FW, FW, FW * D, 2 * HALF, 4 * HALF)
    starts = [0]
    for size in sizes:
        starts.append(starts[-1] + size // 128)
    return starts


NOISE_ROWS = noise_rows()


def bring_noise(noise_ref, begin, raw_ref, sem):
    copy = pltpu.make_async_copy(noise_ref.at[pl.ds(begin, raw_ref.shape[0])], raw_ref, sem)
    copy.start()
    return copy


def put_noised(target, block, rows, col, wide_ref, first, denominator):
    scale = NOISE_MULT * CLIP_FRACTION * math.sqrt(LEN * FF * D)
    per = target.shape[1] // 128
    tall = rows.stop - rows.start
    for tile in range(block.shape[1] // 128):
        place = col // 128 + tile
        noise = wide_ref[pl.ds(first + per * rows.start + place, tall, stride=per), :]
        value = block[:, tile * 128 : (tile + 1) * 128].astype(F32)
        target[rows, place * 128 : (place + 1) * 128] = (value + scale * noise) / denominator


def finish_feed_kernel(columns, denominator, home_ref, *refs):
    own, swapped = refs[:2], refs[2:4]
    noise_ref, grad_ref, raw_ref, wide_ref, sem = refs[4:]
    first = NOISE_ROWS[3 if columns else 5]
    begin = first // 16 * 16
    bring_noise(noise_ref, begin, raw_ref, sem).wait()
    wide_ref[...] = raw_ref[...].astype(F32)
    step = D // 2

    def run(parts):
        for number, part in enumerate(parts):
            for index in range(2):
                row, col = (index * step, number * D) if columns else (number * D + index * step, 0)
                block = part[index][0:step, :]
                put_noised(grad_ref, block, slice(row, row + step), col, wide_ref, first - begin, denominator)

    @pl.when(home_ref[0] == 1)
    def _():
        run((own, swapped))

    @pl.when(home_ref[0] == 0)
    def _():
        run((swapped, own))


def finish_attention_kernel(denominator, home_ref, *refs):
    own, swapped = refs[0:2], refs[2:4]
    noise_ref, qkv_ref, out_ref, raw_ref, wide_ref, sem = refs[4:]
    bring_noise(noise_ref, 0, raw_ref, sem).wait()
    wide_ref[...] = raw_ref[...].astype(F32)

    def run(parts):
        for number, (one, two) in enumerate(parts):
            start = number * HALF
            put_noised(qkv_ref, one[...], slice(start, start + HALF), 0, wide_ref, NOISE_ROWS[0], denominator)
            for index in range(2):
                cols = slice(index * HALF, (index + 1) * HALF)
                rows = slice(start + index * SIDE, start + (index + 1) * SIDE)
                put_noised(qkv_ref, two[0:SIDE, cols], rows, D, wide_ref, NOISE_ROWS[0], denominator)
                rows = slice(index * SIDE, (index + 1) * SIDE)
                put_noised(out_ref, two[SIDE : 2 * SIDE, cols], rows, start, wide_ref, NOISE_ROWS[2], denominator)

    @pl.when(home_ref[0] == 1)
    def _():
        run((own, swapped))

    @pl.when(home_ref[0] == 0)
    def _():
        run((swapped, own))


def finish(kernel, denominator, home, own, swapped, noise, numbers, shapes, name):
    smem, vmem, hbm = (pl.BlockSpec(memory_space=kind) for kind in (pltpu.SMEM, pltpu.VMEM, pl.ANY))
    begin, end = NOISE_ROWS[numbers[0]] // 16 * 16, -(-NOISE_ROWS[numbers[-1] + 1] // 16) * 16
    return pl.pallas_call(
        functools.partial(kernel, denominator),
        out_shape=[shape(dims, F32) for dims in shapes],
        in_specs=[smem] + [vmem] * (2 * len(own)) + [hbm],
        out_specs=[vmem] * len(shapes),
        scratch_shapes=[
            pltpu.VMEM((end - begin, 128), BF),
            pltpu.VMEM((end - begin, 128), F32),
            pltpu.SemaphoreType.DMA,
        ],
        compiler_params=params(),
        cost_estimate=cost(1e7, 1.6e7),
        name=name,
    )(home, *own, *swapped, noise)


def send(values, route):
    sections, ranks = lax.axis_size("section"), lax.axis_size("dp")
    pairs = []
    for section in range(sections):
        for rank in range(ranks):
            target = route(section, rank // 2, rank % 2)
            if target is not None:
                to_section, to_pair, to_core = target
                pairs.append((section * ranks + rank, to_section * ranks + to_pair * 2 + to_core))
    return lax.ppermute(values, ("section", "dp"), pairs)


def swap_cores(values):
    return send(values, lambda s, z, c: (s, z, 1 - c))


def is_home(s, c):
    return s % 2 == c


def after(values, *others):
    return lax.optimization_barrier((values, *others))[0]


def local(
    inputs,
    cotangent,
    included,
    qkv_weight,
    qkv_bias,
    out_weight,
    fc_weight,
    fc_bias,
    proj_weight,
    norm_gains,
    shifts,
    noise,
):
    clip_norm = CLIP_FRACTION * math.sqrt(LEN * FF * D)
    section = lax.axis_index("section")
    rank = lax.axis_index("dp")
    ranks = lax.axis_size("dp")
    row, half = section // 2, section % 2
    place, core = rank // 2, rank % 2
    home = half == core
    on_top = row == 0
    flip = home.astype(jnp.int32).reshape(1)
    denominator = SAMPLE_RATE * inputs.shape[0] * ranks

    side = place % 2

    def piece_of(weight, number):
        tall = weight.shape[0] // 2
        if number is None:
            return lax.dynamic_slice_in_dim(weight, side * tall, tall, 0)
        return weight[number * tall : (number + 1) * tall]

    def attention_piece(number):
        qkv = piece_of(qkv_weight, number)
        tail = jnp.concatenate([qkv[:SIDE, D:], qkv[SIDE:, D:]], axis=1)
        return jnp.concatenate([qkv[:, :D], tail, piece_of(out_weight, number)])

    fc_piece = piece_of(fc_weight, None)
    fc_piece = jnp.concatenate([fc_piece[:, :D], fc_piece[:, D:]])

    def near(piece):
        return send(piece, lambda s, z, c: (s ^ 2, z, c) if is_home(s, c) else (s ^ 1, z, 1 - c))

    def far(one, two):
        far_one = send(one, lambda s, z, c: (s ^ 1, z, c) if is_home(s, c) else None)
        return far_one, send(two, lambda s, z, c: None if is_home(s, c) else (s ^ 2, z, c))

    def next_plane(one):
        return send(one, lambda s, z, c: (s, z ^ 1, c))

    fc_one = near(fc_piece)
    *parts, fc_one = lax.optimization_barrier((attention_piece(0), attention_piece(1), fc_one))
    attention_pieces = tuple(near(part) for part in parts)
    fc_two = next_plane(fc_one)
    *parts, one, two = lax.optimization_barrier((*(piece_of(proj_weight, i) for i in range(2)), *attention_pieces))
    attention_pieces = (one, two)
    attention_far = far(*attention_pieces)
    proj_pieces = tuple(near(part) for part in parts)
    fc_again, *attention_far = lax.optimization_barrier((fc_one, *attention_far))
    fc_far = far(fc_again, fc_two)
    proj_pieces = (*proj_pieces, *far(*proj_pieces))
    attention_pieces = (*attention_pieces, *attention_far)
    attention_weights = (qkv_weight, out_weight, *attention_pieces)

    def which_of(layer):
        kind = jnp.where(row == layer, jnp.where(home, 0, 1), jnp.where(home, 1, 2))
        nothing = jnp.zeros_like(side)
        return [jnp.stack([kind, first, nothing]).astype(jnp.int32) for first in (nothing, side)]

    which_attention, which_feed = zip(which_of(0), which_of(1))

    def own_sequence(values):
        mine = lax.dynamic_index_in_dim(values, half, 0, keepdims=False)
        theirs = swap_cores(mine)
        return jnp.where(core == row, mine, theirs)

    small = jnp.concatenate([qkv_bias, fc_bias, norm_gains.reshape(-1), shifts.reshape(-1)]).reshape(1, -1)
    others = [send(small, lambda s, z, c, bits=bits: (s ^ bits, z, c)) for bits in (1, 2, 3)]
    x0 = own_sequence(inputs)
    cot = own_sequence(cotangent)
    drawn = own_sequence(jnp.broadcast_to(included.astype(F32)[:, None, None], (2, 8, 128)))[0, 0]
    x0, cot = lax.optimization_barrier((x0, cot))
    small_all = jnp.concatenate([small] + others, axis=0)
    small_all = jnp.where(half == 0, small_all, jnp.concatenate([small_all[i : i + 1] for i in (1, 0, 3, 2)]))
    small_all = jnp.where(on_top, small_all, jnp.concatenate([small_all[2:], small_all[:2]]))
    small_all = small_all.reshape(2, 2, -1)
    bias = jnp.where(core == 0, small_all[:, 0], small_all[:, 1])
    bqkv, bfc = bias[:, :QW], bias[:, QW : QW + FW]
    vecs = small_all[:, :, QW + FW :].reshape(2, 2, 6, HALF).transpose(0, 2, 1, 3).reshape(2, 6, D)
    vecs = jnp.pad(vecs, ((0, 0), (0, 2), (0, 0))).reshape(16, D)

    shapes = ((D, QW), (QW,), (HALF, D), (D, FW), (FW,), (FW, D), (2, HALF), (4, HALF))
    a0, qkv0, o0, lse0, part = attention_forward(0, which_attention[0], attention_weights, vecs, bqkv, x0)
    part, *fc_far = lax.optimization_barrier((part, *fc_far))
    feed_weights_all = (fc_weight, proj_weight, fc_one, fc_two, *fc_far, *proj_pieces)
    part_theirs = swap_cores(part)
    h0, c0, g0, part_two, slope0 = feed_forward(
        0, which_feed[0], feed_weights_all, vecs, bfc, x0, part, part_theirs
    )
    a1, qkv1, o1, lse1, part, x1 = attention_forward(
        1, which_attention[1], attention_weights, vecs, bqkv, h0, part_two, swap_cores(part_two)
    )
    h1, c1, g1, part_two, du1, dc = feed_forward(
        1, which_feed[1], feed_weights_all, vecs, bfc, x1, part, swap_cores(part), cot
    )
    dc_theirs = swap_cores(dc)

    def spread(block_for):
        received = []
        for step in range(2):
            block = block_for(2 * core + (step ^ half))
            received.append(send(block, lambda s, z, c, step=step: (2 * c + (step ^ (s % 2)), z, s // 2)))
        return received

    def over_x(values):
        return send(values, lambda s, z, c: None if is_home(s, c) else (s ^ 1, z, c))

    def over_y(layer, values):
        return send(values, lambda s, z, c: None if s // 2 == layer else (s ^ 2, z, c))

    *grads1, squares_feed1, bias_fc1 = feed_grad(g1, cot, c1, du1)
    dc, dc_theirs, *grads1 = lax.optimization_barrier((dc, dc_theirs, *grads1))
    proj_x1, fc_x1, proj_y1 = over_x(grads1[0]), over_x(grads1[1]), over_y(1, grads1[2])
    dh1, dz1, dqkv1, da, sums1, bias_qkv1 = attention_back(
        1, which_attention[1], attention_weights, vecs, cot, dc, dc_theirs, h1, qkv1, o1, lse1
    )
    da, proj_x1, fc_x1, proj_y1 = lax.optimization_barrier((da, proj_x1, fc_x1, proj_y1))
    da_theirs = swap_cores(da)
    fc_y1 = over_y(1, grads1[3])
    first1, second1, squares_attention1 = attention_grad(o1, dz1, a1, dqkv1)
    da, da_theirs, first1 = lax.optimization_barrier((da, da_theirs, first1))
    dm0, du0, dc, first_sums1 = feed_back(which_feed[0], feed_weights_all, vecs, dh1, da, da_theirs, x1, slope0)
    dc, fc_y1 = lax.optimization_barrier((dc, fc_y1))
    dc_theirs = swap_cores(dc)
    attention_x1 = over_x(first1)
    *grads0, squares_feed0, bias_fc0 = feed_grad(g0, dm0, c0, du0)
    dc, dc_theirs, attention_x1, *grads0 = lax.optimization_barrier((dc, dc_theirs, attention_x1, *grads0))
    proj_x0, fc_x0, proj_y0 = over_x(grads0[0]), over_x(grads0[1]), over_y(0, grads0[2])
    attention_y1 = over_y(1, second1)
    dh0, dz0, dqkv0, da, sums0, bias_qkv0 = attention_back(
        0, which_attention[0], attention_weights, vecs, dm0, dc, dc_theirs, h0, qkv0, o0, lse0
    )
    da, proj_x0, fc_x0, proj_y0, attention_y1 = lax.optimization_barrier((da, proj_x0, fc_x0, proj_y0, attention_y1))
    da_theirs = swap_cores(da)
    fc_y0 = over_y(0, grads0[3])
    first0, second0, squares_attention0 = attention_grad(o0, dz0, a0, dqkv0)
    dx0, first_sums0 = input_back(vecs, dh0, da, da_theirs, x0)
    small_pair, squares = pack_small(
        core.astype(jnp.int32).reshape(1),
        *(bias_qkv0, bias_fc0, first_sums0, sums0, squares_feed0, squares_attention0),
        *(bias_qkv1, bias_fc1, first_sums1, sums1, squares_feed1, squares_attention1),
    )
    small_there = send(small_pair, lambda s, z, c: None if is_home(s, c) else (s ^ 1, z, c))

    squares = squares + swap_cores(squares)
    factor = drawn * jnp.minimum(1.0, clip_norm / jnp.sqrt(squares))
    across = send(factor, lambda s, z, c: (s ^ 1, z, 1 - c) if is_home(s, c) else None)
    above = send(factor, lambda s, z, c: (s ^ 2, z, c))
    factor, across, above, fc_y0 = lax.optimization_barrier((factor, across, above, fc_y0))
    weights = (factor, across, above)
    roles = jnp.stack([row, home]).astype(jnp.int32)

    def send_first(first, small_pair):
        there = over_x(jnp.concatenate([first, small_pair[:, :8].reshape(16, D).astype(BF)]))
        small = there[D:].astype(F32).reshape(2, 8, D)
        small = jnp.where(home, weights[0][0, 0] * small_pair[:, :8] + weights[1][0, 0] * small, 0.0)
        return there, jnp.pad(small, ((0, 0), (0, 8), (0, 0)))


    proj0, proj1 = (grads0[0], proj_x0, grads0[2], proj_y0), (grads1[0], proj_x1, grads1[2], proj_y1)
    fc0, fc1 = (grads0[1], fc_x0, grads0[3], fc_y0), (grads1[1], fc_x1, grads1[3], fc_y1)
    attention1 = (first1, attention_x1, second1, attention_y1)

    token_rows = LEN // lax.axis_size("section")

    def last_output(part_two):
        return (h1 + (part_two.astype(F32) + swap_cores(part_two).astype(F32)) + vecs[13:14]).astype(BF)

    def exchange_outputs(y1, dx0):
        both_out = jnp.concatenate([x1, y1], axis=1)

        def block_for(number):
            columns = lax.dynamic_slice_in_dim(both_out, number * HALF, HALF, 1)
            rows = lax.dynamic_slice_in_dim(dx0, number * token_rows, token_rows, 0)
            return jnp.concatenate([columns, rows[:, :HALF], rows[:, HALF:]])

        return spread(block_for)

    def ordered_outputs(outputs):
        outputs = in_order(*outputs)
        rows = (outputs[:, LEN : LEN + token_rows], outputs[:, LEN + token_rows :])
        return outputs[:, :LEN], jnp.concatenate(rows, axis=2)

    def in_order(first, second):
        return jnp.where(half == 0, jnp.stack([first, second]), jnp.stack([second, first]))

    places = ranks // 2
    middle = places // 2

    def to_middle(step):
        def route(s, z, c):
            if z == step:
                return (s, z + 1, c)
            if z == places - 1 - step:
                return (s, z - 1, c)
            return None

        return route

    def at_middle(s, z, c):
        return (s, places - 1 - z, c) if z in (middle - 1, middle) else None

    def from_middle(step):
        def route(s, z, c):
            if z == middle - 1 - step:
                return (s, z - 1, c)
            if z == middle + step:
                return (s, z + 1, c)
            return None

        return route

    def add(left, right):
        return (left.astype(F32) + right.astype(F32)).astype(BF)

    def weigh_stage(args):
        other, keep, aside = weigh(*args)
        arrived = send(other, lambda s, z, c: (s ^ 2, z, c) if is_home(s, c) else (s ^ 1, z, 1 - c))
        aside = send(aside, lambda s, z, c: (s, z, 1 - c) if is_home(s, c) else None)
        return keep, aside, arrived

    def weigh_end(held):
        keep, aside, arrived = held
        return (jnp.where(home, keep, aside.astype(F32)) + arrived.astype(F32)).astype(BF)

    def chain_stage(hop):
        def stage(held):
            total = add(*held) if len(held) == 2 else weigh_end(held)
            return total, send(total, hop)

        return stage

    def spread_stage(step):
        def stage(held):
            total, arrived = held
            if step == 0:
                total = add(total, arrived)
            else:
                takes = (place == middle - 1 - step) | (place == middle + step)
                total = jnp.where(takes, arrived, total)
            return total, send(total, from_middle(step))

        return stage

    def last_stage(held):
        total, arrived = held
        if middle > 1:
            takes = (place == 0) | (place == places - 1)
            total = jnp.where(takes, arrived, total)
        else:
            total = add(total, arrived)
        return total, swap_cores(total)

    hops = [to_middle(step) for step in range(middle - 1)] + [at_middle]
    stages = [weigh_stage] + [chain_stage(hop) for hop in hops]
    stages += [spread_stage(step) for step in range(middle - 1)] + [last_stage]

    chunk = D // 2

    noise_flat = noise.reshape(-1, 128)

    def small_noise(number, dims):
        first = NOISE_ROWS[number] * 128
        return noise[first : first + math.prod(dims)].reshape(dims).astype(F32)

    def finish_proj(one, two):
        return finish(
            functools.partial(finish_feed_kernel, False), denominator, flip, *zip(one, two), noise_flat, (5,), ((FW, D),), "finish_feed"
        )[0]

    def finish_fc(one, two):
        return finish(
            functools.partial(finish_feed_kernel, True), denominator, flip, *zip(one, two), noise_flat, (3,), ((D, FW),), "finish_feed"
        )[0]

    if middle == 2:
        edge = (place == 0) | (place == places - 1)

        def to_next(s, z, c):
            return (s, z ^ 1, c)

        count = 6
        begun, sums, lows, totals, ready = ({} for _ in range(5))
        outer, last = None, None

        def tie(*values):
            if last is None or last[1] not in last[0]:
                return values if len(values) > 1 else values[0]
            store, name = last
            *values, store[name] = lax.optimization_barrier((*values, store[name]))
            return values if len(values) > 1 else values[0]

        def begin(group, pair, *small):
            begun[group], begun[group, 1], begun[group, 2] = weigh_stage(
                (slice(0, D), roles, tie(*weights), pair, *small)
            )
            return begun, group

        attention_x0, small_sum = send_first(first0, small_pair)
        last = begin(0, (proj0, proj1))
        last = begin(1, (fc0, fc1))
        second0 = tie(second0)
        attention_y0 = over_y(0, second0)
        inners = {}
        for tick in range(count + 4):
            old_outer = outer
            if 0 <= tick - 3 < count:
                totals[tick - 3] = add(tie(lows.pop(tick - 3)), inners.pop(tick - 3))
                last = totals, tick - 3
            if tick < count and tick % 2 == 0:
                group = tick // 2
                total = weigh_end((tie(begun.pop(group)), begun.pop((group, 1)), begun.pop((group, 2))))
                sums[tick], sums[tick + 1] = total[:chunk], total[chunk:]
                last = sums, tick
            inward, outward = sums.get(tick), totals.get(tick - 3)
            if inward is not None and outward is not None:
                tall = [inward.shape[0], outward.shape[0]]
                padded = [jnp.pad(part, ((0, max(tall) - part.shape[0]), (0, 0))) for part in (inward, outward)]
                outer = send(jnp.where(edge, *padded), to_next)
                outer = (outer[: tall[0]], outer[: tall[1]])
            else:
                outer = (
                    None if inward is None else send(inward, to_middle(0)),
                    None if outward is None else send(outward, from_middle(0)),
                )
            if 0 <= tick - 1 < count:
                lows[tick - 1] = add(tie(sums.pop(tick - 1)), old_outer[0])
                last = lows, tick - 1
                inners[tick - 1] = send(lows[tick - 1], at_middle)
            if 0 <= tick - 4 < count:
                total = tie(totals.pop(tick - 4))
                if tick == count + 3:
                    total, layer_out, input_grad = lax.optimization_barrier(
                        (total, *ordered_outputs(outputs))
                    )
                ready[tick - 4] = jnp.where(edge, old_outer[1], total)
                last = ready, tick - 4
            if tick == 2:
                attention_x0, attention_y0, small_sum = tie(attention_x0, attention_y0, small_sum)
                attention0 = (first0, attention_x0, second0, attention_y0)
                last = begin(2, (attention0, attention1), small_sum)
            if tick == 2:
                y1 = last_output(tie(part_two))
            if tick == 4:
                outputs = exchange_outputs(*tie(y1, dx0))
            if tick == 6:
                proj_grad = finish_proj(*((ready[i], swap_cores(ready[i])) for i in (0, 1)))
            if tick == 8:
                proj_grad = tie(proj_grad)
                fc_grad = finish_fc(*((ready[i], swap_cores(ready[i])) for i in (2, 3)))
            if tick == 9:
                fc_grad = tie(fc_grad)
        jobs = [None] * 4 + [(ready[i], swap_cores(ready[i])) for i in (4, 5)]
        small_own, small_swapped = jobs[5]
        stages = []
    else:
        attention_x0, small_sum = send_first(first0, small_pair)
        attention0 = (first0, attention_x0, second0, over_y(0, second0))
        jobs = []
        for pair in ((proj0, proj1), (fc0, fc1), (attention0, attention1)):
            jobs += [(slice(i * chunk, (i + 1) * chunk), roles, weights, pair) for i in range(2)]
        jobs[5] += (small_sum,)
        layer_out, input_grad = ordered_outputs(exchange_outputs(last_output(part_two), dx0))
    for tick in range(len(jobs) + len(stages) - 1 if stages else 0):
        for stage in reversed(range(len(stages))):
            index = tick - stage
            if 0 <= index < len(jobs):
                held = jobs[index]
                jobs[index] = stages[stage](held)
    if stages:
        proj_grad, fc_grad = finish_proj(*jobs[0:2]), finish_fc(*jobs[2:4])
        small_own, small_swapped = jobs[5]
    attention = jobs[4:]
    own, swapped = zip(*attention)
    qkv_grad, out_grad = finish(
        finish_attention_kernel, denominator, flip, own, swapped, noise_flat, (0, 2), ((D, QW), (HALF, D)), "finish_attention"
    )
    small_sum = jnp.where(home, small_own[chunk:], small_swapped[chunk:]).astype(F32)
    small_done = [
        (part + NOISE_MULT * clip_norm * small_noise(number, part.shape)) / denominator
        for part, number in zip(unpack_small(small_sum), (1, 4, 6, 7))
    ]
    return (
        layer_out,
        input_grad,
        qkv_grad,
        small_done[0],
        out_grad,
        fc_grad,
        small_done[1],
        proj_grad,
        small_done[2],
        small_done[3],
    )


def solution(mesh):
    return jax.shard_map(
        local,
        mesh=mesh,
        in_specs=(
            P("dp", None, None),
            P("dp", None, None),
            P("dp"),
            P(None, "section"),
            P("section"),
            P("section", None),
            P(None, "section"),
            P("section"),
            P("section", None),
            P(None, "section"),
            P(None, "section"),
            P("section"),
        ),
        out_specs=(
            P("dp", None, "section"),
            P("dp", "section", None),
            P(None, "section"),
            P("section"),
            P("section", None),
            P(None, "section"),
            P("section"),
            P("section", None),
            P(None, "section"),
            P(None, "section"),
        ),
        check_vma=False,
    )
```
